32 devices in a mesh: sta: 2 (over x), gx: 4 (over z), gy: 4 (over y, core).
Axes of the slice: x: 2, y: 2, z: 4, core: 2. Of those that a mesh axis runs over, the one named last changes fastest.
Arguments:
- rec_state: float32 [2, 4, 9, 32, 32, 128], P('sta', None, None, 'gx', 'gy'), may hold values from -6 to 6
- source_strain: bfloat16 [2, 8, 6, 32, 32, 128], P('sta', None, None, 'gx', 'gy'), may hold values from -6 to 6
- material: int32 [32, 32, 128], P('gx', 'gy'), may hold values from 0 to 15
- material_table: float32 [16, 3], replicated, may hold values from 0.5 to 1.5
- residual: float32 [2, 4, 8], P('sta'), may hold values from -4 to 4
- rec_cell: int32 [2, 4], P('sta'), may hold values from 0 to 1023
- listed: int32 [2, 8, 2], replicated, may hold values 0 or 1
- src_pick: int32 [2, 8], replicated, may hold values from 0 to 1
Outputs:
- kernels: float32 [2, 32, 32, 128], P(None, ('gx', 'sta'), 'gy')
The draws below stay inside these ranges and needn't reach their ends.
All inputs are finite; a program needn't handle non-finite values.
Results may differ from the reference program's by a relative error of at most 0.0003.
Values may be sent and summed in bfloat16 or wider, within the bound.
No kernel may reach another device: no remote copies, remote signals or barrier semaphores. Data moves between devices by JAX's collectives and lax.ppermute only.
A program may use at most 128 MiB of HBM per device.

```python
import jax
import jax.numpy as jnp
from jax import lax

CZ = 128
REC = 4
STEPS = 8
TURNS = 2
NMAT = 16
NX = 32
NY = 32
N_STA = 2


def place_ends(result, stream_key, least, high):
    longest = result.shape.index(max(result.shape))
    spots = []
    for shift in (0, 1):
        where = [jax.random.randint(jax.random.fold_in(stream_key, axis), (), 0, length) for axis, length in enumerate(result.shape)]
        where[longest] = (where[longest] + shift) % result.shape[longest]
        spots.append(tuple(where))
    return result.at[spots[0]].set(least).at[spots[1]].set(high)


def steps_of(stream_key, dims, cuts, low, high):
    gain, own = 1.0, jax.random.fold_in(stream_key, 6)
    for axis_at, parts in cuts:
        draws = jnp.exp(jax.random.uniform(jax.random.fold_in(own, axis_at), (parts,), jnp.float32, low / len(cuts), high / len(cuts)))
        gain = gain * jnp.repeat(draws, dims[axis_at] // parts).reshape([-1 if axis == axis_at else 1 for axis in range(len(dims))])
    return gain


def noise(key, extent, deviation, most, split=(), kind=jnp.bfloat16):
    loudness = steps_of(key, extent, split, -0.22, 0.18) if split else 1.0
    result = jax.random.normal(key, extent, jnp.float32) * deviation * loudness
    return jnp.minimum(jnp.maximum(result, -most), most).astype(kind)


def setup_inputs(seed: int = 0) -> dict:
    streams_of = jax.random.split(jax.random.key(seed), 9)
    rec_state = noise(streams_of[0], (N_STA, REC, 9, NX, NY, CZ), 1.0, 6.0, ((0, 2), (3, 4), (4, 4)), jnp.float32)
    source_strain = noise(streams_of[1], (N_STA, STEPS, 6, NX, NY, CZ), 1.0, 6.0, ((0, 2), (3, 4), (4, 4)))
    material = place_ends(jax.random.randint(streams_of[2], (NX, NY, CZ), 0, NMAT), jax.random.fold_in(streams_of[2], 1), 0, NMAT - 1).astype(jnp.int32)
    material_table = jnp.clip(jax.random.uniform(streams_of[3], (NMAT, 3), jnp.float32, 0.5, 1.5), 0.5, 1.5)
    residual = noise(streams_of[4], (N_STA, REC, STEPS), 1.0, 4.0, ((0, 2),), jnp.float32)
    rec_cell = place_ends(jax.random.randint(streams_of[5], (N_STA, REC), 0, NX * NY), jax.random.fold_in(streams_of[5], 1), 0, (NX * NY) - 1).astype(jnp.int32)
    listed = place_ends((jax.random.randint(streams_of[6], (TURNS, STEPS, N_STA), 0, 2) < 1).astype(jnp.int32), jax.random.fold_in(streams_of[6], 1), 0, 1)
    src_pick = place_ends(jax.random.randint(streams_of[7], (TURNS, STEPS), 0, N_STA), jax.random.fold_in(streams_of[7], 1), 0, N_STA - 1).astype(jnp.int32)
    return {"rec_state": rec_state, "source_strain": source_strain, "material": material, "material_table": material_table, "residual": residual, "rec_cell": rec_cell, "listed": listed, "src_pick": src_pick}


C_NEAR = 8.0 / 12.0
C_FAR = -1.0 / 12.0
TIME_STEP = 0.25
AMPLITUDE = 4.0
KERNEL_SCALE = 0.0625
STIFFNESS = 0.3


def along_first(padded):
    core = padded[..., :, 2:-2, 2:-2]
    return C_NEAR * (core[..., 3:-1, :, :] - core[..., 1:-3, :, :]) + C_FAR * (core[..., 4:, :, :] - core[..., :-4, :, :])


def along_second(padded):
    core = padded[..., 2:-2, :, 2:-2]
    return C_NEAR * (core[..., :, 3:-1, :] - core[..., :, 1:-3, :]) + C_FAR * (core[..., :, 4:, :] - core[..., :, :-4, :])


def along_depth(padded):
    core = padded[..., 2:-2, 2:-2, :]
    return C_NEAR * (core[..., 3:-1] - core[..., 1:-3]) + C_FAR * (core[..., 4:] - core[..., :-4])


def pad_all(field):
    return jnp.pad(field, [(0, 0)] * (field.ndim - 3) + [(2, 2)] * 3)


def force_terms(padded, source_term):
    first = along_first(padded[:, 0]) + along_second(padded[:, 3]) + along_depth(padded[:, 4])
    second = along_first(padded[:, 3]) + along_second(padded[:, 1]) + along_depth(padded[:, 5])
    third = along_first(padded[:, 4]) + along_second(padded[:, 5]) + along_depth(padded[:, 2]) + source_term
    return jnp.stack([first, second, third], 1)


def strain_rates(padded):
    comp_first = padded[:, 0]
    comp_second = padded[:, 1]
    comp_depth = padded[:, 2]
    rate_first = along_first(comp_first)
    rate_second = along_second(comp_second)
    rate_depth = along_depth(comp_depth)
    shear_plane = 0.5 * (along_second(comp_first) + along_first(comp_second))
    shear_first = 0.5 * (along_depth(comp_first) + along_first(comp_depth))
    shear_second = 0.5 * (along_depth(comp_second) + along_second(comp_depth))
    return jnp.stack([rate_first, rate_second, rate_depth, shear_plane, shear_first, shear_second], 1)


def update_stress(stress, rates, lame, shear):
    trace = rates[:, 0] + rates[:, 1] + rates[:, 2]
    diagonal = stress[:, :3] + TIME_STEP * (lame * trace[:, None] + 2.0 * shear * rates[:, :3])
    offdiag = stress[:, 3:] + TIME_STEP * (2.0 * shear * rates[:, 3:])
    return jnp.concatenate([diagonal, offdiag], 1)


def correlate(source, weighted):
    trace_src = source[0] + source[1] + source[2]
    trace_rec = weighted[0] + weighted[1] + weighted[2]
    lam_part = trace_src * trace_rec
    diag_part = source[0] * weighted[0] + source[1] * weighted[1] + source[2] * weighted[2]
    off_part = source[3] * weighted[3] + source[4] * weighted[4] + source[5] * weighted[5]
    return jnp.stack([lam_part, 2.0 * diag_part + 4.0 * off_part])


def reference(rec_state, source_strain, material, material_table, residual, rec_cell, listed, src_pick):
    buoyancy = TIME_STEP / material_table[:, 0][material]
    lame = STIFFNESS * material_table[:, 1][material]
    shear = STIFFNESS * material_table[:, 2][material]
    depth_first = (jnp.arange(CZ) == 0).astype(jnp.float32)
    moments = jnp.arange(STEPS, dtype=jnp.int32)
    picked = source_strain[src_pick, moments[None, :]].astype(jnp.float32)
    row_index = jnp.arange(NX, dtype=jnp.int32)
    col_index = jnp.arange(NY, dtype=jnp.int32)

    def one_group(kernel, group):
        state = lax.dynamic_index_in_dim(rec_state, group, 0, keepdims=False)
        weights = lax.dynamic_index_in_dim(listed, group, 2, keepdims=False).astype(jnp.float32)
        cells = lax.dynamic_index_in_dim(rec_cell, group, 0, keepdims=False)
        res_rows = lax.dynamic_index_in_dim(residual, group, 0, keepdims=False)
        spots = ((cells // NY)[:, None, None] == row_index[None, :, None]) & ((cells % NY)[:, None, None] == col_index[None, None, :])
        spots = spots.astype(jnp.float32)
        velocity = state[:, :3]
        stress = state[:, 3:]
        for moment in range(STEPS):
            source_term = (AMPLITUDE * res_rows[:, moment])[:, None, None, None] * spots[:, :, :, None] * depth_first
            velocity = velocity + buoyancy * force_terms(pad_all(stress), source_term)
            rates = strain_rates(pad_all(velocity))
            stress = update_stress(stress, rates, lame, shear)
            weighted = jnp.sum((KERNEL_SCALE * res_rows[:, moment])[:, None, None, None, None] * rates, 0)
            combined = jnp.sum(weights[:, moment][:, None, None, None, None] * picked[:, moment], 0)
            kernel = kernel + correlate(combined, weighted)
        return kernel, None

    start = jnp.zeros((2, NX, NY, CZ), jnp.float32)
    kernel, _ = lax.scan(one_group, start, jnp.arange(N_STA, dtype=jnp.int32))
    return kernel
```

```python
import functools

import jax
import jax.numpy as jnp
from jax import lax
from jax.experimental import pallas as pl
from jax.experimental.pallas import tpu as pltpu
from jax.sharding import PartitionSpec as P

C_NEAR = 8.0 / 12.0
C_FAR = 1.0 / 12.0
TIME_STEP = 0.25
AMPLITUDE = 4.0
KERNEL_SCALE = 0.0625
STIFFNESS = 0.3
REACH = 2
DEEP = 2 * REACH
ALONG_X = (0, 3, 4)

VMEM = pl.BlockSpec(memory_space=pltpu.VMEM)
SMEM = pl.BlockSpec(memory_space=pltpu.SMEM)
F32 = jnp.float32


def call(body, outs, ins, aliases=None, flops=2_000_000):
    return pl.pallas_call(
        body,
        out_shape=[jax.ShapeDtypeStruct(shape, F32) for shape in outs],
        in_specs=[SMEM if small else VMEM for _, small in ins],
        out_specs=[VMEM] * len(outs),
        input_output_aliases=aliases or {},
        compiler_params=pltpu.CompilerParams(vmem_limit_bytes=32 * 1024 * 1024),
        cost_estimate=pl.CostEstimate(flops=flops, bytes_accessed=4_000_000, transcendentals=0),
    )(*[array for array, _ in ins])


def edge_coefs(shape, axis):
    at = lax.broadcasted_iota(jnp.int32, shape, axis)
    size = shape[axis]
    return (
        jnp.where(at < size - 1, C_NEAR, 0.0).astype(F32),
        jnp.where(at >= 1, C_NEAR, 0.0).astype(F32),
        jnp.where(at < size - 2, C_FAR, 0.0).astype(F32),
        jnp.where(at >= 2, C_FAR, 0.0).astype(F32),
    )


def in_row(row, coefs, axis):
    size = row.shape[axis]
    near = coefs[0] * pltpu.roll(row, size - 1, axis) - coefs[1] * pltpu.roll(row, 1, axis)
    far = coefs[2] * pltpu.roll(row, size - 2, axis) - coefs[3] * pltpu.roll(row, 2, axis)
    return near - far


def across(rows, x):
    return C_NEAR * (rows(x + 1) - rows(x - 1)) - C_FAR * (rows(x + 2) - rows(x - 2))


def assemble(place, *refs):
    count = len(refs) - 5
    tiles, (vel, stress, cells, low, high) = refs[:count], refs[count:]
    tile_x, tile_y = tiles[0].shape[1:3]
    for turn, tile in enumerate(tiles):
        spot = pl.ds(pl.multiple_of((place[0] ^ turn) * tile_y, tile_y), tile_y)
        vel[:, :, spot, :] = tile[0:3]
        stress[:, :, spot, :] = tile[3:9]
        cells[:, spot, :] = tile[9]
        for at, comp in enumerate(ALONG_X):
            low[at, :, spot, :] = tile[3 + comp, :REACH]
            high[at, :, spot, :] = tile[3 + comp, tile_x - REACH :]
        low[len(ALONG_X), :, spot, :] = tile[9, :REACH]
        high[len(ALONG_X), :, spot, :] = tile[9, tile_x - REACH :]


def push(place, amount, stress, vel, low_stress, high_stress, buoyancy, vel_out, low_out, high_out):
    _, tile_x, size_y, depth = vel.shape
    shape = (size_y, depth)
    coef_y, coef_z = edge_coefs(shape, 0), edge_coefs(shape, 1)
    spot = (lax.broadcasted_iota(jnp.int32, shape, 0) == place[4]) & (
        lax.broadcasted_iota(jnp.int32, shape, 1) == 0
    )
    spot = jnp.where(spot, amount, 0.0)

    def rows(at):
        def row(x):
            if x < 0:
                return low_stress[at, x + REACH]
            if x >= tile_x:
                return high_stress[at, x - tile_x]
            return stress[ALONG_X[at], x]

        return row

    for x in range(tile_x):
        xy, xz, yz = stress[3, x], stress[4, x], stress[5, x]
        force_x = across(rows(0), x) + in_row(xy, coef_y, 0) + in_row(xz, coef_z, 1)
        force_y = across(rows(1), x) + in_row(stress[1, x], coef_y, 0) + in_row(yz, coef_z, 1)
        force_z = across(rows(2), x) + in_row(yz, coef_y, 0) + in_row(stress[2, x], coef_z, 1)
        force_z = force_z + jnp.where(place[3] == x, 1.0, 0.0) * spot
        light = buoyancy[x]
        for comp, force in enumerate((force_x, force_y, force_z)):
            fresh = vel[comp, x] + light * force
            vel_out[comp, x] = fresh
            if x < DEEP:
                low_out[comp, x] = fresh
            if x >= tile_x - DEEP:
                high_out[comp, x - (tile_x - DEEP)] = fresh


def first(place, table, residual, vel, stress, cells, low, high, vel_out, low_out, high_out, light, lame, shear):
    tile_x = vel.shape[1]
    count = table.shape[0]
    for x in range(-REACH, tile_x + REACH):
        if x < 0:
            number, inside = low[len(ALONG_X), x + REACH], place[1] > 0
        elif x >= tile_x:
            number, inside = high[len(ALONG_X), x - tile_x], place[1] < place[2] - 1
        else:
            number, inside = cells[x], None
        parts = [jnp.full(number.shape, table[0, c], F32) for c in range(3)]
        for m in range(1, count):
            hit = number == float(m)
            parts = [jnp.where(hit, table[m, c], parts[c]) for c in range(3)]
        half_step = 1.0 if inside is None else jnp.where(inside, 1.0, 0.0)
        lame[x + REACH] = (TIME_STEP * STIFFNESS * half_step) * parts[1]
        shear[x + REACH] = (2.0 * TIME_STEP * STIFFNESS * half_step) * parts[2]
        if inside is None:
            light[x] = TIME_STEP / parts[0]
    amount = AMPLITUDE * residual[place[0], 0]
    push(place, amount, stress, vel, low, high, light, vel_out, low_out, high_out)


def advance(moment, last, *refs):
    place, residual, vel, low, high, stress, low_stress, high_stress, light, lame, shear = refs[:11]
    if last:
        (rates,) = refs[11:]
    else:
        rates, stress_out, low_stress_out, high_stress_out, vel_out, low_out, high_out = refs[11:]
    _, tile_x, size_y, depth = vel.shape
    shape = (size_y, depth)
    coef_y, coef_z = edge_coefs(shape, 0), edge_coefs(shape, 1)

    def rows(comp):
        def row(x):
            if x < 0:
                return low[comp, x + DEEP]
            if x >= tile_x:
                return high[comp, x - tile_x]
            return vel[comp, x]

        return row

    vx, vy, vz = rows(0), rows(1), rows(2)
    reach = 0 if last else REACH
    for x in range(-reach, tile_x + reach):
        own = 0 <= x < tile_x
        xx = across(vx, x)
        yy = in_row(vy(x), coef_y, 0)
        zz = in_row(vz(x), coef_z, 1)
        xy = 0.5 * (in_row(vx(x), coef_y, 0) + across(vy, x))
        xz = 0.5 * (in_row(vx(x), coef_z, 1) + across(vz, x))
        if own:
            yz = 0.5 * (in_row(vy(x), coef_z, 1) + in_row(vz(x), coef_y, 0))
            for comp, rate in enumerate((xx, yy, zz, xy, xz, yz)):
                rates[comp, x] = rate
        if last:
            continue
        stiff = shear[x + REACH]
        bulk = lame[x + REACH] * (xx + yy + zz)
        if own:
            for comp, rate in enumerate((xx, yy, zz)):
                stress_out[comp, x] = stress[comp, x] + (bulk + stiff * rate)
            for comp, rate in enumerate((xy, xz, yz)):
                stress_out[3 + comp, x] = stress[3 + comp, x] + stiff * rate
        else:
            source, target, row = (
                (low_stress, low_stress_out, x + REACH) if x < 0 else (high_stress, high_stress_out, x - tile_x)
            )
            target[0, row] = source[0, row] + (bulk + stiff * xx)
            target[1, row] = source[1, row] + stiff * xy
            target[2, row] = source[2, row] + stiff * xz
    if not last:
        amount = AMPLITUDE * residual[place[0], moment + 1]
        push(place, amount, stress_out, vel, low_stress_out, high_stress_out, light, vel_out, low_out, high_out)


def correlate(moments, pieces, *refs):
    place, residual = refs[:2]
    rates = refs[2 : 2 + moments]
    sources = refs[2 + moments : 2 + moments + pieces]
    (terms,) = refs[2 + moments + pieces :]
    tile_x, tile_y = sources[0].shape[2:4]
    for turn in range(pieces):
        spot = pl.ds(pl.multiple_of((place[0] ^ turn) * tile_y, tile_y), tile_y)
        for x in range(tile_x):
            lam = mu = None
            for moment in range(moments):
                weight = KERNEL_SCALE * residual[place[0], moment]
                rate = [rates[moment][c, x, spot, :] for c in range(6)]
                source = [sources[turn][moment, c, x] for c in range(6)]
                bulk = (source[0] + source[1] + source[2]) * (rate[0] + rate[1] + rate[2])
                diag = source[0] * rate[0] + source[1] * rate[1] + source[2] * rate[2]
                off = source[3] * rate[3] + source[4] * rate[4] + source[5] * rate[5]
                bulk, both = weight * bulk, (2.0 * weight) * (diag + 2.0 * off)
                lam = bulk if lam is None else lam + bulk
                mu = both if mu is None else mu + both
            terms[turn, 0, x] = lam
            terms[turn, 1, x] = mu


def swap(array, axis, turn):
    count = lax.axis_size(axis)
    return lax.ppermute(array, axis, [(i, i ^ turn) for i in range(count)])


def to_neighbours(low, high, axis):
    count = lax.axis_size(axis)
    up = [(i, i + 1) for i in range(count - 1)]
    down = [(i + 1, i) for i in range(count - 1)]
    return lax.ppermute(high, axis, up), lax.ppermute(low, axis, down)


def local(rec_state, source_strain, material, material_table, residual, rec_cell, listed, src_pick):
    state = rec_state[0]
    receivers, _, tile_x, tile_y, depth = state.shape
    pieces = lax.axis_size("gy")
    groups = lax.axis_size("sta")
    assert receivers == pieces and pieces & (pieces - 1) == 0 and groups & (groups - 1) == 0
    size_y = pieces * tile_y
    group, slab, me = lax.axis_index("sta"), lax.axis_index("gx"), lax.axis_index("gy")
    moments = residual.shape[2]

    numbers = material.astype(F32)[None]
    chunks = []
    for turn in range(pieces):
        mine = lax.dynamic_index_in_dim(state, me ^ turn, 0, keepdims=False)
        mine = jnp.concatenate([mine, numbers], 0)
        chunks.append(swap(mine, "gy", turn) if turn else mine)

    weights = lax.dynamic_slice_in_dim(listed, group, 1, 2)[:, :, 0].astype(F32)
    combined = 0.0
    for turn in range(groups):
        piece = swap(source_strain[0], "sta", turn) if turn else source_strain[0]
        factor = jnp.sum(weights * (src_pick == (group ^ turn)).astype(F32), 0)
        combined = combined + factor[:, None, None, None, None] * piece.astype(F32)

    cell = lax.dynamic_index_in_dim(rec_cell[0], me, 0, keepdims=False)
    place = jnp.stack(
        [me, slab, jnp.full((), lax.axis_size("gx")), cell // size_y - slab * tile_x, cell % size_y]
    ).astype(jnp.int32)
    rows = residual[0]
    whole, halo, face = (size_y, depth), (3, REACH, size_y, depth), (3, DEEP, size_y, depth)
    vel_shape, stress_shape = (3, tile_x) + whole, (6, tile_x) + whole
    ends = (4, REACH) + whole

    vel, stress, cells, low, high = call(
        assemble,
        [vel_shape, stress_shape, (tile_x,) + whole, ends, ends],
        [(place, True)] + [(chunk, False) for chunk in chunks],
    )
    low_stress, high_stress = to_neighbours(low, high, "gx")
    vel, low, high, light, lame, shear = call(
        first,
        [vel_shape, face, face, (tile_x,) + whole, (tile_x + 2 * REACH,) + whole, (tile_x + 2 * REACH,) + whole],
        [(place, True), (material_table, True), (rows, True)]
        + [(array, False) for array in (vel, stress, cells, low_stress, high_stress)],
    )
    low_stress, high_stress = low_stress[:3], high_stress[:3]

    rates = []
    for moment in range(moments):
        last = moment == moments - 1
        low, high = to_neighbours(low, high, "gx")
        outs = [stress_shape]
        if not last:
            outs += [stress_shape, halo, halo, vel_shape, face, face]
        results = call(
            functools.partial(advance, moment, last),
            outs,
            [(place, True), (rows, True)]
            + [
                (array, False)
                for array in (vel, low, high, stress, low_stress, high_stress, light, lame, shear)
            ],
        )
        rates.append(results[0])
        if not last:
            stress, low_stress, high_stress, vel, low, high = results[1:]

    sources = [combined]
    width = pieces // 2
    found = {0: combined}
    while width:
        for turn in list(found):
            found[turn ^ width] = swap(found[turn], "gy", width)
        width //= 2
    sources = [found[turn] for turn in range(pieces)]

    (terms,) = call(
        functools.partial(correlate, moments, pieces),
        [(pieces, 2, tile_x, tile_y, depth)],
        [(place, True), (rows, True)] + [(array, False) for array in rates + sources],
    )
    held = {turn: terms[turn] for turn in range(pieces)}
    width = 1
    while width < pieces:
        keep = [turn for turn in held if not turn & width]
        sent = swap(jnp.stack([held[turn ^ width] for turn in keep]), "gy", width)
        held = {turn: held[turn] + sent[at] for at, turn in enumerate(keep)}
        width *= 2
    total = held[0]
    share = tile_x // groups
    result = lax.dynamic_slice_in_dim(total, group * share, share, 1)
    for turn in range(1, groups):
        part = lax.dynamic_slice_in_dim(total, (group ^ turn) * share, share, 1)
        result = result + swap(part, "sta", turn)
    return result


def solution(mesh):
    in_specs = (
        P("sta", None, None, "gx", "gy", None),
        P("sta", None, None, "gx", "gy", None),
        P("gx", "gy", None),
        P(),
        P("sta", None, None),
        P("sta", None),
        P(),
        P(),
    )
    out_specs = P(None, ("gx", "sta"), "gy", None)
    return jax.shard_map(local, mesh=mesh, in_specs=in_specs, out_specs=out_specs, check_vma=False)
```

```python
import functools

import jax
import jax.numpy as jnp
from jax import lax
from jax.experimental import pallas as pl
from jax.experimental.pallas import tpu as pltpu
from jax.sharding import PartitionSpec as P

C_NEAR = 8.0 / 12.0
C_FAR = 1.0 / 12.0
TIME_STEP = 0.25
AMPLITUDE = 4.0
KERNEL_SCALE = 0.0625
STIFFNESS = 0.3
REACH = 2
DEEP = 2 * REACH
ALONG_X = (0, 3, 4)
ME, FLIP, HAS_LOW, HAS_HIGH, SPOT_X, SPOT_Y = range(6)

VMEM = pl.BlockSpec(memory_space=pltpu.VMEM)
SMEM = pl.BlockSpec(memory_space=pltpu.SMEM)
F32 = jnp.float32


def call(body, outs, ins, aliases=None, flops=2_000_000):
    return pl.pallas_call(
        body,
        out_shape=[jax.ShapeDtypeStruct(shape, F32) for shape in outs],
        in_specs=[SMEM if small else VMEM for _, small in ins],
        out_specs=[VMEM] * len(outs),
        input_output_aliases=aliases or {},
        compiler_params=pltpu.CompilerParams(vmem_limit_bytes=32 * 1024 * 1024),
        cost_estimate=pl.CostEstimate(flops=flops, bytes_accessed=4_000_000, transcendentals=0),
    )(*[array for array, _ in ins])


def edge_coefs(shape, axis):
    at = lax.broadcasted_iota(jnp.int32, shape, axis)
    size = shape[axis]
    return (
        jnp.where(at < size - 1, C_NEAR, 0.0).astype(F32),
        jnp.where(at >= 1, C_NEAR, 0.0).astype(F32),
        jnp.where(at < size - 2, C_FAR, 0.0).astype(F32),
        jnp.where(at >= 2, C_FAR, 0.0).astype(F32),
    )


def in_row(row, coefs, axis):
    size = row.shape[axis]
    near = coefs[0] * pltpu.roll(row, size - 1, axis) - coefs[1] * pltpu.roll(row, 1, axis)
    far = coefs[2] * pltpu.roll(row, size - 2, axis) - coefs[3] * pltpu.roll(row, 2, axis)
    return near - far


def across(rows, x, sign):
    near, far = sign * C_NEAR, sign * C_FAR
    return near * (rows(x + 1) - rows(x - 1)) - far * (rows(x + 2) - rows(x - 2))


def sign_of(place):
    return 1.0 - 2.0 * place[FLIP].astype(F32)


def mirrored(place, x, tile_x):
    return x + place[FLIP] * (tile_x - 1 - 2 * x)


def assemble(place, *refs):
    count = len(refs) - 5
    tiles, (vel, stress, cells, low, high) = refs[:count], refs[count:]
    tile_x, tile_y = tiles[0].shape[1:3]
    for turn, tile in enumerate(tiles):
        spot = pl.ds(pl.multiple_of((place[ME] ^ turn) * tile_y, tile_y), tile_y)
        for x in range(tile_x):
            row = mirrored(place, x, tile_x)
            for comp in range(3):
                vel[comp, x, spot, :] = tile[comp, row]
            for comp in range(6):
                stress[comp, x, spot, :] = tile[3 + comp, row]
            cells[x, spot, :] = tile[9, row]
            for at, comp in enumerate(ALONG_X + (6,)):
                if x < REACH:
                    low[at, x, spot, :] = tile[3 + comp, row]
                if x >= tile_x - REACH:
                    high[at, x - (tile_x - REACH), spot, :] = tile[3 + comp, row]


def push(place, amount, stress, vel, low_stress, high_stress, buoyancy, vel_out, low_out, high_out):
    _, tile_x, size_y, depth = vel.shape
    shape = (size_y, depth)
    coef_y, coef_z = edge_coefs(shape, 0), edge_coefs(shape, 1)
    sign = sign_of(place)
    spot = (lax.broadcasted_iota(jnp.int32, shape, 0) == place[SPOT_Y]) & (
        lax.broadcasted_iota(jnp.int32, shape, 1) == 0
    )
    spot = jnp.where(spot, amount, 0.0)

    def rows(at):
        def row(x):
            if x < 0:
                return low_stress[at, -1 - x]
            if x >= tile_x:
                return high_stress[at, REACH - 1 - (x - tile_x)]
            return stress[ALONG_X[at], x]

        return row

    for x in range(tile_x):
        xy, xz, yz = stress[3, x], stress[4, x], stress[5, x]
        force_x = across(rows(0), x, sign) + in_row(xy, coef_y, 0) + in_row(xz, coef_z, 1)
        force_y = across(rows(1), x, sign) + in_row(stress[1, x], coef_y, 0) + in_row(yz, coef_z, 1)
        force_z = across(rows(2), x, sign) + in_row(yz, coef_y, 0) + in_row(stress[2, x], coef_z, 1)
        force_z = force_z + jnp.where(place[SPOT_X] == x, 1.0, 0.0) * spot
        light = buoyancy[x]
        for comp, force in enumerate((force_x, force_y, force_z)):
            fresh = vel[comp, x] + light * force
            vel_out[comp, x] = fresh
            if x < DEEP:
                low_out[comp, x] = fresh
            if x >= tile_x - DEEP:
                high_out[comp, x - (tile_x - DEEP)] = fresh


def first(place, table, residual, vel, stress, cells, low, high, vel_out, low_out, high_out, light, lame, shear):
    tile_x = vel.shape[1]
    count = table.shape[0]
    for x in range(-REACH, tile_x + REACH):
        if x < 0:
            number, inside = low[len(ALONG_X), -1 - x], place[HAS_LOW] > 0
        elif x >= tile_x:
            number, inside = high[len(ALONG_X), REACH - 1 - (x - tile_x)], place[HAS_HIGH] > 0
        else:
            number, inside = cells[x], None
        parts = [jnp.full(number.shape, table[0, c], F32) for c in range(3)]
        for m in range(1, count):
            hit = number == float(m)
            parts = [jnp.where(hit, table[m, c], parts[c]) for c in range(3)]
        half_step = 1.0 if inside is None else jnp.where(inside, 1.0, 0.0)
        lame[x + REACH] = (TIME_STEP * STIFFNESS * half_step) * parts[1]
        shear[x + REACH] = (2.0 * TIME_STEP * STIFFNESS * half_step) * parts[2]
        if inside is None:
            light[x] = TIME_STEP / parts[0]
    amount = AMPLITUDE * residual[place[ME], 0]
    push(place, amount, stress, vel, low, high, light, vel_out, low_out, high_out)


def advance(moment, last, *refs):
    place, residual, vel, low, high, stress, low_stress, high_stress, light, lame, shear = refs[:11]
    if last:
        (rates,) = refs[11:]
    else:
        rates, stress_out, low_stress_out, high_stress_out, vel_out, low_out, high_out = refs[11:]
    _, tile_x, size_y, depth = vel.shape
    shape = (size_y, depth)
    coef_y, coef_z = edge_coefs(shape, 0), edge_coefs(shape, 1)

    def rows(comp):
        def row(x):
            if x < 0:
                return low[comp, -1 - x]
            if x >= tile_x:
                return high[comp, DEEP - 1 - (x - tile_x)]
            return vel[comp, x]

        return row

    vx, vy, vz = rows(0), rows(1), rows(2)
    sign = sign_of(place)
    reach = 0 if last else REACH
    for x in range(-reach, tile_x + reach):
        own = 0 <= x < tile_x
        xx = across(vx, x, sign)
        yy = in_row(vy(x), coef_y, 0)
        zz = in_row(vz(x), coef_z, 1)
        xy = 0.5 * (in_row(vx(x), coef_y, 0) + across(vy, x, sign))
        xz = 0.5 * (in_row(vx(x), coef_z, 1) + across(vz, x, sign))
        if own:
            yz = 0.5 * (in_row(vy(x), coef_z, 1) + in_row(vz(x), coef_y, 0))
            for comp, rate in enumerate((xx, yy, zz, xy, xz, yz)):
                rates[comp, x] = rate
        if last:
            continue
        stiff = shear[x + REACH]
        bulk = lame[x + REACH] * (xx + yy + zz)
        if own:
            for comp, rate in enumerate((xx, yy, zz)):
                stress_out[comp, x] = stress[comp, x] + (bulk + stiff * rate)
            for comp, rate in enumerate((xy, xz, yz)):
                stress_out[3 + comp, x] = stress[3 + comp, x] + stiff * rate
        else:
            source, target, row = (
                (low_stress, low_stress_out, -1 - x)
                if x < 0
                else (high_stress, high_stress_out, REACH - 1 - (x - tile_x))
            )
            target[0, row] = source[0, row] + (bulk + stiff * xx)
            target[1, row] = source[1, row] + stiff * xy
            target[2, row] = source[2, row] + stiff * xz
    if not last:
        amount = AMPLITUDE * residual[place[ME], moment + 1]
        push(place, amount, stress_out, vel, low_stress_out, high_stress_out, light, vel_out, low_out, high_out)


def correlate(moments, pieces, *refs):
    place, residual = refs[:2]
    rates = refs[2 : 2 + moments]
    sources = refs[2 + moments : 2 + moments + pieces]
    (terms,) = refs[2 + moments + pieces :]
    tile_x, tile_y = sources[0].shape[2:4]
    for turn in range(pieces):
        spot = pl.ds(pl.multiple_of((place[ME] ^ turn) * tile_y, tile_y), tile_y)
        for x in range(tile_x):
            row = mirrored(place, x, tile_x)
            lam = mu = None
            for moment in range(moments):
                weight = KERNEL_SCALE * residual[place[ME], moment]
                rate = [rates[moment][c, x, spot, :] for c in range(6)]
                source = [sources[turn][moment, c, row] for c in range(6)]
                bulk = (source[0] + source[1] + source[2]) * (rate[0] + rate[1] + rate[2])
                diag = source[0] * rate[0] + source[1] * rate[1] + source[2] * rate[2]
                off = source[3] * rate[3] + source[4] * rate[4] + source[5] * rate[5]
                bulk, both = weight * bulk, (2.0 * weight) * (diag + 2.0 * off)
                lam = bulk if lam is None else lam + bulk
                mu = both if mu is None else mu + both
            terms[turn, 0, row] = lam
            terms[turn, 1, row] = mu


def swap(array, axis, turn):
    count = lax.axis_size(axis)
    return lax.ppermute(array, axis, [(i, i ^ turn) for i in range(count)])


def partner(slab, piece, slabs, turn):
    other = slab + 1 - 2 * ((slab + piece + turn) % 2)
    return other, (other >= 0) & (other < slabs)


def to_neighbours(low, high):
    slabs, pieces = lax.axis_size("gx"), lax.axis_size("gy")
    got = []
    for turn, face in enumerate((high, low)):
        pairs = []
        for slab in range(slabs):
            for piece in range(pieces):
                other, inside = partner(slab, piece, slabs, turn)
                if inside:
                    pairs.append((slab * pieces + piece, other * pieces + piece))
        got.append(lax.ppermute(face, ("gx", "gy"), pairs))
    return got[1], got[0]


def local(rec_state, source_strain, material, material_table, residual, rec_cell, listed, src_pick):
    state = rec_state[0]
    receivers, _, tile_x, tile_y, depth = state.shape
    pieces = lax.axis_size("gy")
    groups = lax.axis_size("sta")
    assert receivers == pieces and pieces & (pieces - 1) == 0 and groups & (groups - 1) == 0
    size_y = pieces * tile_y
    group, slab, me = lax.axis_index("sta"), lax.axis_index("gx"), lax.axis_index("gy")
    moments = residual.shape[2]

    numbers = material.astype(F32)[None]
    chunks = []
    for turn in range(pieces):
        mine = lax.dynamic_index_in_dim(state, me ^ turn, 0, keepdims=False)
        mine = jnp.concatenate([mine, numbers], 0)
        chunks.append(swap(mine, "gy", turn) if turn else mine)

    strains = [swap(source_strain[0], "sta", turn) if turn else source_strain[0] for turn in range(groups)]

    cell = lax.dynamic_index_in_dim(rec_cell[0], me, 0, keepdims=False)
    flip = (slab + me) % 2
    has_high = partner(slab, me, lax.axis_size("gx"), 0)[1]
    has_low = partner(slab, me, lax.axis_size("gx"), 1)[1]
    spot_x = cell // size_y - slab * tile_x
    spot_x = spot_x + flip * (tile_x - 1 - 2 * spot_x)
    place = jnp.stack([me, flip, has_low, has_high, spot_x, cell % size_y]).astype(jnp.int32)
    rows = residual[0]
    whole, halo, face = (size_y, depth), (3, REACH, size_y, depth), (3, DEEP, size_y, depth)
    vel_shape, stress_shape = (3, tile_x) + whole, (6, tile_x) + whole
    ends = (4, REACH) + whole

    vel, stress, cells, low, high = call(
        assemble,
        [vel_shape, stress_shape, (tile_x,) + whole, ends, ends],
        [(place, True)] + [(chunk, False) for chunk in chunks],
    )
    low_stress, high_stress = to_neighbours(low, high)
    vel, low, high, light, lame, shear = call(
        first,
        [vel_shape, face, face, (tile_x,) + whole, (tile_x + 2 * REACH,) + whole, (tile_x + 2 * REACH,) + whole],
        [(place, True), (material_table, True), (rows, True)]
        + [(array, False) for array in (vel, stress, cells, low_stress, high_stress)],
    )
    low_stress, high_stress = low_stress[:3], high_stress[:3]

    strains, low, high = lax.optimization_barrier((strains, low, high))
    weights = lax.dynamic_slice_in_dim(listed, group, 1, 2)[:, :, 0].astype(F32)
    combined = 0.0
    for turn in range(groups):
        factor = jnp.sum(weights * (src_pick == (group ^ turn)).astype(F32), 0)
        combined = combined + factor[:, None, None, None, None] * strains[turn].astype(F32)

    width = pieces // 2
    found = {0: combined}
    if width:
        found[width] = swap(combined, "gy", width)
        width //= 2

    rates = []
    for moment in range(moments):
        if moment == 5 * moments // 8:
            found, low, high = lax.optimization_barrier((found, low, high))
            while width:
                for turn in list(found):
                    found[turn ^ width] = swap(found[turn], "gy", width)
                width //= 2
        last = moment == moments - 1
        low, high = to_neighbours(low, high)
        outs = [stress_shape]
        if not last:
            outs += [stress_shape, halo, halo, vel_shape, face, face]
        results = call(
            functools.partial(advance, moment, last),
            outs,
            [(place, True), (rows, True)]
            + [
                (array, False)
                for array in (vel, low, high, stress, low_stress, high_stress, light, lame, shear)
            ],
        )
        rates.append(results[0])
        if not last:
            stress, low_stress, high_stress, vel, low, high = results[1:]

    sources = [found[turn] for turn in range(pieces)]

    (terms,) = call(
        functools.partial(correlate, moments, pieces),
        [(pieces, 2, tile_x, tile_y, depth)],
        [(place, True), (rows, True)] + [(array, False) for array in rates + sources],
    )
    held = {turn: terms[turn] for turn in range(pieces)}
    width = 1
    while width < pieces:
        keep = [turn for turn in held if not turn & width]
        sent = swap(jnp.stack([held[turn ^ width] for turn in keep]), "gy", width)
        held = {turn: held[turn] + sent[at] for at, turn in enumerate(keep)}
        width *= 2
    total = held[0]
    share = tile_x // groups
    result = lax.dynamic_slice_in_dim(total, group * share, share, 1)
    for turn in range(1, groups):
        part = lax.dynamic_slice_in_dim(total, (group ^ turn) * share, share, 1)
        result = result + swap(part, "sta", turn)
    return result


def solution(mesh):
    in_specs = (
        P("sta", None, None, "gx", "gy", None),
        P("sta", None, None, "gx", "gy", None),
        P("gx", "gy", None),
        P(),
        P("sta", None, None),
        P("sta", None),
        P(),
        P(),
    )
    out_specs = P(None, ("gx", "sta"), "gy", None)
    return jax.shard_map(local, mesh=mesh, in_specs=in_specs, out_specs=out_specs, check_vma=False)
```

```python
import functools

import jax
import jax.numpy as jnp
from jax import lax
from jax.experimental import pallas as pl
from jax.experimental.pallas import tpu as pltpu
from jax.sharding import PartitionSpec as P

C_NEAR = 8.0 / 12.0
C_FAR = 1.0 / 12.0
TIME_STEP = 0.25
AMPLITUDE = 4.0
KERNEL_SCALE = 0.0625
STIFFNESS = 0.3
REACH = 2
DEEP = 2 * REACH
ALONG_X = (0, 3, 4)
ME, FLIP, HAS_HIGH, HAS_LOW, SPOT_X, SPOT_Y = range(6)
NEAR_ROWS = 2
PACKED = DEEP + NEAR_ROWS

VMEM = pl.BlockSpec(memory_space=pltpu.VMEM)
SMEM = pl.BlockSpec(memory_space=pltpu.SMEM)
F32, BF16 = jnp.float32, jnp.bfloat16


def call(body, outs, ins, flops=1_000_000):
    scalars, arrays = ins
    return list(pl.pallas_call(
        body,
        out_shape=[jax.ShapeDtypeStruct(shape, kind) for shape, kind in outs],
        in_specs=[SMEM] * len(scalars) + [VMEM] * len(arrays),
        out_specs=[VMEM] * len(outs),
        compiler_params=pltpu.CompilerParams(vmem_limit_bytes=32 * 1024 * 1024),
        cost_estimate=pl.CostEstimate(flops=flops, bytes_accessed=2_000_000, transcendentals=0),
    )(*scalars, *arrays))


def edge_coefs(shape, axis):
    at = lax.broadcasted_iota(jnp.int32, shape, axis)
    size = shape[axis]
    return (
        jnp.where(at < size - 1, C_NEAR, 0.0).astype(F32),
        jnp.where(at >= 1, C_NEAR, 0.0).astype(F32),
        jnp.where(at < size - 2, C_FAR, 0.0).astype(F32),
        jnp.where(at >= 2, C_FAR, 0.0).astype(F32),
    )


def in_row(row, coefs, axis):
    size = row.shape[axis]
    near = coefs[0] * pltpu.roll(row, size - 1, axis) - coefs[1] * pltpu.roll(row, 1, axis)
    far = coefs[2] * pltpu.roll(row, size - 2, axis) - coefs[3] * pltpu.roll(row, 2, axis)
    return near - far


def across(rows, out, sign):
    near, far = sign * C_NEAR, sign * C_FAR
    return near * (rows(out + 1) - rows(out - 1)) - far * (rows(out + 2) - rows(out - 2))


def sign_of(place, side):
    return (1.0 - 2.0 * place[FLIP].astype(F32)) * (1.0 - 2.0 * side)


def row_of(place, side, out, tile_x):
    x = tile_x // 2 - 1 - out if side else tile_x // 2 + out
    return x + place[FLIP] * (tile_x - 1 - 2 * x)


def assemble(place, *refs):
    count = len(refs) - 10
    tiles, sides = refs[:count], (refs[count : count + 5], refs[count + 5 :])
    tile_x, tile_y = tiles[0].shape[1:3]
    for side, (vel, middle, edge, cells, face) in enumerate(sides):
        for turn, tile in enumerate(tiles):
            spot = pl.ds(pl.multiple_of((place[ME] ^ turn) * tile_y, tile_y), tile_y)
            for out in range(DEEP):
                row = row_of(place, side, out, tile_x)
                for comp in range(3):
                    vel[comp, out, spot, :] = tile[comp, row]
                part, at = (middle, out) if out < REACH else (edge, out - REACH)
                for comp in range(6):
                    part[comp, at, spot, :] = tile[3 + comp, row]
                cells[out, spot, :] = tile[9, row]
                if out >= REACH:
                    for at, comp in enumerate(ALONG_X + (6,)):
                        face[at, out - REACH, spot, :] = tile[3 + comp, row]


def push(place, side, amount, stress_row, vel, light, vel_out, sent):
    shape = vel.shape[2:]
    coef_y, coef_z = edge_coefs(shape, 0), edge_coefs(shape, 1)
    sign = sign_of(place, side)
    spot = (lax.broadcasted_iota(jnp.int32, shape, 0) == place[SPOT_Y]) & (
        lax.broadcasted_iota(jnp.int32, shape, 1) == 0
    )
    spot = jnp.where(spot, amount, 0.0)
    rows = [functools.partial(stress_row, comp) for comp in range(6)]
    for out in reversed(range(DEEP)):
        xy, xz, yz = rows[3](out), rows[4](out), rows[5](out)
        force_x = across(rows[0], out, sign) + in_row(xy, coef_y, 0) + in_row(xz, coef_z, 1)
        force_y = across(rows[3], out, sign) + in_row(rows[1](out), coef_y, 0) + in_row(yz, coef_z, 1)
        force_z = across(rows[4], out, sign) + in_row(yz, coef_y, 0) + in_row(rows[2](out), coef_z, 1)
        here = place[SPOT_X] == (-1 - out if side else out)
        force_z = force_z + jnp.where(here, 1.0, 0.0) * spot
        near = DEEP - 1 - out
        for comp, force in enumerate((force_x, force_y, force_z)):
            fresh = vel[comp, out] + light[out] * force
            vel_out[comp, out] = fresh
            high = fresh.astype(BF16)
            if near < NEAR_ROWS:
                sent[comp * PACKED + 2 * near] = high
                sent[comp * PACKED + 2 * near + 1] = (fresh - high.astype(F32)).astype(BF16)
            else:
                sent[comp * PACKED + NEAR_ROWS + near] = high


def from_halo(halo, comp, near):
    if near < NEAR_ROWS:
        at = comp * PACKED + 2 * near
        return halo[at].astype(F32) + halo[at + 1].astype(F32)
    return halo[comp * PACKED + NEAR_ROWS + near].astype(F32)


def first(side, place, table, residual, vel, middle, other, edge, cells, halo, *outs):
    vel_out, sent, light, lame, shear, halo_out = outs
    count = table.shape[0]
    for out in range(DEEP + REACH):
        if out < DEEP:
            number, share = cells[out], 1.0
        else:
            number = halo[len(ALONG_X), REACH - 1 - (out - DEEP)]
            share = jnp.where(place[HAS_LOW if side else HAS_HIGH] > 0, 1.0, 0.0)
        parts = [jnp.full(number.shape, table[0, c], F32) for c in range(3)]
        for m in range(1, count):
            hit = number == float(m)
            parts = [jnp.where(hit, table[m, c], parts[c]) for c in range(3)]
        lame[out] = (TIME_STEP * STIFFNESS * share) * parts[1]
        shear[out] = (2.0 * TIME_STEP * STIFFNESS * share) * parts[2]
        if out < DEEP:
            light[out] = TIME_STEP / parts[0]
    for at in range(len(ALONG_X)):
        for near in range(REACH):
            halo_out[at, near] = halo[at, REACH - 1 - near]
    amount = AMPLITUDE * residual[place[ME], 0]
    push(place, side, amount, stress_rows(middle, other, edge, halo_out), vel, light, vel_out, sent)


def stress_rows(middle, other, edge, halo):
    def row(comp, out):
        if out < 0:
            return other[comp, -1 - out]
        if out < REACH:
            return middle[comp, out]
        if out < DEEP:
            return edge[comp, out - REACH]
        return halo[ALONG_X.index(comp), out - DEEP]

    return row


def strain_rate(vx, vy, vz, out, sign, coef_y, coef_z, full):
    x, y, z = vx(out), vy(out), vz(out)
    rates = [
        across(vx, out, sign),
        in_row(y, coef_y, 0),
        in_row(z, coef_z, 1),
        0.5 * (in_row(x, coef_y, 0) + across(vy, out, sign)),
        0.5 * (in_row(x, coef_z, 1) + across(vz, out, sign)),
    ]
    if full:
        rates.append(0.5 * (in_row(y, coef_z, 1) + in_row(z, coef_y, 0)))
    return rates


def renew(rates, lame, shear, before):
    bulk = lame * (rates[0] + rates[1] + rates[2])
    return {
        comp: old + (bulk + shear * rates[comp] if comp < 3 else shear * rates[comp])
        for comp, old in before.items()
    }


def outer(side, moment, last, place, residual, vel, halo, edge, *refs):
    if last:
        (rates_out,) = refs
    else:
        old_halo, middle, other, light, lame, shear, rates_out, edge_out, halo_out, vel_out, sent = refs
    shape = vel.shape[2:]
    coef_y, coef_z = edge_coefs(shape, 0), edge_coefs(shape, 1)
    sign = sign_of(place, side)

    def rows(comp):
        return lambda out: vel[comp, out] if out < DEEP else from_halo(halo, comp, out - DEEP)

    vx, vy, vz = rows(0), rows(1), rows(2)
    for out in range(REACH, DEEP if last else DEEP + REACH):
        own = out < DEEP
        rates = strain_rate(vx, vy, vz, out, sign, coef_y, coef_z, own)
        if own:
            for comp in range(6):
                rates_out[comp, out - REACH] = rates[comp]
        if last:
            continue
        if own:
            fresh = renew(rates, lame[out], shear[out], {comp: edge[comp, out - REACH] for comp in range(6)})
            for comp, value in fresh.items():
                edge_out[comp, out - REACH] = value
        else:
            before = {comp: old_halo[at, out - DEEP] for at, comp in enumerate(ALONG_X)}
            fresh = renew(rates, lame[out], shear[out], before)
            for at, comp in enumerate(ALONG_X):
                halo_out[at, out - DEEP] = fresh[comp]
    if not last:
        amount = AMPLITUDE * residual[place[ME], moment + 1]
        push(place, side, amount, stress_rows(middle, other, edge_out, halo_out), vel, light, vel_out, sent)


def inner(last, place, *refs):
    vels = refs[:2]
    shape = vels[0].shape[2:]
    coef_y, coef_z = edge_coefs(shape, 0), edge_coefs(shape, 1)
    if last:
        rates_out = refs[2:]
    else:
        middles, lames, shears = refs[2:4], refs[4:6], refs[6:8]
        rates_out, middles_out = refs[8:10], refs[10:12]
    for side in range(2):
        sign = sign_of(place, side)

        def rows(comp):
            return lambda out: vels[side][comp, out] if out >= 0 else vels[1 - side][comp, -1 - out]

        for out in range(REACH):
            rates = strain_rate(rows(0), rows(1), rows(2), out, sign, coef_y, coef_z, True)
            for comp in range(6):
                rates_out[side][comp, out] = rates[comp]
            if not last:
                before = {comp: middles[side][comp, out] for comp in range(6)}
                fresh = renew(rates, lames[side][out], shears[side][out], before)
                for comp, value in fresh.items():
                    middles_out[side][comp, out] = value


def correlate(moments, pieces, place, residual, *refs):
    rates, sources, terms = refs[: 4 * moments], refs[4 * moments : 4 * moments + pieces], refs[-1]
    tile_x, tile_y = sources[0].shape[2:4]
    for turn in range(pieces):
        spot = pl.ds(pl.multiple_of((place[ME] ^ turn) * tile_y, tile_y), tile_y)
        for side in range(2):
            for out in range(DEEP):
                row = row_of(place, side, out, tile_x)
                lam = mu = None
                for moment in range(moments):
                    weight = KERNEL_SCALE * residual[place[ME], moment]
                    held = rates[4 * moment + 2 * (out // REACH) + side]
                    rate = [held[c, out % REACH, spot, :] for c in range(6)]
                    source = [sources[turn][moment, c, row] for c in range(6)]
                    bulk = (source[0] + source[1] + source[2]) * (rate[0] + rate[1] + rate[2])
                    diag = source[0] * rate[0] + source[1] * rate[1] + source[2] * rate[2]
                    off = source[3] * rate[3] + source[4] * rate[4] + source[5] * rate[5]
                    bulk, both = weight * bulk, (2.0 * weight) * (diag + 2.0 * off)
                    lam = bulk if lam is None else lam + bulk
                    mu = both if mu is None else mu + both
                terms[turn, 0, row] = lam
                terms[turn, 1, row] = mu


def swap(array, axis, turn):
    count = lax.axis_size(axis)
    return lax.ppermute(array, axis, [(i, i ^ turn) for i in range(count)])


def partner(slab, piece, slabs, side):
    other = slab + 1 - 2 * ((slab + piece + side) % 2)
    return other, (other >= 0) & (other < slabs)


def to_neighbour(face, side):
    slabs, pieces = lax.axis_size("gx"), lax.axis_size("gy")
    pairs = []
    for slab in range(slabs):
        for piece in range(pieces):
            other, inside = partner(slab, piece, slabs, side)
            if inside:
                pairs.append((slab * pieces + piece, other * pieces + piece))
    return lax.ppermute(face, ("gx", "gy"), pairs)


def local(rec_state, source_strain, material, material_table, residual, rec_cell, listed, src_pick):
    state = rec_state[0]
    receivers, _, tile_x, tile_y, depth = state.shape
    pieces, slabs, groups = lax.axis_size("gy"), lax.axis_size("gx"), lax.axis_size("sta")
    assert receivers == pieces and tile_x == 2 * DEEP
    assert pieces & (pieces - 1) == 0 and groups & (groups - 1) == 0
    size_y = pieces * tile_y
    group, slab, me = lax.axis_index("sta"), lax.axis_index("gx"), lax.axis_index("gy")
    moments = residual.shape[2]

    numbers = material.astype(F32)[None]
    chunks = []
    for turn in range(pieces):
        mine = lax.dynamic_index_in_dim(state, me ^ turn, 0, keepdims=False)
        mine = jnp.concatenate([mine, numbers], 0)
        chunks.append(swap(mine, "gy", turn) if turn else mine)

    strains = [swap(source_strain[0], "sta", turn) if turn else source_strain[0] for turn in range(groups)]

    cell = lax.dynamic_index_in_dim(rec_cell[0], me, 0, keepdims=False)
    flip = (slab + me) % 2
    spot_x = cell // size_y - slab * tile_x
    spot_x = spot_x + flip * (tile_x - 1 - 2 * spot_x) - tile_x // 2
    inside = [partner(slab, me, slabs, side)[1] for side in range(2)]
    place = jnp.stack([me, flip, *inside, spot_x, cell % size_y]).astype(jnp.int32)
    rows = residual[0]

    def shape(*lead, kind=F32):
        return lead + (size_y, depth), kind

    vel_shape, pair_shape = shape(3, DEEP), shape(6, REACH)
    halo_shape, sent_shape = shape(3, REACH), shape(3 * PACKED, kind=BF16)

    results = call(
        assemble,
        [vel_shape, pair_shape, pair_shape, shape(DEEP), shape(4, REACH)] * 2,
        ([place], chunks),
    )
    vels, middles, edges, cells, faces = ([results[at], results[5 + at]] for at in range(5))
    halos = [to_neighbour(faces[side], side) for side in range(2)]

    strains, vels = lax.optimization_barrier((strains, vels))
    weights = lax.dynamic_slice_in_dim(listed, group, 1, 2)[:, :, 0].astype(F32)
    combined = 0.0
    for turn in range(groups):
        factor = jnp.sum(weights * (src_pick == (group ^ turn)).astype(F32), 0)
        combined = combined + factor[:, None, None, None, None] * strains[turn].astype(F32)
    width = pieces // 2
    found = {0: combined}
    if width:
        found[width] = swap(combined, "gy", width)
        width //= 2

    sent, lights, lames, shears, old_halos = ([None, None] for _ in range(5))
    fresh = [None, None]
    for side in range(2):
        fresh[side], sent[side], lights[side], lames[side], shears[side], old_halos[side] = call(
            functools.partial(first, side),
            [vel_shape, sent_shape, shape(DEEP), shape(DEEP + REACH), shape(DEEP + REACH), halo_shape],
            (
                [place, material_table, rows],
                [vels[side], middles[side], middles[1 - side], edges[side], cells[side], halos[side]],
            ),
        )
        sent[side] = to_neighbour(sent[side], side)
    vels = fresh

    rates = []
    for moment in range(moments):
        last = moment == moments - 1
        if moment == 3 * moments // 4:
            found, vels = lax.optimization_barrier((found, vels))
            while width:
                for turn in list(found):
                    found[turn ^ width] = swap(found[turn], "gy", width)
                width //= 2
        results = call(
            functools.partial(inner, last),
            [pair_shape] * (2 if last else 4),
            ([place], vels if last else vels + middles + lames + shears),
        )
        rates += results[:2]
        if not last:
            middles = results[2:]
        fresh = [None, None]
        for side in range(2):
            arrays = [vels[side], sent[side], edges[side]]
            outs = [pair_shape]
            if not last:
                arrays += [old_halos[side], middles[side], middles[1 - side]]
                arrays += [lights[side], lames[side], shears[side]]
                outs += [pair_shape, halo_shape, vel_shape, sent_shape]
            results = call(functools.partial(outer, side, moment, last), outs, ([place, rows], arrays))
            rates.append(results[0])
            if not last:
                edges[side], old_halos[side], fresh[side] = results[1:4]
                sent[side] = to_neighbour(results[4], side)
        vels = fresh

    (terms,) = call(
        functools.partial(correlate, moments, pieces),
        [((pieces, 2, tile_x, tile_y, depth), F32)],
        ([place, rows], rates + [found[turn] for turn in range(pieces)]),
    )
    held = {turn: terms[turn] for turn in range(pieces)}
    width = 1
    while width < pieces:
        keep = [turn for turn in held if not turn & width]
        got = swap(jnp.stack([held[turn ^ width] for turn in keep]), "gy", width)
        held = {turn: held[turn] + got[at] for at, turn in enumerate(keep)}
        width *= 2
    total = held[0]
    share = tile_x // groups
    result = lax.dynamic_slice_in_dim(total, group * share, share, 1)
    for turn in range(1, groups):
        part = lax.dynamic_slice_in_dim(total, (group ^ turn) * share, share, 1)
        result = result + swap(part, "sta", turn)
    return result


def solution(mesh):
    in_specs = (
        P("sta", None, None, "gx", "gy", None),
        P("sta", None, None, "gx", "gy", None),
        P("gx", "gy", None),
        P(),
        P("sta", None, None),
        P("sta", None),
        P(),
        P(),
    )
    out_specs = P(None, ("gx", "sta"), "gy", None)
    return jax.shard_map(local, mesh=mesh, in_specs=in_specs, out_specs=out_specs, check_vma=False)
```

```python
import functools

import jax
import jax.numpy as jnp
from jax import lax
from jax.experimental import pallas as pl
from jax.experimental.pallas import tpu as pltpu
from jax.sharding import PartitionSpec as P

NEAR = 8.0
UNIT = 12.0
SUBLANES = 8
TIME_STEP = 0.25
AMPLITUDE = 4.0
KERNEL_SCALE = 0.0625
STIFFNESS = 0.3
REACH = 2
DEEP = 2 * REACH
ALONG_X = (0, 3, 4)
ME, FLIP, HAS_HIGH, HAS_LOW, SPOT_X, SPOT_Y = range(6)
NEAR_ROWS = 2
PACKED = DEEP + NEAR_ROWS

VMEM = pl.BlockSpec(memory_space=pltpu.VMEM)
SMEM = pl.BlockSpec(memory_space=pltpu.SMEM)
F32, BF16 = jnp.float32, jnp.bfloat16


def call(body, outs, ins, scratch=(), flops=1_000_000):
    scalars, arrays = ins
    return list(pl.pallas_call(
        body,
        out_shape=[jax.ShapeDtypeStruct(shape, kind) for shape, kind in outs],
        in_specs=[SMEM] * len(scalars) + [VMEM] * len(arrays),
        out_specs=[VMEM] * len(outs),
        scratch_shapes=list(scratch),
        compiler_params=pltpu.CompilerParams(vmem_limit_bytes=6 * 1024 * 1024),
        cost_estimate=pl.CostEstimate(flops=flops, bytes_accessed=2_000_000, transcendentals=0),
    )(*scalars, *arrays))


def band(depth):
    row = lax.broadcasted_iota(jnp.int32, (depth, depth), 0)
    step = row - lax.broadcasted_iota(jnp.int32, (depth, depth), 1)
    parts = jnp.where(step == 1, NEAR, 0.0) - jnp.where(step == -1, NEAR, 0.0)
    parts = parts - jnp.where(step == 2, 1.0, 0.0) + jnp.where(step == -2, 1.0, 0.0)
    parts = parts.astype(BF16)
    return jnp.concatenate([parts, parts], 0)


def along_depth(rows):
    stacked = jnp.concatenate(rows, 0)
    high = stacked.astype(BF16)
    low = (stacked - high.astype(F32)).astype(BF16)
    split = jnp.concatenate([high, low], 1)
    result = jnp.dot(split, band(stacked.shape[1]), preferred_element_type=F32)
    size = rows[0].shape[0]
    return [result[at * size : (at + 1) * size] for at in range(len(rows))]


def along_y(row):
    count = row.shape[0] // SUBLANES
    at = lax.broadcasted_iota(jnp.int32, (SUBLANES, row.shape[1]), 0)
    planes = [row[SUBLANES * p : SUBLANES * (p + 1)] for p in range(count)]
    before = [jnp.where(at > 0, pltpu.roll(plane, 1, 0), 0.0) for plane in planes[-2:]]
    after = [jnp.where(at < SUBLANES - 1, pltpu.roll(plane, SUBLANES - 1, 0), 0.0) for plane in planes[:2]]
    spread = before + planes + after

    def shifted(by):
        return jnp.concatenate(spread[2 + by : 2 + by + count], 0)

    return shifted(1) - shifted(-1), shifted(2) - shifted(-2)


def across(rows, out, side):
    near, far = rows(out + 1) - rows(out - 1), rows(out + 2) - rows(out - 2)
    return (-near, -far) if side else (near, far)


def across_and_along(rows, out, side, row):
    near_y, far_y = along_y(row)
    near, far = rows(out + 1) - rows(out - 1), rows(out + 2) - rows(out - 2)
    if side:
        return NEAR * (near_y - near) - (far_y - far)
    return NEAR * (near_y + near) - (far_y + far)


def derivative(pair):
    return NEAR * pair[0] - pair[1]


MIRRORED_VEL = (0,)
MIRRORED_STRESS = (3, 4)


def sign_of(place):
    return 1.0 - 2.0 * place[FLIP].astype(F32)


def row_of(place, side, out, tile_x):
    x = tile_x // 2 - 1 - out if side else tile_x // 2 + out
    return x + place[FLIP] * (tile_x - 1 - 2 * x)


def interleave(place, tiles, comp, row, held):
    tile_y = tiles[0].shape[2]
    for turn, tile in enumerate(tiles):
        held[pl.ds(pl.multiple_of((place[ME] ^ turn) * tile_y, tile_y), tile_y), :] = tile[comp, row]
    count = held.shape[0] // SUBLANES
    return jnp.concatenate([held[pl.ds(p, SUBLANES, stride=count), :] for p in range(count)], 0)


def assemble_stress(place, *refs):
    count = len(refs) - 9
    tiles, sides, held = refs[:count], (refs[count : count + 4], refs[count + 4 : -1]), refs[-1]
    tile_x = tiles[0].shape[1]
    sign = sign_of(place)
    for side, (middle, edge, cells, face) in enumerate(sides):
        for out in range(DEEP):
            row = row_of(place, side, out, tile_x)
            part, at = (middle, out) if out < REACH else (edge, out - REACH)
            for comp in range(7):
                value = interleave(place, tiles, comp, row, held.at[(out * 7 + comp) % held.shape[0]])
                if comp in MIRRORED_STRESS:
                    value = sign * value
                if comp < 6:
                    part[comp, at] = value
                else:
                    cells[out] = value
                if out >= REACH and comp in ALONG_X + (6,):
                    face[(ALONG_X + (6,)).index(comp), out - REACH] = value


def assemble_vel(place, *refs):
    count = len(refs) - 3
    tiles, vels, held = refs[:count], refs[count:-1], refs[-1]
    tile_x = tiles[0].shape[1]
    sign = sign_of(place)
    for side, vel in enumerate(vels):
        for out in range(DEEP):
            row = row_of(place, side, out, tile_x)
            for comp in range(3):
                value = interleave(place, tiles, comp, row, held.at[(out * 3 + comp) % held.shape[0]])
                vel[comp, out] = sign * value if comp in MIRRORED_VEL else value


def push(place, side, amount, stress_row, vel, light, vel_out, sent):
    shape = vel.shape[2:]
    spot = (lax.broadcasted_iota(jnp.int32, shape, 0) == place[SPOT_Y]) & (
        lax.broadcasted_iota(jnp.int32, shape, 1) == 0
    )
    spot = jnp.where(spot, UNIT * amount, 0.0)
    rows = [functools.partial(stress_row, comp) for comp in range(6)]
    deep = along_depth([rows[comp](out) for out in range(DEEP) for comp in (4, 5, 2)])
    for out in range(DEEP):
        force_x = across_and_along(rows[0], out, side, rows[3](out)) + deep[3 * out]
        force_y = across_and_along(rows[3], out, side, rows[1](out)) + deep[3 * out + 1]
        force_z = across_and_along(rows[4], out, side, rows[5](out)) + deep[3 * out + 2]
        here = place[SPOT_X] == (-1 - out if side else out)
        force_z = force_z + jnp.where(here, 1.0, 0.0) * spot
        near = DEEP - 1 - out
        for comp, force in enumerate((force_x, force_y, force_z)):
            fresh = vel[comp, out] + light[out] * force
            vel_out[comp, out] = fresh
            if comp in MIRRORED_VEL:
                fresh = -fresh
            high = fresh.astype(BF16)
            if near < NEAR_ROWS:
                sent[comp * PACKED + 2 * near] = high
                sent[comp * PACKED + 2 * near + 1] = (fresh - high.astype(F32)).astype(BF16)
            else:
                sent[comp * PACKED + NEAR_ROWS + near] = high


def from_halo(halo, comp, near):
    if near < NEAR_ROWS:
        at = comp * PACKED + 2 * near
        return halo[at].astype(F32) + halo[at + 1].astype(F32)
    return halo[comp * PACKED + NEAR_ROWS + near].astype(F32)


def first(side, place, table, residual, vel, middle, other, edge, cells, halo, *outs):
    vel_out, sent, light, lame, shear, halo_out = outs
    count = table.shape[0]
    for out in range(DEEP + REACH):
        if out < DEEP:
            number, share = cells[out], 1.0
        else:
            number = halo[len(ALONG_X), REACH - 1 - (out - DEEP)]
            share = jnp.where(place[HAS_LOW if side else HAS_HIGH] > 0, 1.0, 0.0)
        parts = [jnp.full(number.shape, table[0, c], F32) for c in range(3)]
        for m in range(1, count):
            hit = number == float(m)
            parts = [jnp.where(hit, table[m, c], parts[c]) for c in range(3)]
        lame[out] = (TIME_STEP * STIFFNESS / UNIT * share) * parts[1]
        shear[out] = (TIME_STEP * STIFFNESS / UNIT * share) * parts[2]
        if out < DEEP:
            light[out] = (TIME_STEP / UNIT) / parts[0]
    for at in range(len(ALONG_X)):
        for near in range(REACH):
            value = halo[at, REACH - 1 - near]
            halo_out[at, near] = -value if ALONG_X[at] in MIRRORED_STRESS else value
    amount = AMPLITUDE * residual[place[ME], 0]
    push(place, side, amount, stress_rows(middle, other, edge, halo_out), vel, light, vel_out, sent)


def stress_rows(middle, other, edge, halo):
    def row(comp, out):
        if out < 0:
            return other[comp, -1 - out]
        if out < REACH:
            return middle[comp, out]
        if out < DEEP:
            return edge[comp, out - REACH]
        return halo[ALONG_X.index(comp), out - DEEP]

    return row


def strain_rates(vx, vy, vz, side, first_out, last_out, full_out):
    outs = range(first_out, last_out)
    wanted = [(vel, out) for out in outs for vel in (vx, vz)] + [(vy, out) for out in outs if out < full_out]
    deep = along_depth([vel(out) for vel, out in wanted])
    deep = {key: value for key, value in zip(wanted, deep)}
    for out in outs:
        rates = [
            derivative(across(vx, out, side)),
            derivative(along_y(vy(out))),
            deep[vz, out],
            across_and_along(vy, out, side, vx(out)),
            deep[vx, out] + derivative(across(vz, out, side)),
        ]
        if out < full_out:
            rates.append(deep[vy, out] + derivative(along_y(vz(out))))
        yield out, rates


def store(target, at, rates):
    count = rates[0].shape[0] // SUBLANES
    for comp, rate in enumerate(rates):
        for p in range(count):
            spot = pl.ds(p, SUBLANES, stride=count)
            target[comp, at, spot, :] = rate[SUBLANES * p : SUBLANES * (p + 1)]


def renew(rates, lame, shear, before):
    bulk = lame * (rates[0] + rates[1] + rates[2])
    twice = shear + shear
    return {
        comp: old + (bulk + twice * rates[comp] if comp < 3 else shear * rates[comp])
        for comp, old in before.items()
    }


def outer(side, moment, last, place, residual, vel, halo, edge, *refs):
    if last:
        (rates_out,) = refs
    else:
        old_halo, middle, other, light, lame, shear, rates_out, edge_out, halo_out, vel_out, sent = refs

    def rows(comp):
        return lambda out: vel[comp, out] if out < DEEP else from_halo(halo, comp, out - DEEP)

    until = DEEP if last else DEEP + REACH
    for out, rates in strain_rates(rows(0), rows(1), rows(2), side, REACH, until, DEEP):
        own = out < DEEP
        if own:
            store(rates_out, out - REACH, rates)
        if last:
            continue
        if own:
            fresh = renew(rates, lame[out], shear[out], {comp: edge[comp, out - REACH] for comp in range(6)})
            for comp, value in fresh.items():
                edge_out[comp, out - REACH] = value
        else:
            before = {comp: old_halo[at, out - DEEP] for at, comp in enumerate(ALONG_X)}
            fresh = renew(rates, lame[out], shear[out], before)
            for at, comp in enumerate(ALONG_X):
                halo_out[at, out - DEEP] = fresh[comp]
    if not last:
        amount = AMPLITUDE * residual[place[ME], moment + 1]
        push(place, side, amount, stress_rows(middle, other, edge_out, halo_out), vel, light, vel_out, sent)


def inner(last, place, *refs):
    vels = refs[:2]
    if last:
        rates_out = refs[2:]
    else:
        middles, lames, shears = refs[2:4], refs[4:6], refs[6:8]
        rates_out, middles_out = refs[8:10], refs[10:12]
    for side in range(2):

        def rows(comp):
            return lambda out: vels[side][comp, out] if out >= 0 else vels[1 - side][comp, -1 - out]

        for out, rates in strain_rates(rows(0), rows(1), rows(2), side, 0, REACH, REACH):
            store(rates_out[side], out, rates)
            if not last:
                before = {comp: middles[side][comp, out] for comp in range(6)}
                fresh = renew(rates, lames[side][out], shears[side][out], before)
                for comp, value in fresh.items():
                    middles_out[side][comp, out] = value


def correlate(moments, pieces, place, residual, *refs):
    rates, sources, terms = refs[: 4 * moments], refs[4 * moments : 4 * moments + pieces], refs[-1]
    tile_x, tile_y = sources[0].shape[2:4]
    sign = sign_of(place)
    for turn in range(pieces):
        spot = pl.ds(pl.multiple_of((place[ME] ^ turn) * tile_y, tile_y), tile_y)
        for side in range(2):
            for out in range(DEEP):
                row = row_of(place, side, out, tile_x)
                lam = mu = None
                for moment in range(moments):
                    weight = (KERNEL_SCALE / UNIT) * residual[place[ME], moment]
                    held = rates[4 * moment + 2 * (out // REACH) + side]
                    rate = [held[c, out % REACH, spot, :] for c in range(6)]
                    source = [sources[turn][moment, c, row] for c in range(6)]
                    bulk = (source[0] + source[1] + source[2]) * (rate[0] + rate[1] + rate[2])
                    diag = source[0] * rate[0] + source[1] * rate[1] + source[2] * rate[2]
                    off = sign * (source[3] * rate[3] + source[4] * rate[4]) + source[5] * rate[5]
                    bulk, both = weight * bulk, (2.0 * weight) * (diag + off)
                    lam = bulk if lam is None else lam + bulk
                    mu = both if mu is None else mu + both
                terms[turn, 0, row] = lam
                terms[turn, 1, row] = mu


def swap(array, axis, turn):
    count = lax.axis_size(axis)
    return lax.ppermute(array, axis, [(i, i ^ turn) for i in range(count)])


def partner(slab, piece, slabs, side):
    other = slab + 1 - 2 * ((slab + piece + side) % 2)
    return other, (other >= 0) & (other < slabs)


def to_neighbour(face, side):
    slabs, pieces = lax.axis_size("gx"), lax.axis_size("gy")
    pairs = []
    for slab in range(slabs):
        for piece in range(pieces):
            other, inside = partner(slab, piece, slabs, side)
            if inside:
                pairs.append((slab * pieces + piece, other * pieces + piece))
    return lax.ppermute(face, ("gx", "gy"), pairs)


def local(rec_state, source_strain, material, material_table, residual, rec_cell, listed, src_pick):
    state = rec_state[0]
    receivers, _, tile_x, tile_y, depth = state.shape
    pieces, slabs, groups = lax.axis_size("gy"), lax.axis_size("gx"), lax.axis_size("sta")
    assert receivers == pieces and tile_x == 2 * DEEP
    assert pieces & (pieces - 1) == 0 and groups & (groups - 1) == 0
    size_y = pieces * tile_y
    group, slab, me = lax.axis_index("sta"), lax.axis_index("gx"), lax.axis_index("gy")
    moments = residual.shape[2]

    numbers = material.astype(F32)[None]
    picked = [lax.dynamic_index_in_dim(state, me ^ turn, 0, keepdims=False) for turn in range(pieces)]
    order = sorted(range(pieces), reverse=True)
    stresses = {turn: jnp.concatenate([picked[turn][3:], numbers], 0) for turn in order}
    stresses = {turn: swap(stresses[turn], "gy", turn) if turn else stresses[turn] for turn in order}
    speeds = {turn: swap(picked[turn][:3], "gy", turn) if turn else picked[turn][:3] for turn in order}
    strains = [swap(source_strain[0], "sta", turn) if turn else source_strain[0] for turn in range(groups)]

    cell = lax.dynamic_index_in_dim(rec_cell[0], me, 0, keepdims=False)
    flip = (slab + me) % 2
    spot_x = cell // size_y - slab * tile_x
    spot_x = spot_x + flip * (tile_x - 1 - 2 * spot_x) - tile_x // 2
    inside = [partner(slab, me, slabs, side)[1] for side in range(2)]
    planes = size_y // SUBLANES
    spot_y = cell % size_y
    spot_y = (spot_y % planes) * SUBLANES + spot_y // planes
    place = jnp.stack([me, flip, *inside, spot_x, spot_y]).astype(jnp.int32)
    rows = residual[0]

    def shape(*lead, kind=F32):
        return lead + (size_y, depth), kind

    vel_shape, pair_shape = shape(3, DEEP), shape(6, REACH)
    halo_shape, sent_shape = shape(3, REACH), shape(3 * PACKED, kind=BF16)

    held = [pltpu.VMEM((8, size_y, depth), F32)]
    results = call(
        assemble_stress,
        [pair_shape, pair_shape, shape(DEEP), shape(4, REACH)] * 2,
        ([place], [stresses[turn] for turn in range(pieces)]),
        held,
    )
    middles, edges, cells, faces = ([results[at], results[4 + at]] for at in range(4))
    halos = [to_neighbour(faces[side], side) for side in range(2)]
    vels = call(
        assemble_vel, [vel_shape] * 2, ([place], [speeds[turn] for turn in range(pieces)]), held
    )

    sent, lights, lames, shears, old_halos = ([None, None] for _ in range(5))
    fresh = [None, None]
    for side in range(2):
        fresh[side], sent[side], lights[side], lames[side], shears[side], old_halos[side] = call(
            functools.partial(first, side),
            [vel_shape, sent_shape, shape(DEEP), shape(DEEP + REACH), shape(DEEP + REACH), halo_shape],
            (
                [place, material_table, rows],
                [vels[side], middles[side], middles[1 - side], edges[side], cells[side], halos[side]],
            ),
        )
        sent[side] = to_neighbour(sent[side], side)
    vels = fresh

    strains, vels = lax.optimization_barrier((strains, vels))
    weights = lax.dynamic_slice_in_dim(listed, group, 1, 2)[:, :, 0].astype(F32)
    combined = 0.0
    for turn in range(groups):
        factor = jnp.sum(weights * (src_pick == (group ^ turn)).astype(F32), 0)
        combined = combined + factor[:, None, None, None, None] * strains[turn].astype(F32)
    width = pieces // 2
    found = {0: combined}
    if width:
        found[width] = swap(combined, "gy", width)
        width //= 2

    rates = []
    for moment in range(moments):
        last = moment == moments - 1
        results = call(
            functools.partial(inner, last),
            [pair_shape] * (2 if last else 4),
            ([place], vels if last else vels + middles + lames + shears),
        )
        rates += results[:2]
        if not last:
            middles = results[2:]
        if moment == 3 * moments // 4:
            found, middles = lax.optimization_barrier((found, middles))
            while width:
                for turn in list(found):
                    found[turn ^ width] = swap(found[turn], "gy", width)
                width //= 2
        fresh = [None, None]
        for side in range(2):
            arrays = [vels[side], sent[side], edges[side]]
            outs = [pair_shape]
            if not last:
                arrays += [old_halos[side], middles[side], middles[1 - side]]
                arrays += [lights[side], lames[side], shears[side]]
                outs += [pair_shape, halo_shape, vel_shape, sent_shape]
            results = call(functools.partial(outer, side, moment, last), outs, ([place, rows], arrays))
            rates.append(results[0])
            if not last:
                edges[side], old_halos[side], fresh[side] = results[1:4]
                sent[side] = to_neighbour(results[4], side)
        vels = fresh

    (terms,) = call(
        functools.partial(correlate, moments, pieces),
        [((pieces, 2, tile_x, tile_y, depth), F32)],
        ([place, rows], rates + [found[turn] for turn in range(pieces)]),
    )
    held = {turn: terms[turn] for turn in range(pieces)}
    if pieces > 1:
        keep = [turn for turn in held if not turn & 1]
        got = swap(jnp.stack([held[turn ^ 1] for turn in keep]), "gy", 1)
        held = {turn: held[turn] + got[at] for at, turn in enumerate(keep)}
    share = tile_x // groups
    result = 0.0
    for across_sta in reversed(range(groups)):
        for turn in reversed(list(held)):
            part = lax.dynamic_slice_in_dim(held[turn], (group ^ across_sta) * share, share, 1)
            if across_sta or turn:
                pairs = [
                    (a * pieces + b, (a ^ across_sta) * pieces + (b ^ turn))
                    for a in range(groups)
                    for b in range(pieces)
                ]
                part = lax.ppermute(part, ("sta", "gy"), pairs)
            result = result + part
    return result


def solution(mesh):
    in_specs = (
        P("sta", None, None, "gx", "gy", None),
        P("sta", None, None, "gx", "gy", None),
        P("gx", "gy", None),
        P(),
        P("sta", None, None),
        P("sta", None),
        P(),
        P(),
    )
    out_specs = P(None, ("gx", "sta"), "gy", None)
    return jax.shard_map(local, mesh=mesh, in_specs=in_specs, out_specs=out_specs, check_vma=False)
```

```python
import functools

import jax
import jax.numpy as jnp
from jax import lax
from jax.experimental import pallas as pl
from jax.experimental.pallas import tpu as pltpu
from jax.sharding import PartitionSpec as P

NEAR = 8.0
UNIT = 12.0
SUBLANES = 8
TIME_STEP = 0.25
AMPLITUDE = 4.0
KERNEL_SCALE = 0.0625
STIFFNESS = 0.3
REACH = 2
DEEP = 2 * REACH
ALONG_X = (0, 3, 4)
NEAR_ROWS = 2
PACKED = DEEP + NEAR_ROWS

VMEM = pl.BlockSpec(memory_space=pltpu.VMEM)
SMEM = pl.BlockSpec(memory_space=pltpu.SMEM)
F32, BF16 = jnp.float32, jnp.bfloat16


def call(body, outs, ins, scratch=(), flops=1_000_000):
    scalars, arrays = ins
    return list(pl.pallas_call(
        body,
        out_shape=[jax.ShapeDtypeStruct(shape, kind) for shape, kind in outs],
        in_specs=[SMEM] * len(scalars) + [VMEM] * len(arrays),
        out_specs=[VMEM] * len(outs),
        scratch_shapes=list(scratch),
        compiler_params=pltpu.CompilerParams(vmem_limit_bytes=6 * 1024 * 1024),
        cost_estimate=pl.CostEstimate(flops=flops, bytes_accessed=2_000_000, transcendentals=0),
    )(*scalars, *arrays))


def band(depth):
    row = lax.broadcasted_iota(jnp.int32, (depth, depth), 0)
    step = row - lax.broadcasted_iota(jnp.int32, (depth, depth), 1)
    parts = jnp.where(step == 1, NEAR, 0.0) - jnp.where(step == -1, NEAR, 0.0)
    parts = parts - jnp.where(step == 2, 1.0, 0.0) + jnp.where(step == -2, 1.0, 0.0)
    parts = parts.astype(BF16)
    return jnp.concatenate([parts, parts], 0)


def along_depth(rows):
    stacked = jnp.concatenate(rows, 0)
    high = stacked.astype(BF16)
    low = (stacked - high.astype(F32)).astype(BF16)
    split = jnp.concatenate([high, low], 1)
    result = jnp.dot(split, band(stacked.shape[1]), preferred_element_type=F32)
    size = rows[0].shape[0]
    return [result[at * size : (at + 1) * size] for at in range(len(rows))]


def along_y(row):
    count = row.shape[0] // SUBLANES
    at = lax.broadcasted_iota(jnp.int32, (SUBLANES, row.shape[1]), 0)
    planes = [row[SUBLANES * p : SUBLANES * (p + 1)] for p in range(count)]
    before = [jnp.where(at > 0, pltpu.roll(plane, 1, 0), 0.0) for plane in planes[-2:]]
    after = [jnp.where(at < SUBLANES - 1, pltpu.roll(plane, SUBLANES - 1, 0), 0.0) for plane in planes[:2]]
    spread = before + planes + after

    def shifted(by):
        return jnp.concatenate(spread[2 + by : 2 + by + count], 0)

    return shifted(1) - shifted(-1), shifted(2) - shifted(-2)


def across(rows, out, side):
    near, far = rows(out + 1) - rows(out - 1), rows(out + 2) - rows(out - 2)
    return (-near, -far) if side else (near, far)


def across_and_along(rows, out, side, row):
    near_y, far_y = along_y(row)
    near, far = rows(out + 1) - rows(out - 1), rows(out + 2) - rows(out - 2)
    if side:
        return NEAR * (near_y - near) - (far_y - far)
    return NEAR * (near_y + near) - (far_y + far)


def derivative(pair):
    return NEAR * pair[0] - pair[1]


MIRRORED_VEL = (0,)
MIRRORED_STRESS = (3, 4)


def position():
    slab, me = lax.axis_index("gx"), lax.axis_index("gy")
    return slab, me, (slab + me) % 2


def sign_of(flip):
    return 1.0 - 2.0 * flip.astype(F32)


def row_of(flip, side, out, tile_x):
    x = tile_x // 2 - 1 - out if side else tile_x // 2 + out
    return x + flip * (tile_x - 1 - 2 * x)


def interleave(me, tiles, comp, row, held):
    tile_y = tiles[0].shape[2]
    for turn, tile in enumerate(tiles):
        held[pl.ds(pl.multiple_of((me ^ turn) * tile_y, tile_y), tile_y), :] = tile[comp, row]
    count = held.shape[0] // SUBLANES
    return jnp.concatenate([held[pl.ds(p, SUBLANES, stride=count), :] for p in range(count)], 0)


def assemble(*refs):
    count = len(refs) - 11
    tiles, sides, held = refs[:count], (refs[count : count + 5], refs[count + 5 : -1]), refs[-1]
    tile_x = tiles[0].shape[1]
    _, me, flip = position()
    sign = sign_of(flip)
    face_comps = tuple(3 + comp for comp in ALONG_X) + (9,)
    for side, (vel, middle, edge, cells, face) in enumerate(sides):
        for out in range(DEEP):
            row = row_of(flip, side, out, tile_x)
            part, at = (middle, out) if out < REACH else (edge, out - REACH)
            for comp in range(10):
                value = interleave(me, tiles, comp, row, held.at[(out * 10 + comp) % held.shape[0]])
                if comp in MIRRORED_VEL or comp - 3 in MIRRORED_STRESS:
                    value = sign * value
                if comp < 3:
                    vel[comp, out] = value
                elif comp < 9:
                    part[comp - 3, at] = value
                else:
                    cells[out] = value
                if out >= REACH and comp in face_comps:
                    face[face_comps.index(comp), out - REACH] = value


def push(side, spots, amount, stress_row, vel, light, vel_out, sent):
    rows = [functools.partial(stress_row, comp) for comp in range(6)]
    deep = along_depth([rows[comp](out) for out in range(DEEP) for comp in (4, 5, 2)])
    for out in range(DEEP):
        force_x = across_and_along(rows[0], out, side, rows[3](out)) + deep[3 * out]
        force_y = across_and_along(rows[3], out, side, rows[1](out)) + deep[3 * out + 1]
        force_z = across_and_along(rows[4], out, side, rows[5](out)) + deep[3 * out + 2]
        force_z = force_z + amount * spots[out]
        near = DEEP - 1 - out
        for comp, force in enumerate((force_x, force_y, force_z)):
            fresh = vel[comp, out] + light[out] * force
            vel_out[comp, out] = fresh
            if comp in MIRRORED_VEL:
                fresh = -fresh
            high = fresh.astype(BF16)
            if near < NEAR_ROWS:
                sent[comp * PACKED + 2 * near] = high
                sent[comp * PACKED + 2 * near + 1] = (fresh - high.astype(F32)).astype(BF16)
            else:
                sent[comp * PACKED + NEAR_ROWS + near] = high


def from_halo(halo, comp, near):
    if near < NEAR_ROWS:
        at = comp * PACKED + 2 * near
        return halo[at].astype(F32) + halo[at + 1].astype(F32)
    return halo[comp * PACKED + NEAR_ROWS + near].astype(F32)


def first(side, table, residual, rec_cell, vel, middle, other, edge, cells, halo, *outs):
    vel_out, sent, light, lame, shear, halo_out, spots, amounts = outs
    size_y, depth = vel.shape[2:]
    planes = size_y // SUBLANES
    slab, me, flip = position()
    cell = rec_cell[0, me]
    spot_x, spot_y = cell // size_y - slab * (2 * DEEP), cell % size_y
    spot_x = spot_x + flip * (2 * DEEP - 1 - 2 * spot_x)
    spot_y = (spot_y % planes) * SUBLANES + spot_y // planes
    at_spot = (lax.broadcasted_iota(jnp.int32, (size_y, depth), 0) == spot_y) & (
        lax.broadcasted_iota(jnp.int32, (size_y, depth), 1) == 0
    )
    for out in range(DEEP):
        here = spot_x == (DEEP - 1 - out if side else DEEP + out)
        spots[out] = jnp.where(at_spot, jnp.where(here, UNIT * AMPLITUDE, 0.0), 0.0)
    for moment in range(residual.shape[2]):
        amounts[moment] = jnp.full((size_y, depth), residual[0, me, moment], F32)
    _, inside = partner(slab, me, lax.axis_size("gx"), side)
    count = table.shape[0]
    for out in range(DEEP + REACH):
        if out < DEEP:
            number, share = cells[out], 1.0
        else:
            number = halo[len(ALONG_X), REACH - 1 - (out - DEEP)]
            share = jnp.where(inside, 1.0, 0.0)
        parts = [jnp.full(number.shape, table[0, c], F32) for c in range(3)]
        for m in range(1, count):
            hit = number == float(m)
            parts = [jnp.where(hit, table[m, c], parts[c]) for c in range(3)]
        lame[out] = (TIME_STEP * STIFFNESS / UNIT * share) * parts[1]
        shear[out] = (TIME_STEP * STIFFNESS / UNIT * share) * parts[2]
        if out < DEEP:
            light[out] = (TIME_STEP / UNIT) / parts[0]
    for at in range(len(ALONG_X)):
        for near in range(REACH):
            value = halo[at, REACH - 1 - near]
            halo_out[at, near] = -value if ALONG_X[at] in MIRRORED_STRESS else value
    push(side, spots, amounts[0], stress_rows(middle, other, edge, halo_out), vel, light, vel_out, sent)


def stress_rows(middle, other, edge, halo):
    def row(comp, out):
        if out < 0:
            return other[comp, -1 - out]
        if out < REACH:
            return middle[comp, out]
        if out < DEEP:
            return edge[comp, out - REACH]
        return halo[ALONG_X.index(comp), out - DEEP]

    return row


def strain_rates(vx, vy, vz, side, first_out, last_out, full_out):
    outs = range(first_out, last_out)
    wanted = [(vel, out) for out in outs for vel in (vx, vz)] + [(vy, out) for out in outs if out < full_out]
    deep = along_depth([vel(out) for vel, out in wanted])
    deep = {key: value for key, value in zip(wanted, deep)}
    for out in outs:
        rates = [
            derivative(across(vx, out, side)),
            derivative(along_y(vy(out))),
            deep[vz, out],
            across_and_along(vy, out, side, vx(out)),
            deep[vx, out] + derivative(across(vz, out, side)),
        ]
        if out < full_out:
            rates.append(deep[vy, out] + derivative(along_y(vz(out))))
        yield out, rates


def store(target, at, rates):
    count = rates[0].shape[0] // SUBLANES
    for comp, rate in enumerate(rates):
        for p in range(count):
            spot = pl.ds(p, SUBLANES, stride=count)
            target[comp, at, spot, :] = rate[SUBLANES * p : SUBLANES * (p + 1)]


def renew(rates, lame, shear, before):
    bulk = lame * (rates[0] + rates[1] + rates[2])
    twice = shear + shear
    return {
        comp: old + (bulk + twice * rates[comp] if comp < 3 else shear * rates[comp])
        for comp, old in before.items()
    }


def outer(side, moment, last, vel, halo, edge, *refs):
    if last:
        (rates_out,) = refs
    else:
        old_halo, middle, other, light, lame, shear, spots, amounts, rates_out, edge_out, halo_out, vel_out, sent = refs

    def rows(comp):
        return lambda out: vel[comp, out] if out < DEEP else from_halo(halo, comp, out - DEEP)

    until = DEEP if last else DEEP + REACH
    for out, rates in strain_rates(rows(0), rows(1), rows(2), side, REACH, until, DEEP):
        own = out < DEEP
        if own:
            store(rates_out, out - REACH, rates)
        if last:
            continue
        if own:
            fresh = renew(rates, lame[out], shear[out], {comp: edge[comp, out - REACH] for comp in range(6)})
            for comp, value in fresh.items():
                edge_out[comp, out - REACH] = value
        else:
            before = {comp: old_halo[at, out - DEEP] for at, comp in enumerate(ALONG_X)}
            fresh = renew(rates, lame[out], shear[out], before)
            for at, comp in enumerate(ALONG_X):
                halo_out[at, out - DEEP] = fresh[comp]
    if not last:
        rows = stress_rows(middle, other, edge_out, halo_out)
        push(side, spots, amounts[moment + 1], rows, vel, light, vel_out, sent)


def inner(last, *refs):
    vels = refs[:2]
    if last:
        rates_out = refs[2:]
    else:
        middles, lames, shears = refs[2:4], refs[4:6], refs[6:8]
        rates_out, middles_out = refs[8:10], refs[10:12]
    for side in range(2):

        def rows(comp):
            return lambda out: vels[side][comp, out] if out >= 0 else vels[1 - side][comp, -1 - out]

        for out, rates in strain_rates(rows(0), rows(1), rows(2), side, 0, REACH, REACH):
            store(rates_out[side], out, rates)
            if not last:
                before = {comp: middles[side][comp, out] for comp in range(6)}
                fresh = renew(rates, lames[side][out], shears[side][out], before)
                for comp, value in fresh.items():
                    middles_out[side][comp, out] = value


def correlate(moments, pieces, residual, *refs):
    count = len(moments)
    rates, sources, rest = refs[: 4 * count], refs[4 * count : 4 * count + pieces], refs[4 * count + pieces :]
    before, terms = rest[:-1], rest[-1]
    tile_x, tile_y = sources[0].shape[2:4]
    _, me, flip = position()
    sign = sign_of(flip)
    for turn in range(pieces):
        spot = pl.ds(pl.multiple_of((me ^ turn) * tile_y, tile_y), tile_y)
        for side in range(2):
            for out in range(DEEP):
                row = row_of(flip, side, out, tile_x)
                lam, mu = (before[0][turn, 0, row], before[0][turn, 1, row]) if before else (0.0, 0.0)
                for at, moment in enumerate(moments):
                    weight = (KERNEL_SCALE / UNIT) * residual[0, me, moment]
                    held = rates[4 * at + 2 * (out // REACH) + side]
                    rate = [held[c, out % REACH, spot, :] for c in range(6)]
                    source = [sources[turn][moment, c, row] for c in range(6)]
                    bulk = (source[0] + source[1] + source[2]) * (rate[0] + rate[1] + rate[2])
                    diag = source[0] * rate[0] + source[1] * rate[1] + source[2] * rate[2]
                    off = sign * (source[3] * rate[3] + source[4] * rate[4]) + source[5] * rate[5]
                    lam = lam + weight * bulk
                    mu = mu + (2.0 * weight) * (diag + off)
                terms[turn, 0, row] = lam
                terms[turn, 1, row] = mu


def swap(array, axis, turn):
    count = lax.axis_size(axis)
    return lax.ppermute(array, axis, [(i, i ^ turn) for i in range(count)])


def partner(slab, piece, slabs, side):
    other = slab + 1 - 2 * ((slab + piece + side) % 2)
    return other, (other >= 0) & (other < slabs)


def to_neighbour(face, side):
    slabs, pieces = lax.axis_size("gx"), lax.axis_size("gy")
    pairs = []
    for slab in range(slabs):
        for piece in range(pieces):
            other, inside = partner(slab, piece, slabs, side)
            if inside:
                pairs.append((slab * pieces + piece, other * pieces + piece))
    return lax.ppermute(face, ("gx", "gy"), pairs)


def sources_first(pieces):
    return sorted((turn for turn in range(1, pieces) if turn & (turn - 1) == 0), reverse=True)


def local(rec_state, source_strain, material, material_table, residual, rec_cell, listed, src_pick):
    state = rec_state[0]
    receivers, _, tile_x, tile_y, depth = state.shape
    pieces, slabs, groups = lax.axis_size("gy"), lax.axis_size("gx"), lax.axis_size("sta")
    assert receivers == pieces and tile_x == 2 * DEEP
    assert pieces & (pieces - 1) == 0 and groups & (groups - 1) == 0
    size_y = pieces * tile_y
    group, me = lax.axis_index("sta"), lax.axis_index("gy")
    moments = residual.shape[2]

    numbers = material.astype(F32)[None]
    order = sorted(range(pieces), reverse=True)
    picked = {turn: lax.dynamic_index_in_dim(state, me ^ turn, 0, keepdims=False) for turn in order}
    own, picked = lax.optimization_barrier((source_strain[0], picked))
    chunks = {turn: jnp.concatenate([picked[turn], numbers], 0) for turn in order}
    chunks = [swap(chunks[turn], "gy", turn) if turn else chunks[turn] for turn in range(pieces)]
    strains = [swap(own, "sta", turn) if turn else own for turn in range(groups)]

    def shape(*lead, kind=F32):
        return lead + (size_y, depth), kind

    vel_shape, pair_shape = shape(3, DEEP), shape(6, REACH)
    halo_shape, sent_shape = shape(3, REACH), shape(3 * PACKED, kind=BF16)

    results = call(
        assemble,
        [vel_shape, pair_shape, pair_shape, shape(DEEP), shape(4, REACH)] * 2,
        ([], chunks),
        [pltpu.VMEM((8, size_y, depth), F32)],
    )
    vels, middles, edges, cells, faces = ([results[at], results[5 + at]] for at in range(5))
    halos = [to_neighbour(faces[side], side) for side in range(2)]

    strains, cells = lax.optimization_barrier((strains, cells))
    weights = lax.dynamic_slice_in_dim(listed, group, 1, 2)[:, :, 0].astype(F32)
    combined = 0.0
    for turn in range(groups):
        factor = jnp.sum(weights * (src_pick == (group ^ turn)).astype(F32), 0)
        combined = combined + factor[:, None, None, None, None] * strains[turn].astype(F32)

    sent, lights, lames, shears, old_halos, spots, amounts = ([None, None] for _ in range(7))
    fresh = [None, None]
    for side in range(2):
        results = call(
            functools.partial(first, side),
            [vel_shape, sent_shape, shape(DEEP), shape(DEEP + REACH), shape(DEEP + REACH), halo_shape]
            + [shape(DEEP), shape(moments)],
            (
                [material_table, residual, rec_cell],
                [vels[side], middles[side], middles[1 - side], edges[side], cells[side], halos[side]],
            ),
        )
        fresh[side], sent[side], lights[side], lames[side], shears[side], old_halos[side] = results[:6]
        spots[side], amounts[side] = results[6:]
        sent[side] = to_neighbour(sent[side], side)
    vels = fresh

    rates = []
    for moment in range(moments):
        last = moment == moments - 1
        results = call(
            functools.partial(inner, last),
            [pair_shape] * (2 if last else 4),
            ([], vels if last else vels + middles + lames + shears),
        )
        rates += results[:2]
        if not last:
            middles = results[2:]
        if moment == 5 * moments // 8:
            found, middles = lax.optimization_barrier((found, middles))
            for turn in range(pieces):
                if turn not in found:
                    low = turn & -turn
                    found[turn] = swap(found[turn ^ low], "gy", low)
        if last:
            (terms,) = call(
                functools.partial(correlate, list(range(moment)), pieces),
                [((pieces, 2, tile_x, tile_y, depth), F32)],
                ([residual], rates[: 4 * moment] + [found[turn] for turn in range(pieces)]),
            )
            terms, vels = lax.optimization_barrier((terms, vels))
        fresh = [None, None]
        for side in range(2):
            arrays = [vels[side], sent[side], edges[side]]
            outs = [pair_shape]
            if not last:
                arrays += [old_halos[side], middles[side], middles[1 - side]]
                arrays += [lights[side], lames[side], shears[side], spots[side], amounts[side]]
                outs += [pair_shape, halo_shape, vel_shape, sent_shape]
            results = call(functools.partial(outer, side, moment, last), outs, ([], arrays))
            rates.append(results[0])
            if not last:
                edges[side], old_halos[side], fresh[side] = results[1:4]
                sent[side] = to_neighbour(results[4], side)
        if moment == 0:
            combined, rates[-1] = lax.optimization_barrier((combined, rates[-1]))
            found = {turn: swap(combined, "gy", turn) for turn in sources_first(pieces)}
            found[0] = combined
        vels = fresh

    (terms,) = call(
        functools.partial(correlate, [moments - 1], pieces),
        [((pieces, 2, tile_x, tile_y, depth), F32)],
        ([residual], rates[-4:] + [found[turn] for turn in range(pieces)] + [terms]),
    )
    held = {turn: terms[turn] for turn in range(pieces)}
    if pieces > 1:
        keep = [turn for turn in held if not turn & 1]
        got = swap(jnp.stack([held[turn ^ 1] for turn in keep]), "gy", 1)
        held = {turn: held[turn] + got[at] for at, turn in enumerate(keep)}
    share = tile_x // groups
    result = 0.0
    for across_sta in reversed(range(groups)):
        for turn in reversed(list(held)):
            part = lax.dynamic_slice_in_dim(held[turn], (group ^ across_sta) * share, share, 1)
            if across_sta or turn:
                pairs = [
                    (a * pieces + b, (a ^ across_sta) * pieces + (b ^ turn))
                    for a in range(groups)
                    for b in range(pieces)
                ]
                part = lax.ppermute(part, ("sta", "gy"), pairs)
            result = result + part
    return result


def solution(mesh):
    in_specs = (
        P("sta", None, None, "gx", "gy", None),
        P("sta", None, None, "gx", "gy", None),
        P("gx", "gy", None),
        P(),
        P("sta", None, None),
        P("sta", None),
        P(),
        P(),
    )
    out_specs = P(None, ("gx", "sta"), "gy", None)
    return jax.shard_map(local, mesh=mesh, in_specs=in_specs, out_specs=out_specs, check_vma=False)
```

```python
import functools

import jax
import jax.numpy as jnp
from jax import lax
from jax.experimental import pallas as pl
from jax.experimental.pallas import tpu as pltpu
from jax.sharding import PartitionSpec as P

NEAR = 8.0
UNIT = 12.0
SUBLANES = 8
TIME_STEP = 0.25
AMPLITUDE = 4.0
KERNEL_SCALE = 0.0625
STIFFNESS = 0.3
REACH = 2
DEEP = 2 * REACH
ALONG_X = (0, 3, 4)
NEAR_ROWS = 2
PACKED = DEEP + NEAR_ROWS

VMEM = pl.BlockSpec(memory_space=pltpu.VMEM)
SMEM = pl.BlockSpec(memory_space=pltpu.SMEM)
F32, BF16 = jnp.float32, jnp.bfloat16


def call(body, outs, ins, scratch=(), flops=1_000_000):
    scalars, arrays = ins
    return list(pl.pallas_call(
        body,
        out_shape=[jax.ShapeDtypeStruct(shape, kind) for shape, kind in outs],
        in_specs=[SMEM] * len(scalars) + [VMEM] * len(arrays),
        out_specs=[VMEM] * len(outs),
        scratch_shapes=list(scratch),
        compiler_params=pltpu.CompilerParams(vmem_limit_bytes=6 * 1024 * 1024),
        cost_estimate=pl.CostEstimate(flops=flops, bytes_accessed=2_000_000, transcendentals=0),
    )(*scalars, *arrays))


def band(depth):
    row = lax.broadcasted_iota(jnp.int32, (depth, depth), 0)
    step = row - lax.broadcasted_iota(jnp.int32, (depth, depth), 1)
    parts = jnp.where(step == 1, NEAR, 0.0) - jnp.where(step == -1, NEAR, 0.0)
    parts = parts - jnp.where(step == 2, 1.0, 0.0) + jnp.where(step == -2, 1.0, 0.0)
    parts = parts.astype(BF16)
    return jnp.concatenate([parts, parts], 0)


def along_depth(rows):
    stacked = jnp.concatenate(rows, 0)
    high = stacked.astype(BF16)
    low = (stacked - high.astype(F32)).astype(BF16)
    split = jnp.concatenate([high, low], 1)
    result = jnp.dot(split, band(stacked.shape[1]), preferred_element_type=F32)
    size = rows[0].shape[0]
    return [result[at * size : (at + 1) * size] for at in range(len(rows))]


def along_y(row):
    count = row.shape[0] // SUBLANES
    at = lax.broadcasted_iota(jnp.int32, (SUBLANES, row.shape[1]), 0)
    planes = [row[SUBLANES * p : SUBLANES * (p + 1)] for p in range(count)]
    before = [jnp.where(at > 0, pltpu.roll(plane, 1, 0), 0.0) for plane in planes[-2:]]
    after = [jnp.where(at < SUBLANES - 1, pltpu.roll(plane, SUBLANES - 1, 0), 0.0) for plane in planes[:2]]
    spread = before + planes + after

    def shifted(by):
        return jnp.concatenate(spread[2 + by : 2 + by + count], 0)

    return shifted(1) - shifted(-1), shifted(2) - shifted(-2)


def across(rows, out, side):
    near, far = rows(out + 1) - rows(out - 1), rows(out + 2) - rows(out - 2)
    return (-near, -far) if side else (near, far)


def across_and_along(rows, out, side, row):
    near_y, far_y = along_y(row)
    near, far = rows(out + 1) - rows(out - 1), rows(out + 2) - rows(out - 2)
    if side:
        return NEAR * (near_y - near) - (far_y - far)
    return NEAR * (near_y + near) - (far_y + far)


def derivative(pair):
    return NEAR * pair[0] - pair[1]


MIRRORED_VEL = (0,)
MIRRORED_STRESS = (3, 4)


def position():
    slab, me = lax.axis_index("gx"), lax.axis_index("gy")
    return slab, me, (slab + me) % 2


def sign_of(flip):
    return 1.0 - 2.0 * flip.astype(F32)


def row_of(flip, side, out, tile_x):
    x = tile_x // 2 - 1 - out if side else tile_x // 2 + out
    return x + flip * (tile_x - 1 - 2 * x)


def interleave(me, tiles, comp, row, held):
    tile_y = tiles[0].shape[2]
    for turn, tile in enumerate(tiles):
        held[pl.ds(pl.multiple_of((me ^ turn) * tile_y, tile_y), tile_y), :] = tile[comp, row]
    count = held.shape[0] // SUBLANES
    return jnp.concatenate([held[pl.ds(p, SUBLANES, stride=count), :] for p in range(count)], 0)


def assemble(*refs):
    count = len(refs) - 11
    tiles, sides, held = refs[:count], (refs[count : count + 5], refs[count + 5 : -1]), refs[-1]
    tile_x = tiles[0].shape[1]
    _, me, flip = position()
    sign = sign_of(flip)
    face_comps = tuple(3 + comp for comp in ALONG_X) + (9,)
    for side, (vel, middle, edge, cells, face) in enumerate(sides):
        for out in range(DEEP):
            row = row_of(flip, side, out, tile_x)
            part, at = (middle, out) if out < REACH else (edge, out - REACH)
            for comp in range(10):
                value = interleave(me, tiles, comp, row, held.at[(out * 10 + comp) % held.shape[0]])
                if comp in MIRRORED_VEL or comp - 3 in MIRRORED_STRESS:
                    value = sign * value
                if comp < 3:
                    vel[comp, out] = value
                elif comp < 9:
                    part[comp - 3, at] = value
                else:
                    cells[out] = value
                if out >= REACH and comp in face_comps:
                    face[face_comps.index(comp), out - REACH] = value


def push(side, spots, amount, stress_row, vel, light, vel_out, sent):
    rows = [functools.partial(stress_row, comp) for comp in range(6)]
    deep = along_depth([rows[comp](out) for out in range(DEEP) for comp in (4, 5, 2)])
    for out in range(DEEP):
        force_x = across_and_along(rows[0], out, side, rows[3](out)) + deep[3 * out]
        force_y = across_and_along(rows[3], out, side, rows[1](out)) + deep[3 * out + 1]
        force_z = across_and_along(rows[4], out, side, rows[5](out)) + deep[3 * out + 2]
        force_z = force_z + amount * spots[out]
        near = DEEP - 1 - out
        for comp, force in enumerate((force_x, force_y, force_z)):
            fresh = vel[comp, out] + light[out] * force
            vel_out[comp, out] = fresh
            if comp in MIRRORED_VEL:
                fresh = -fresh
            high = fresh.astype(BF16)
            if near < NEAR_ROWS:
                sent[comp * PACKED + 2 * near] = high
                sent[comp * PACKED + 2 * near + 1] = (fresh - high.astype(F32)).astype(BF16)
            else:
                sent[comp * PACKED + NEAR_ROWS + near] = high


def from_halo(halo, comp, near):
    if near < NEAR_ROWS:
        at = comp * PACKED + 2 * near
        return halo[at].astype(F32) + halo[at + 1].astype(F32)
    return halo[comp * PACKED + NEAR_ROWS + near].astype(F32)


def first(side, table, residual, rec_cell, vel, middle, other, edge, cells, halo, *outs):
    vel_out, sent, light, lame, shear, halo_out, spots, amounts = outs
    size_y, depth = vel.shape[2:]
    planes = size_y // SUBLANES
    slab, me, flip = position()
    cell = rec_cell[0, me]
    spot_x, spot_y = cell // size_y - slab * (2 * DEEP), cell % size_y
    spot_x = spot_x + flip * (2 * DEEP - 1 - 2 * spot_x)
    spot_y = (spot_y % planes) * SUBLANES + spot_y // planes
    at_spot = (lax.broadcasted_iota(jnp.int32, (size_y, depth), 0) == spot_y) & (
        lax.broadcasted_iota(jnp.int32, (size_y, depth), 1) == 0
    )
    for out in range(DEEP):
        here = spot_x == (DEEP - 1 - out if side else DEEP + out)
        spots[out] = jnp.where(at_spot, jnp.where(here, UNIT * AMPLITUDE, 0.0), 0.0)
    for moment in range(residual.shape[2]):
        amounts[moment] = jnp.full((size_y, depth), residual[0, me, moment], F32)
    _, inside = partner(slab, me, lax.axis_size("gx"), side)
    count = table.shape[0]
    for out in range(DEEP + REACH):
        if out < DEEP:
            number, share = cells[out], 1.0
        else:
            number = halo[len(ALONG_X), REACH - 1 - (out - DEEP)]
            share = jnp.where(inside, 1.0, 0.0)
        parts = [jnp.full(number.shape, table[0, c], F32) for c in range(3)]
        for m in range(1, count):
            hit = number == float(m)
            parts = [jnp.where(hit, table[m, c], parts[c]) for c in range(3)]
        lame[out] = (TIME_STEP * STIFFNESS / UNIT * share) * parts[1]
        shear[out] = (TIME_STEP * STIFFNESS / UNIT * share) * parts[2]
        if out < DEEP:
            light[out] = (TIME_STEP / UNIT) / parts[0]
    for at in range(len(ALONG_X)):
        for near in range(REACH):
            value = halo[at, REACH - 1 - near]
            halo_out[at, near] = -value if ALONG_X[at] in MIRRORED_STRESS else value
    push(side, spots, amounts[0], stress_rows(middle, other, edge, halo_out), vel, light, vel_out, sent)


def stress_rows(middle, other, edge, halo):
    def row(comp, out):
        if out < 0:
            return other[comp, -1 - out]
        if out < REACH:
            return middle[comp, out]
        if out < DEEP:
            return edge[comp, out - REACH]
        return halo[ALONG_X.index(comp), out - DEEP]

    return row


def strain_rates(vx, vy, vz, side, first_out, last_out, full_out):
    outs = range(first_out, last_out)
    wanted = [(vel, out) for out in outs for vel in (vx, vz)] + [(vy, out) for out in outs if out < full_out]
    deep = along_depth([vel(out) for vel, out in wanted])
    deep = {key: value for key, value in zip(wanted, deep)}
    for out in outs:
        rates = [
            derivative(across(vx, out, side)),
            derivative(along_y(vy(out))),
            deep[vz, out],
            across_and_along(vy, out, side, vx(out)),
            deep[vx, out] + derivative(across(vz, out, side)),
        ]
        if out < full_out:
            rates.append(deep[vy, out] + derivative(along_y(vz(out))))
        yield out, rates


def store(target, at, rates):
    count = rates[0].shape[0] // SUBLANES
    for comp, rate in enumerate(rates):
        for p in range(count):
            spot = pl.ds(p, SUBLANES, stride=count)
            target[comp, at, spot, :] = rate[SUBLANES * p : SUBLANES * (p + 1)]


def renew(rates, lame, shear, before):
    bulk = lame * (rates[0] + rates[1] + rates[2])
    twice = shear + shear
    return {
        comp: old + (bulk + twice * rates[comp] if comp < 3 else shear * rates[comp])
        for comp, old in before.items()
    }


def outer(side, moment, last, vel, halo, edge, *refs):
    if last:
        (rates_out,) = refs
    else:
        old_halo, middle, other, light, lame, shear, spots, amounts, rates_out, edge_out, halo_out, vel_out, sent = refs

    def rows(comp):
        return lambda out: vel[comp, out] if out < DEEP else from_halo(halo, comp, out - DEEP)

    until = DEEP if last else DEEP + REACH
    for out, rates in strain_rates(rows(0), rows(1), rows(2), side, REACH, until, DEEP):
        own = out < DEEP
        if own:
            store(rates_out, out - REACH, rates)
        if last:
            continue
        if own:
            fresh = renew(rates, lame[out], shear[out], {comp: edge[comp, out - REACH] for comp in range(6)})
            for comp, value in fresh.items():
                edge_out[comp, out - REACH] = value
        else:
            before = {comp: old_halo[at, out - DEEP] for at, comp in enumerate(ALONG_X)}
            fresh = renew(rates, lame[out], shear[out], before)
            for at, comp in enumerate(ALONG_X):
                halo_out[at, out - DEEP] = fresh[comp]
    if not last:
        rows = stress_rows(middle, other, edge_out, halo_out)
        push(side, spots, amounts[moment + 1], rows, vel, light, vel_out, sent)


def inner(last, *refs):
    vels = refs[:2]
    if last:
        rates_out = refs[2:]
    else:
        middles, lames, shears = refs[2:4], refs[4:6], refs[6:8]
        rates_out, middles_out = refs[8:10], refs[10:12]
    for side in range(2):

        def rows(comp):
            return lambda out: vels[side][comp, out] if out >= 0 else vels[1 - side][comp, -1 - out]

        for out, rates in strain_rates(rows(0), rows(1), rows(2), side, 0, REACH, REACH):
            store(rates_out[side], out, rates)
            if not last:
                before = {comp: middles[side][comp, out] for comp in range(6)}
                fresh = renew(rates, lames[side][out], shears[side][out], before)
                for comp, value in fresh.items():
                    middles_out[side][comp, out] = value


def correlate(moments, pieces, residual, *refs):
    count = len(moments)
    rates, sources, before, terms = refs[: 4 * count], refs[4 * count], refs[4 * count + 1 : -1], refs[-1]
    tile_x, tile_y = sources.shape[3:5]
    _, me, flip = position()
    sign = sign_of(flip)
    for turn in range(pieces):
        spot = pl.ds(pl.multiple_of((me ^ turn) * tile_y, tile_y), tile_y)
        for side in range(2):
            for out in range(DEEP):
                row = row_of(flip, side, out, tile_x)
                lam, mu = (before[0][turn, 0, row], before[0][turn, 1, row]) if before else (0.0, 0.0)
                for at, moment in enumerate(moments):
                    weight = (KERNEL_SCALE / UNIT) * residual[0, me, moment]
                    held = rates[4 * at + 2 * (out // REACH) + side]
                    rate = [held[c, out % REACH, spot, :] for c in range(6)]
                    source = [sources[me ^ turn, moment, c, row] for c in range(6)]
                    bulk = (source[0] + source[1] + source[2]) * (rate[0] + rate[1] + rate[2])
                    diag = source[0] * rate[0] + source[1] * rate[1] + source[2] * rate[2]
                    off = sign * (source[3] * rate[3] + source[4] * rate[4]) + source[5] * rate[5]
                    lam = lam + weight * bulk
                    mu = mu + (2.0 * weight) * (diag + off)
                terms[turn, 0, row] = lam
                terms[turn, 1, row] = mu


def swap(array, axis, turn):
    count = lax.axis_size(axis)
    return lax.ppermute(array, axis, [(i, i ^ turn) for i in range(count)])


def partner(slab, piece, slabs, side):
    other = slab + 1 - 2 * ((slab + piece + side) % 2)
    return other, (other >= 0) & (other < slabs)


def to_neighbour(face, side):
    slabs, pieces = lax.axis_size("gx"), lax.axis_size("gy")
    pairs = []
    for slab in range(slabs):
        for piece in range(pieces):
            other, inside = partner(slab, piece, slabs, side)
            if inside:
                pairs.append((slab * pieces + piece, other * pieces + piece))
    return lax.ppermute(face, ("gx", "gy"), pairs)


def local(rec_state, source_strain, material, material_table, residual, rec_cell, listed, src_pick):
    state = rec_state[0]
    receivers, _, tile_x, tile_y, depth = state.shape
    pieces, slabs, groups = lax.axis_size("gy"), lax.axis_size("gx"), lax.axis_size("sta")
    assert receivers == pieces and tile_x == 2 * DEEP
    assert pieces & (pieces - 1) == 0 and groups & (groups - 1) == 0
    size_y = pieces * tile_y
    group, me = lax.axis_index("sta"), lax.axis_index("gy")
    moments = residual.shape[2]

    numbers = material.astype(F32)[None]
    order = sorted(range(pieces), reverse=True)
    picked = {turn: lax.dynamic_index_in_dim(state, me ^ turn, 0, keepdims=False) for turn in order}
    own, picked = lax.optimization_barrier((source_strain[0], picked))
    chunks = {turn: jnp.concatenate([picked[turn], numbers], 0) for turn in order}
    chunks = [swap(chunks[turn], "gy", turn) if turn else chunks[turn] for turn in range(pieces)]
    strains = [swap(own, "sta", turn) if turn else own for turn in range(groups)]

    def shape(*lead, kind=F32):
        return lead + (size_y, depth), kind

    vel_shape, pair_shape = shape(3, DEEP), shape(6, REACH)
    halo_shape, sent_shape = shape(3, REACH), shape(3 * PACKED, kind=BF16)

    results = call(
        assemble,
        [vel_shape, pair_shape, pair_shape, shape(DEEP), shape(4, REACH)] * 2,
        ([], chunks),
        [pltpu.VMEM((8, size_y, depth), F32)],
    )
    vels, middles, edges, cells, faces = ([results[at], results[5 + at]] for at in range(5))
    halos = [to_neighbour(faces[side], side) for side in range(2)]

    strains, cells = lax.optimization_barrier((strains, cells))
    weights = lax.dynamic_slice_in_dim(listed, group, 1, 2)[:, :, 0].astype(F32)
    combined = 0.0
    for turn in range(groups):
        factor = jnp.sum(weights * (src_pick == (group ^ turn)).astype(F32), 0)
        combined = combined + factor[:, None, None, None, None] * strains[turn].astype(F32)
    gathered = lax.all_gather(combined, "gy", axis=0)

    sent, lights, lames, shears, old_halos, spots, amounts = ([None, None] for _ in range(7))
    fresh = [None, None]
    for side in range(2):
        results = call(
            functools.partial(first, side),
            [vel_shape, sent_shape, shape(DEEP), shape(DEEP + REACH), shape(DEEP + REACH), halo_shape]
            + [shape(DEEP), shape(moments)],
            (
                [material_table, residual, rec_cell],
                [vels[side], middles[side], middles[1 - side], edges[side], cells[side], halos[side]],
            ),
        )
        fresh[side], sent[side], lights[side], lames[side], shears[side], old_halos[side] = results[:6]
        spots[side], amounts[side] = results[6:]
        sent[side] = to_neighbour(sent[side], side)
    vels = fresh

    rates = []
    for moment in range(moments):
        last = moment == moments - 1
        results = call(
            functools.partial(inner, last),
            [pair_shape] * (2 if last else 4),
            ([], vels if last else vels + middles + lames + shears),
        )
        rates += results[:2]
        if not last:
            middles = results[2:]
        if last:
            (terms,) = call(
                functools.partial(correlate, list(range(moment)), pieces),
                [((pieces, 2, tile_x, tile_y, depth), F32)],
                ([residual], rates[: 4 * moment] + [gathered]),
            )
            terms, vels = lax.optimization_barrier((terms, vels))
        fresh = [None, None]
        for side in range(2):
            arrays = [vels[side], sent[side], edges[side]]
            outs = [pair_shape]
            if not last:
                arrays += [old_halos[side], middles[side], middles[1 - side]]
                arrays += [lights[side], lames[side], shears[side], spots[side], amounts[side]]
                outs += [pair_shape, halo_shape, vel_shape, sent_shape]
            results = call(functools.partial(outer, side, moment, last), outs, ([], arrays))
            rates.append(results[0])
            if not last:
                edges[side], old_halos[side], fresh[side] = results[1:4]
                sent[side] = to_neighbour(results[4], side)
        vels = fresh

    (terms,) = call(
        functools.partial(correlate, [moments - 1], pieces),
        [((pieces, 2, tile_x, tile_y, depth), F32)],
        ([residual], rates[-4:] + [gathered, terms]),
    )
    held = {turn: terms[turn] for turn in range(pieces)}
    if pieces > 1:
        keep = [turn for turn in held if not turn & 1]
        got = swap(jnp.stack([held[turn ^ 1] for turn in keep]), "gy", 1)
        held = {turn: held[turn] + got[at] for at, turn in enumerate(keep)}
    share = tile_x // groups
    result = 0.0
    for across_sta in reversed(range(groups)):
        for turn in reversed(list(held)):
            part = lax.dynamic_slice_in_dim(held[turn], (group ^ across_sta) * share, share, 1)
            if across_sta or turn:
                pairs = [
                    (a * pieces + b, (a ^ across_sta) * pieces + (b ^ turn))
                    for a in range(groups)
                    for b in range(pieces)
                ]
                part = lax.ppermute(part, ("sta", "gy"), pairs)
            result = result + part
    return result


def solution(mesh):
    in_specs = (
        P("sta", None, None, "gx", "gy", None),
        P("sta", None, None, "gx", "gy", None),
        P("gx", "gy", None),
        P(),
        P("sta", None, None),
        P("sta", None),
        P(),
        P(),
    )
    out_specs = P(None, ("gx", "sta"), "gy", None)
    return jax.shard_map(local, mesh=mesh, in_specs=in_specs, out_specs=out_specs, check_vma=False)
```

```python
import functools

import jax
import jax.numpy as jnp
from jax import lax
from jax.experimental import pallas as pl
from jax.experimental.pallas import tpu as pltpu
from jax.sharding import PartitionSpec as P

NEAR = 8.0
UNIT = 12.0
SUBLANES = 8
TIME_STEP = 0.25
AMPLITUDE = 4.0
KERNEL_SCALE = 0.0625
STIFFNESS = 0.3
REACH = 2
DEEP = 2 * REACH
ALONG_X = (0, 3, 4)
NEAR_ROWS = 1
PACKED = DEEP + NEAR_ROWS

VMEM = pl.BlockSpec(memory_space=pltpu.VMEM)
SMEM = pl.BlockSpec(memory_space=pltpu.SMEM)
F32, BF16 = jnp.float32, jnp.bfloat16


def call(body, outs, ins, scratch=(), flops=1_000_000):
    scalars, arrays = ins
    return list(pl.pallas_call(
        body,
        out_shape=[jax.ShapeDtypeStruct(shape, kind) for shape, kind in outs],
        in_specs=[SMEM] * len(scalars) + [VMEM] * len(arrays),
        out_specs=[VMEM] * len(outs),
        scratch_shapes=list(scratch),
        compiler_params=pltpu.CompilerParams(vmem_limit_bytes=6 * 1024 * 1024),
        cost_estimate=pl.CostEstimate(flops=flops, bytes_accessed=2_000_000, transcendentals=0),
    )(*scalars, *arrays))


def band(depth):
    row = lax.broadcasted_iota(jnp.int32, (depth, depth), 0)
    step = row - lax.broadcasted_iota(jnp.int32, (depth, depth), 1)
    parts = jnp.where(step == 1, NEAR, 0.0) - jnp.where(step == -1, NEAR, 0.0)
    parts = parts - jnp.where(step == 2, 1.0, 0.0) + jnp.where(step == -2, 1.0, 0.0)
    parts = parts.astype(BF16)
    return jnp.concatenate([parts, parts], 0)


def along_depth(rows):
    stacked = jnp.concatenate(rows, 0)
    high = stacked.astype(BF16)
    low = (stacked - high.astype(F32)).astype(BF16)
    split = jnp.concatenate([high, low], 1)
    result = jnp.dot(split, band(stacked.shape[1]), preferred_element_type=F32)
    size = rows[0].shape[0]
    return [result[at * size : (at + 1) * size] for at in range(len(rows))]


def along_y(row):
    count = row.shape[0] // SUBLANES
    at = lax.broadcasted_iota(jnp.int32, (SUBLANES, row.shape[1]), 0)
    planes = [row[SUBLANES * p : SUBLANES * (p + 1)] for p in range(count)]
    before = [jnp.where(at > 0, pltpu.roll(plane, 1, 0), 0.0) for plane in planes[-2:]]
    after = [jnp.where(at < SUBLANES - 1, pltpu.roll(plane, SUBLANES - 1, 0), 0.0) for plane in planes[:2]]
    spread = before + planes + after

    def shifted(by):
        return jnp.concatenate(spread[2 + by : 2 + by + count], 0)

    return shifted(1) - shifted(-1), shifted(2) - shifted(-2)


def across(rows, out, side):
    near, far = rows(out + 1) - rows(out - 1), rows(out + 2) - rows(out - 2)
    return (-near, -far) if side else (near, far)


def across_and_along(rows, out, side, row):
    near_y, far_y = along_y(row)
    near, far = rows(out + 1) - rows(out - 1), rows(out + 2) - rows(out - 2)
    if side:
        return NEAR * (near_y - near) - (far_y - far)
    return NEAR * (near_y + near) - (far_y + far)


def derivative(pair):
    return NEAR * pair[0] - pair[1]


MIRRORED_VEL = (0,)
MIRRORED_STRESS = (3, 4)


def position():
    slab, me = lax.axis_index("gx"), lax.axis_index("gy")
    return slab, me, (slab + me) % 2


def sign_of(flip):
    return 1.0 - 2.0 * flip.astype(F32)


def row_of(flip, side, out, tile_x):
    x = tile_x // 2 - 1 - out if side else tile_x // 2 + out
    return x + flip * (tile_x - 1 - 2 * x)


def interleave(me, tiles, comp, row, held):
    tile_y = tiles[0].shape[2]
    for turn, tile in enumerate(tiles):
        held[pl.ds(pl.multiple_of((me ^ turn) * tile_y, tile_y), tile_y), :] = tile[comp, row]
    count = held.shape[0] // SUBLANES
    return jnp.concatenate([held[pl.ds(p, SUBLANES, stride=count), :] for p in range(count)], 0)


def assemble(*refs):
    count = len(refs) - 11
    tiles, sides, held = refs[:count], (refs[count : count + 5], refs[count + 5 : -1]), refs[-1]
    tile_x = tiles[0].shape[1]
    _, me, flip = position()
    sign = sign_of(flip)
    face_comps = tuple(3 + comp for comp in ALONG_X) + (9,)
    for side, (vel, middle, edge, cells, face) in enumerate(sides):
        for out in range(DEEP):
            row = row_of(flip, side, out, tile_x)
            part, at = (middle, out) if out < REACH else (edge, out - REACH)
            for comp in range(10):
                value = interleave(me, tiles, comp, row, held.at[(out * 10 + comp) % held.shape[0]])
                if comp in MIRRORED_VEL or comp - 3 in MIRRORED_STRESS:
                    value = sign * value
                if comp < 3:
                    vel[comp, out] = value
                elif comp < 9:
                    part[comp - 3, at] = value
                else:
                    cells[out] = value
                if out >= REACH and comp in face_comps:
                    face[face_comps.index(comp), out - REACH] = value


def push(side, spots, amount, stress_row, vel, light, vel_out, sent):
    rows = [functools.partial(stress_row, comp) for comp in range(6)]
    deep = along_depth([rows[comp](out) for out in range(DEEP) for comp in (4, 5, 2)])
    for out in range(DEEP):
        force_x = across_and_along(rows[0], out, side, rows[3](out)) + deep[3 * out]
        force_y = across_and_along(rows[3], out, side, rows[1](out)) + deep[3 * out + 1]
        force_z = across_and_along(rows[4], out, side, rows[5](out)) + deep[3 * out + 2]
        force_z = force_z + amount * spots[out]
        near = DEEP - 1 - out
        for comp, force in enumerate((force_x, force_y, force_z)):
            fresh = vel[comp, out] + light[out] * force
            vel_out[comp, out] = fresh
            if comp in MIRRORED_VEL:
                fresh = -fresh
            high = fresh.astype(BF16)
            if near < NEAR_ROWS:
                sent[comp * PACKED + 2 * near] = high
                sent[comp * PACKED + 2 * near + 1] = (fresh - high.astype(F32)).astype(BF16)
            else:
                sent[comp * PACKED + NEAR_ROWS + near] = high


def from_halo(halo, comp, near):
    if near < NEAR_ROWS:
        at = comp * PACKED + 2 * near
        return halo[at].astype(F32) + halo[at + 1].astype(F32)
    return halo[comp * PACKED + NEAR_ROWS + near].astype(F32)


def first(side, table, residual, rec_cell, vel, middle, other, edge, cells, halo, *outs):
    vel_out, sent, light, lame, shear, halo_out, spots, amounts = outs
    size_y, depth = vel.shape[2:]
    planes = size_y // SUBLANES
    slab, me, flip = position()
    cell = rec_cell[0, me]
    spot_x, spot_y = cell // size_y - slab * (2 * DEEP), cell % size_y
    spot_x = spot_x + flip * (2 * DEEP - 1 - 2 * spot_x)
    spot_y = (spot_y % planes) * SUBLANES + spot_y // planes
    at_spot = (lax.broadcasted_iota(jnp.int32, (size_y, depth), 0) == spot_y) & (
        lax.broadcasted_iota(jnp.int32, (size_y, depth), 1) == 0
    )
    for out in range(DEEP):
        here = spot_x == (DEEP - 1 - out if side else DEEP + out)
        spots[out] = jnp.where(at_spot, jnp.where(here, UNIT * AMPLITUDE, 0.0), 0.0)
    for moment in range(residual.shape[2]):
        amounts[moment] = jnp.full((size_y, depth), residual[0, me, moment], F32)
    _, inside = partner(slab, me, lax.axis_size("gx"), side)
    count = table.shape[0]
    for out in range(DEEP + REACH):
        if out < DEEP:
            number, share = cells[out], 1.0
        else:
            number = halo[len(ALONG_X), REACH - 1 - (out - DEEP)]
            share = jnp.where(inside, 1.0, 0.0)
        parts = [jnp.full(number.shape, table[0, c], F32) for c in range(3)]
        for m in range(1, count):
            hit = number == float(m)
            parts = [jnp.where(hit, table[m, c], parts[c]) for c in range(3)]
        lame[out] = (TIME_STEP * STIFFNESS / UNIT * share) * parts[1]
        shear[out] = (TIME_STEP * STIFFNESS / UNIT * share) * parts[2]
        if out < DEEP:
            light[out] = (TIME_STEP / UNIT) / parts[0]
    for at in range(len(ALONG_X)):
        for near in range(REACH):
            value = halo[at, REACH - 1 - near]
            halo_out[at, near] = -value if ALONG_X[at] in MIRRORED_STRESS else value
    push(side, spots, amounts[0], stress_rows(middle, other, edge, halo_out), vel, light, vel_out, sent)


def stress_rows(middle, other, edge, halo):
    def row(comp, out):
        if out < 0:
            return other[comp, -1 - out]
        if out < REACH:
            return middle[comp, out]
        if out < DEEP:
            return edge[comp, out - REACH]
        return halo[ALONG_X.index(comp), out - DEEP]

    return row


def strain_rates(vx, vy, vz, side, first_out, last_out, full_out):
    outs = range(first_out, last_out)
    wanted = [(vel, out) for out in outs for vel in (vx, vz)] + [(vy, out) for out in outs if out < full_out]
    deep = along_depth([vel(out) for vel, out in wanted])
    deep = {key: value for key, value in zip(wanted, deep)}
    for out in outs:
        rates = [
            derivative(across(vx, out, side)),
            derivative(along_y(vy(out))),
            deep[vz, out],
            across_and_along(vy, out, side, vx(out)),
            deep[vx, out] + derivative(across(vz, out, side)),
        ]
        if out < full_out:
            rates.append(deep[vy, out] + derivative(along_y(vz(out))))
        yield out, rates


def store(target, at, rates):
    count = rates[0].shape[0] // SUBLANES
    for comp, rate in enumerate(rates):
        for p in range(count):
            spot = pl.ds(p, SUBLANES, stride=count)
            target[comp, at, spot, :] = rate[SUBLANES * p : SUBLANES * (p + 1)]


def renew(rates, lame, shear, before):
    bulk = lame * (rates[0] + rates[1] + rates[2])
    twice = shear + shear
    return {
        comp: old + (bulk + twice * rates[comp] if comp < 3 else shear * rates[comp])
        for comp, old in before.items()
    }


def outer(side, moment, last, vel, halo, edge, *refs):
    if last:
        (rates_out,) = refs
    else:
        old_halo, middle, other, light, lame, shear, spots, amounts, rates_out, edge_out, halo_out, vel_out, sent = refs

    def rows(comp):
        return lambda out: vel[comp, out] if out < DEEP else from_halo(halo, comp, out - DEEP)

    until = DEEP if last else DEEP + REACH
    for out, rates in strain_rates(rows(0), rows(1), rows(2), side, REACH, until, DEEP):
        own = out < DEEP
        if own:
            store(rates_out, out - REACH, rates)
        if last:
            continue
        if own:
            fresh = renew(rates, lame[out], shear[out], {comp: edge[comp, out - REACH] for comp in range(6)})
            for comp, value in fresh.items():
                edge_out[comp, out - REACH] = value
        else:
            before = {comp: old_halo[at, out - DEEP] for at, comp in enumerate(ALONG_X)}
            fresh = renew(rates, lame[out], shear[out], before)
            for at, comp in enumerate(ALONG_X):
                halo_out[at, out - DEEP] = fresh[comp]
    if not last:
        rows = stress_rows(middle, other, edge_out, halo_out)
        push(side, spots, amounts[moment + 1], rows, vel, light, vel_out, sent)


def inner(last, *refs):
    vels = refs[:2]
    if last:
        rates_out = refs[2:]
    else:
        middles, lames, shears = refs[2:4], refs[4:6], refs[6:8]
        rates_out, middles_out = refs[8:10], refs[10:12]
    for side in range(2):

        def rows(comp):
            return lambda out: vels[side][comp, out] if out >= 0 else vels[1 - side][comp, -1 - out]

        for out, rates in strain_rates(rows(0), rows(1), rows(2), side, 0, REACH, REACH):
            store(rates_out[side], out, rates)
            if not last:
                before = {comp: middles[side][comp, out] for comp in range(6)}
                fresh = renew(rates, lames[side][out], shears[side][out], before)
                for comp, value in fresh.items():
                    middles_out[side][comp, out] = value


def correlate(moments, pieces, residual, *refs):
    count = len(moments)
    rates, sources, rest = refs[: 4 * count], refs[4 * count : 4 * count + pieces], refs[4 * count + pieces :]
    before, terms = rest[:-1], rest[-1]
    tile_x, tile_y = sources[0].shape[2:4]
    _, me, flip = position()
    sign = sign_of(flip)
    for turn in range(pieces):
        spot = pl.ds(pl.multiple_of((me ^ turn) * tile_y, tile_y), tile_y)
        for side in range(2):
            for out in range(DEEP):
                row = row_of(flip, side, out, tile_x)
                lam, mu = (before[0][turn, 0, row], before[0][turn, 1, row]) if before else (0.0, 0.0)
                for at, moment in enumerate(moments):
                    weight = (KERNEL_SCALE / UNIT) * residual[0, me, moment]
                    held = rates[4 * at + 2 * (out // REACH) + side]
                    rate = [held[c, out % REACH, spot, :] for c in range(6)]
                    source = [sources[turn][moment, c, row] for c in range(6)]
                    bulk = (source[0] + source[1] + source[2]) * (rate[0] + rate[1] + rate[2])
                    diag = source[0] * rate[0] + source[1] * rate[1] + source[2] * rate[2]
                    off = sign * (source[3] * rate[3] + source[4] * rate[4]) + source[5] * rate[5]
                    lam = lam + weight * bulk
                    mu = mu + (2.0 * weight) * (diag + off)
                terms[turn, 0, row] = lam
                terms[turn, 1, row] = mu


def swap(array, axis, turn):
    count = lax.axis_size(axis)
    return lax.ppermute(array, axis, [(i, i ^ turn) for i in range(count)])


def partner(slab, piece, slabs, side):
    other = slab + 1 - 2 * ((slab + piece + side) % 2)
    return other, (other >= 0) & (other < slabs)


def to_neighbour(face, side):
    slabs, pieces = lax.axis_size("gx"), lax.axis_size("gy")
    pairs = []
    for slab in range(slabs):
        for piece in range(pieces):
            other, inside = partner(slab, piece, slabs, side)
            if inside:
                pairs.append((slab * pieces + piece, other * pieces + piece))
    return lax.ppermute(face, ("gx", "gy"), pairs)


def exchange_plan(pieces, moments):
    result, known, width = {}, [0], pieces // 2
    while width:
        for turn in known:
            moment = 0 if len(known) == 1 else 3 * moments // 4
            result.setdefault(moment, []).append((turn ^ width, width))
        known = known + [turn ^ width for turn in known]
        width //= 2
    return result


def local(rec_state, source_strain, material, material_table, residual, rec_cell, listed, src_pick):
    state = rec_state[0]
    receivers, _, tile_x, tile_y, depth = state.shape
    pieces, slabs, groups = lax.axis_size("gy"), lax.axis_size("gx"), lax.axis_size("sta")
    assert receivers == pieces and tile_x == 2 * DEEP
    assert pieces & (pieces - 1) == 0 and groups & (groups - 1) == 0
    size_y = pieces * tile_y
    group, me = lax.axis_index("sta"), lax.axis_index("gy")
    moments = residual.shape[2]

    numbers = material.astype(F32)[None]
    order = sorted(range(pieces), reverse=True)
    picked = {turn: lax.dynamic_index_in_dim(state, me ^ turn, 0, keepdims=False) for turn in order}
    own, picked = lax.optimization_barrier((source_strain[0], picked))
    chunks = {turn: jnp.concatenate([picked[turn], numbers], 0) for turn in order}
    chunks = [swap(chunks[turn], "gy", turn) if turn else chunks[turn] for turn in range(pieces)]
    strains = [swap(own, "sta", turn) if turn else own for turn in range(groups)]

    def shape(*lead, kind=F32):
        return lead + (size_y, depth), kind

    vel_shape, pair_shape = shape(3, DEEP), shape(6, REACH)
    halo_shape, sent_shape = shape(3, REACH), shape(3 * PACKED, kind=BF16)

    results = call(
        assemble,
        [vel_shape, pair_shape, pair_shape, shape(DEEP), shape(4, REACH)] * 2,
        ([], chunks),
        [pltpu.VMEM((8, size_y, depth), F32)],
    )
    vels, middles, edges, cells, faces = ([results[at], results[5 + at]] for at in range(5))
    halos = [to_neighbour(faces[side], side) for side in range(2)]

    strains, cells = lax.optimization_barrier((strains, cells))
    weights = lax.dynamic_slice_in_dim(listed, group, 1, 2)[:, :, 0].astype(F32)
    combined = 0.0
    for turn in range(groups):
        factor = jnp.sum(weights * (src_pick == (group ^ turn)).astype(F32), 0)
        combined = combined + factor[:, None, None, None, None] * strains[turn].astype(F32)

    sent, lights, lames, shears, old_halos, spots, amounts = ([None, None] for _ in range(7))
    fresh = [None, None]
    for side in range(2):
        results = call(
            functools.partial(first, side),
            [vel_shape, sent_shape, shape(DEEP), shape(DEEP + REACH), shape(DEEP + REACH), halo_shape]
            + [shape(DEEP), shape(moments)],
            (
                [material_table, residual, rec_cell],
                [vels[side], middles[side], middles[1 - side], edges[side], cells[side], halos[side]],
            ),
        )
        fresh[side], sent[side], lights[side], lames[side], shears[side], old_halos[side] = results[:6]
        spots[side], amounts[side] = results[6:]
        sent[side] = to_neighbour(sent[side], side)
    vels = fresh

    found, exchanges = {0: combined}, exchange_plan(pieces, moments)
    rates = []
    for moment in range(moments):
        last = moment == moments - 1
        results = call(
            functools.partial(inner, last),
            [pair_shape] * (2 if last else 4),
            ([], vels if last else vels + middles + lames + shears),
        )
        rates += results[:2]
        if not last:
            middles = results[2:]
        if moment in exchanges:
            found, rates[-1] = lax.optimization_barrier((found, rates[-1]))
            for turn, width in exchanges[moment]:
                found[turn] = swap(found[turn ^ width], "gy", width)
        if last:
            (terms,) = call(
                functools.partial(correlate, list(range(moment)), pieces),
                [((pieces, 2, tile_x, tile_y, depth), F32)],
                ([residual], rates[: 4 * moment] + [found[turn] for turn in range(pieces)]),
            )
            terms, vels = lax.optimization_barrier((terms, vels))
        fresh = [None, None]
        for side in range(2):
            arrays = [vels[side], sent[side], edges[side]]
            outs = [pair_shape]
            if not last:
                arrays += [old_halos[side], middles[side], middles[1 - side]]
                arrays += [lights[side], lames[side], shears[side], spots[side], amounts[side]]
                outs += [pair_shape, halo_shape, vel_shape, sent_shape]
            results = call(functools.partial(outer, side, moment, last), outs, ([], arrays))
            rates.append(results[0])
            if not last:
                edges[side], old_halos[side], fresh[side] = results[1:4]
                sent[side] = to_neighbour(results[4], side)
        vels = fresh

    (terms,) = call(
        functools.partial(correlate, [moments - 1], pieces),
        [((pieces, 2, tile_x, tile_y, depth), F32)],
        ([residual], rates[-4:] + [found[turn] for turn in range(pieces)] + [terms]),
    )
    held = {turn: terms[turn] for turn in range(pieces)}
    if pieces > 1:
        keep = [turn for turn in held if not turn & 1]
        got = swap(jnp.stack([held[turn ^ 1] for turn in keep]), "gy", 1)
        held = {turn: held[turn] + got[at] for at, turn in enumerate(keep)}
    share = tile_x // groups
    result = 0.0
    for across_sta in reversed(range(groups)):
        for turn in reversed(list(held)):
            part = lax.dynamic_slice_in_dim(held[turn], (group ^ across_sta) * share, share, 1)
            if across_sta or turn:
                pairs = [
                    (a * pieces + b, (a ^ across_sta) * pieces + (b ^ turn))
                    for a in range(groups)
                    for b in range(pieces)
                ]
                part = lax.ppermute(part, ("sta", "gy"), pairs)
            result = result + part
    return result


def solution(mesh):
    in_specs = (
        P("sta", None, None, "gx", "gy", None),
        P("sta", None, None, "gx", "gy", None),
        P("gx", "gy", None),
        P(),
        P("sta", None, None),
        P("sta", None),
        P(),
        P(),
    )
    out_specs = P(None, ("gx", "sta"), "gy", None)
    return jax.shard_map(local, mesh=mesh, in_specs=in_specs, out_specs=out_specs, check_vma=False)
```

```python
import functools

import jax
import jax.numpy as jnp
from jax import lax
from jax.experimental import pallas as pl
from jax.experimental.pallas import tpu as pltpu
from jax.sharding import PartitionSpec as P

NEAR = 8.0
UNIT = 12.0
SUBLANES = 8
TIME_STEP = 0.25
AMPLITUDE = 4.0
KERNEL_SCALE = 0.0625
STIFFNESS = 0.3
REACH = 2
DEEP = 2 * REACH
ALONG_X = (0, 3, 4)
NEAR_ROWS = 1
PACKED = DEEP + NEAR_ROWS

VMEM = pl.BlockSpec(memory_space=pltpu.VMEM)
SMEM = pl.BlockSpec(memory_space=pltpu.SMEM)
F32, BF16 = jnp.float32, jnp.bfloat16


def call(body, outs, ins, scratch=(), flops=1_000_000):
    scalars, arrays = ins
    return list(pl.pallas_call(
        body,
        out_shape=[jax.ShapeDtypeStruct(shape, kind) for shape, kind in outs],
        in_specs=[SMEM] * len(scalars) + [VMEM] * len(arrays),
        out_specs=[VMEM] * len(outs),
        scratch_shapes=list(scratch),
        compiler_params=pltpu.CompilerParams(vmem_limit_bytes=6 * 1024 * 1024),
        cost_estimate=pl.CostEstimate(flops=flops, bytes_accessed=2_000_000, transcendentals=0),
    )(*scalars, *arrays))


def band(depth):
    row = lax.broadcasted_iota(jnp.int32, (depth, depth), 0)
    step = row - lax.broadcasted_iota(jnp.int32, (depth, depth), 1)
    parts = jnp.where(step == 1, NEAR, 0.0) - jnp.where(step == -1, NEAR, 0.0)
    parts = parts - jnp.where(step == 2, 1.0, 0.0) + jnp.where(step == -2, 1.0, 0.0)
    parts = parts.astype(BF16)
    return jnp.concatenate([parts, parts], 0)


def along_depth(rows):
    stacked = jnp.concatenate(rows, 0)
    high = stacked.astype(BF16)
    low = (stacked - high.astype(F32)).astype(BF16)
    split = jnp.concatenate([high, low], 1)
    result = jnp.dot(split, band(stacked.shape[1]), preferred_element_type=F32)
    size = rows[0].shape[0]
    return [result[at * size : (at + 1) * size] for at in range(len(rows))]


def along_y(row):
    count = row.shape[0] // SUBLANES
    at = lax.broadcasted_iota(jnp.int32, (SUBLANES, row.shape[1]), 0)
    planes = [row[SUBLANES * p : SUBLANES * (p + 1)] for p in range(count)]
    before = [jnp.where(at > 0, pltpu.roll(plane, 1, 0), 0.0) for plane in planes[-2:]]
    after = [jnp.where(at < SUBLANES - 1, pltpu.roll(plane, SUBLANES - 1, 0), 0.0) for plane in planes[:2]]
    spread = before + planes + after

    def shifted(by):
        return jnp.concatenate(spread[2 + by : 2 + by + count], 0)

    return shifted(1) - shifted(-1), shifted(2) - shifted(-2)


def across(rows, out, side):
    near, far = rows(out + 1) - rows(out - 1), rows(out + 2) - rows(out - 2)
    return (-near, -far) if side else (near, far)


def across_and_along(rows, out, side, row):
    near_y, far_y = along_y(row)
    near, far = rows(out + 1) - rows(out - 1), rows(out + 2) - rows(out - 2)
    if side:
        return NEAR * (near_y - near) - (far_y - far)
    return NEAR * (near_y + near) - (far_y + far)


def derivative(pair):
    return NEAR * pair[0] - pair[1]


MIRRORED_VEL = (0,)
MIRRORED_STRESS = (3, 4)


def position():
    slab, me = lax.axis_index("gx"), lax.axis_index("gy")
    return slab, me, (slab + me) % 2


def sign_of(flip):
    return 1.0 - 2.0 * flip.astype(F32)


def row_of(flip, side, out, tile_x):
    x = tile_x // 2 - 1 - out if side else tile_x // 2 + out
    return x + flip * (tile_x - 1 - 2 * x)


def interleave(me, tiles, comp, row, held):
    tile_y = tiles[0].shape[2]
    for turn, tile in enumerate(tiles):
        held[pl.ds(pl.multiple_of((me ^ turn) * tile_y, tile_y), tile_y), :] = tile[comp, row]
    count = held.shape[0] // SUBLANES
    return jnp.concatenate([held[pl.ds(p, SUBLANES, stride=count), :] for p in range(count)], 0)


def assemble(*refs):
    count = len(refs) - 11
    tiles, sides, held = refs[:count], (refs[count : count + 5], refs[count + 5 : -1]), refs[-1]
    tile_x = tiles[0].shape[1]
    _, me, flip = position()
    sign = sign_of(flip)
    face_comps = tuple(3 + comp for comp in ALONG_X) + (9,)
    for side, (vel, middle, edge, cells, face) in enumerate(sides):
        for out in range(DEEP):
            row = row_of(flip, side, out, tile_x)
            part, at = (middle, out) if out < REACH else (edge, out - REACH)
            for comp in range(10):
                value = interleave(me, tiles, comp, row, held.at[(out * 10 + comp) % held.shape[0]])
                if comp in MIRRORED_VEL or comp - 3 in MIRRORED_STRESS:
                    value = sign * value
                if comp < 3:
                    vel[comp, out] = value
                elif comp < 9:
                    part[comp - 3, at] = value
                else:
                    cells[out] = value
                if out >= REACH and comp in face_comps:
                    face[face_comps.index(comp), out - REACH] = value


def push(side, spots, amount, stress_row, vel, light, vel_out, sent):
    rows = [functools.partial(stress_row, comp) for comp in range(6)]
    deep = along_depth([rows[comp](out) for out in range(DEEP) for comp in (4, 5, 2)])
    for out in range(DEEP):
        force_x = across_and_along(rows[0], out, side, rows[3](out)) + deep[3 * out]
        force_y = across_and_along(rows[3], out, side, rows[1](out)) + deep[3 * out + 1]
        force_z = across_and_along(rows[4], out, side, rows[5](out)) + deep[3 * out + 2]
        force_z = force_z + amount * spots[out]
        near = DEEP - 1 - out
        for comp, force in enumerate((force_x, force_y, force_z)):
            fresh = vel[comp, out] + light[out] * force
            vel_out[comp, out] = fresh
            if comp in MIRRORED_VEL:
                fresh = -fresh
            high = fresh.astype(BF16)
            if near < NEAR_ROWS:
                sent[comp * PACKED + 2 * near] = high
                sent[comp * PACKED + 2 * near + 1] = (fresh - high.astype(F32)).astype(BF16)
            else:
                sent[comp * PACKED + NEAR_ROWS + near] = high


def from_halo(halo, comp, near):
    if near < NEAR_ROWS:
        at = comp * PACKED + 2 * near
        return halo[at].astype(F32) + halo[at + 1].astype(F32)
    return halo[comp * PACKED + NEAR_ROWS + near].astype(F32)


def first(side, table, residual, rec_cell, vel, middle, other, edge, cells, halo, *outs):
    vel_out, sent, light, lame, shear, halo_out, spots, amounts = outs
    size_y, depth = vel.shape[2:]
    planes = size_y // SUBLANES
    slab, me, flip = position()
    cell = rec_cell[0, me]
    spot_x, spot_y = cell // size_y - slab * (2 * DEEP), cell % size_y
    spot_x = spot_x + flip * (2 * DEEP - 1 - 2 * spot_x)
    spot_y = (spot_y % planes) * SUBLANES + spot_y // planes
    at_spot = (lax.broadcasted_iota(jnp.int32, (size_y, depth), 0) == spot_y) & (
        lax.broadcasted_iota(jnp.int32, (size_y, depth), 1) == 0
    )
    for out in range(DEEP):
        here = spot_x == (DEEP - 1 - out if side else DEEP + out)
        spots[out] = jnp.where(at_spot, jnp.where(here, UNIT * AMPLITUDE, 0.0), 0.0)
    for moment in range(residual.shape[2]):
        amounts[moment] = jnp.full((size_y, depth), residual[0, me, moment], F32)
    _, inside = partner(slab, me, lax.axis_size("gx"), side)
    count = table.shape[0]
    for out in range(DEEP + REACH):
        if out < DEEP:
            number, share = cells[out], 1.0
        else:
            number = halo[len(ALONG_X), REACH - 1 - (out - DEEP)]
            share = jnp.where(inside, 1.0, 0.0)
        parts = [jnp.full(number.shape, table[0, c], F32) for c in range(3)]
        for m in range(1, count):
            hit = number == float(m)
            parts = [jnp.where(hit, table[m, c], parts[c]) for c in range(3)]
        lame[out] = (TIME_STEP * STIFFNESS / UNIT * share) * parts[1]
        shear[out] = (TIME_STEP * STIFFNESS / UNIT * share) * parts[2]
        if out < DEEP:
            light[out] = (TIME_STEP / UNIT) / parts[0]
    for at in range(len(ALONG_X)):
        for near in range(REACH):
            value = halo[at, REACH - 1 - near]
            halo_out[at, near] = -value if ALONG_X[at] in MIRRORED_STRESS else value
    push(side, spots, amounts[0], stress_rows(middle, other, edge, halo_out), vel, light, vel_out, sent)


def stress_rows(middle, other, edge, halo):
    def row(comp, out):
        if out < 0:
            return other[comp, -1 - out]
        if out < REACH:
            return middle[comp, out]
        if out < DEEP:
            return edge[comp, out - REACH]
        return halo[ALONG_X.index(comp), out - DEEP]

    return row


def strain_rates(vx, vy, vz, side, first_out, last_out, full_out):
    outs = range(first_out, last_out)
    wanted = [(vel, out) for out in outs for vel in (vx, vz)] + [(vy, out) for out in outs if out < full_out]
    deep = along_depth([vel(out) for vel, out in wanted])
    deep = {key: value for key, value in zip(wanted, deep)}
    for out in outs:
        rates = [
            derivative(across(vx, out, side)),
            derivative(along_y(vy(out))),
            deep[vz, out],
            across_and_along(vy, out, side, vx(out)),
            deep[vx, out] + derivative(across(vz, out, side)),
        ]
        if out < full_out:
            rates.append(deep[vy, out] + derivative(along_y(vz(out))))
        yield out, rates


def store(target, at, rates):
    count = rates[0].shape[0] // SUBLANES
    for comp, rate in enumerate(rates):
        for p in range(count):
            spot = pl.ds(p, SUBLANES, stride=count)
            target[comp, at, spot, :] = rate[SUBLANES * p : SUBLANES * (p + 1)]


def renew(rates, lame, shear, before):
    bulk = lame * (rates[0] + rates[1] + rates[2])
    twice = shear + shear
    return {
        comp: old + (bulk + twice * rates[comp] if comp < 3 else shear * rates[comp])
        for comp, old in before.items()
    }


def outer(side, moment, last, vel, halo, edge, *refs):
    if last:
        (rates_out,) = refs
    else:
        old_halo, middle, other, light, lame, shear, spots, amounts, rates_out, edge_out, halo_out, vel_out, sent = refs

    def rows(comp):
        return lambda out: vel[comp, out] if out < DEEP else from_halo(halo, comp, out - DEEP)

    until = DEEP if last else DEEP + REACH
    for out, rates in strain_rates(rows(0), rows(1), rows(2), side, REACH, until, DEEP):
        own = out < DEEP
        if own:
            store(rates_out, out - REACH, rates)
        if last:
            continue
        if own:
            fresh = renew(rates, lame[out], shear[out], {comp: edge[comp, out - REACH] for comp in range(6)})
            for comp, value in fresh.items():
                edge_out[comp, out - REACH] = value
        else:
            before = {comp: old_halo[at, out - DEEP] for at, comp in enumerate(ALONG_X)}
            fresh = renew(rates, lame[out], shear[out], before)
            for at, comp in enumerate(ALONG_X):
                halo_out[at, out - DEEP] = fresh[comp]
    if not last:
        rows = stress_rows(middle, other, edge_out, halo_out)
        push(side, spots, amounts[moment + 1], rows, vel, light, vel_out, sent)


def inner(last, *refs):
    vels = refs[:2]
    if last:
        rates_out = refs[2:]
    else:
        middles, lames, shears = refs[2:4], refs[4:6], refs[6:8]
        rates_out, middles_out = refs[8:10], refs[10:12]
    for side in range(2):

        def rows(comp):
            return lambda out: vels[side][comp, out] if out >= 0 else vels[1 - side][comp, -1 - out]

        for out, rates in strain_rates(rows(0), rows(1), rows(2), side, 0, REACH, REACH):
            store(rates_out[side], out, rates)
            if not last:
                before = {comp: middles[side][comp, out] for comp in range(6)}
                fresh = renew(rates, lames[side][out], shears[side][out], before)
                for comp, value in fresh.items():
                    middles_out[side][comp, out] = value


def correlate(jobs, moments, residual, *refs):
    count = 4 * moments
    rates, sources, before, terms = refs[:count], refs[count : count + len(jobs)], refs[count + len(jobs) : -1], refs[-1]
    tile_x, tile_y = sources[0].shape[2:4]
    _, me, flip = position()
    sign = sign_of(flip)
    for job, turn in enumerate(jobs):
        spot = pl.ds(pl.multiple_of((me ^ turn) * tile_y, tile_y), tile_y)
        for side in range(2):
            for out in range(DEEP):
                row = row_of(flip, side, out, tile_x)
                lam = mu = 0.0
                if before and job < before[0].shape[0]:
                    lam, mu = before[0][job, 0, row], before[0][job, 1, row]
                for moment in jobs[turn]:
                    weight = (KERNEL_SCALE / UNIT) * residual[0, me, moment]
                    held = rates[4 * moment + 2 * (out // REACH) + side]
                    rate = [held[c, out % REACH, spot, :] for c in range(6)]
                    source = [sources[job][moment, c, row] for c in range(6)]
                    bulk = (source[0] + source[1] + source[2]) * (rate[0] + rate[1] + rate[2])
                    diag = source[0] * rate[0] + source[1] * rate[1] + source[2] * rate[2]
                    off = sign * (source[3] * rate[3] + source[4] * rate[4]) + source[5] * rate[5]
                    lam = lam + weight * bulk
                    mu = mu + (2.0 * weight) * (diag + off)
                terms[job, 0, row] = lam
                terms[job, 1, row] = mu


def swap(array, axis, turn):
    count = lax.axis_size(axis)
    return lax.ppermute(array, axis, [(i, i ^ turn) for i in range(count)])


def partner(slab, piece, slabs, side):
    other = slab + 1 - 2 * ((slab + piece + side) % 2)
    return other, (other >= 0) & (other < slabs)


def to_neighbour(face, side):
    slabs, pieces = lax.axis_size("gx"), lax.axis_size("gy")
    pairs = []
    for slab in range(slabs):
        for piece in range(pieces):
            other, inside = partner(slab, piece, slabs, side)
            if inside:
                pairs.append((slab * pieces + piece, other * pieces + piece))
    return lax.ppermute(face, ("gx", "gy"), pairs)


def local(rec_state, source_strain, material, material_table, residual, rec_cell, listed, src_pick):
    state = rec_state[0]
    receivers, _, tile_x, tile_y, depth = state.shape
    pieces, slabs, groups = lax.axis_size("gy"), lax.axis_size("gx"), lax.axis_size("sta")
    assert receivers == pieces and tile_x == 2 * DEEP
    assert pieces & (pieces - 1) == 0 and groups & (groups - 1) == 0
    size_y = pieces * tile_y
    group, me = lax.axis_index("sta"), lax.axis_index("gy")
    moments = residual.shape[2]

    numbers = material.astype(F32)[None]
    order = sorted(range(pieces), reverse=True)
    picked = {turn: lax.dynamic_index_in_dim(state, me ^ turn, 0, keepdims=False) for turn in order}
    own, picked = lax.optimization_barrier((source_strain[0], picked))
    chunks = {turn: jnp.concatenate([picked[turn], numbers], 0) for turn in order}
    chunks = [swap(chunks[turn], "gy", turn) if turn else chunks[turn] for turn in range(pieces)]
    strains = [swap(own, "sta", turn) if turn else own for turn in range(groups)]

    def shape(*lead, kind=F32):
        return lead + (size_y, depth), kind

    vel_shape, pair_shape = shape(3, DEEP), shape(6, REACH)
    halo_shape, sent_shape = shape(3, REACH), shape(3 * PACKED, kind=BF16)

    results = call(
        assemble,
        [vel_shape, pair_shape, pair_shape, shape(DEEP), shape(4, REACH)] * 2,
        ([], chunks),
        [pltpu.VMEM((8, size_y, depth), F32)],
    )
    vels, middles, edges, cells, faces = ([results[at], results[5 + at]] for at in range(5))
    halos = [to_neighbour(faces[side], side) for side in range(2)]

    strains, cells = lax.optimization_barrier((strains, cells))
    weights = lax.dynamic_slice_in_dim(listed, group, 1, 2)[:, :, 0].astype(F32)
    combined = 0.0
    for turn in range(groups):
        factor = jnp.sum(weights * (src_pick == (group ^ turn)).astype(F32), 0)
        combined = combined + factor[:, None, None, None, None] * strains[turn].astype(F32)
    combined, halos = lax.optimization_barrier((combined, halos))
    found = {turn: swap(combined, "gy", turn) for turn in range(pieces - 1, 0, -1) if turn & (turn - 1) == 0}
    found[0] = combined

    sent, lights, lames, shears, old_halos, spots, amounts = ([None, None] for _ in range(7))
    fresh = [None, None]
    for side in range(2):
        results = call(
            functools.partial(first, side),
            [vel_shape, sent_shape, shape(DEEP), shape(DEEP + REACH), shape(DEEP + REACH), halo_shape]
            + [shape(DEEP), shape(moments)],
            (
                [material_table, residual, rec_cell],
                [vels[side], middles[side], middles[1 - side], edges[side], cells[side], halos[side]],
            ),
        )
        fresh[side], sent[side], lights[side], lames[side], shears[side], old_halos[side] = results[:6]
        spots[side], amounts[side] = results[6:]
        sent[side] = to_neighbour(sent[side], side)
    vels = fresh

    rates = []
    for moment in range(moments):
        last = moment == moments - 1
        results = call(
            functools.partial(inner, last),
            [pair_shape] * (2 if last else 4),
            ([], vels if last else vels + middles + lames + shears),
        )
        rates += results[:2]
        if not last:
            middles = results[2:]
        if moment == 3 * moments // 4:
            ready, rates[-1] = lax.optimization_barrier((found, rates[-1]))
            for turn in range(pieces):
                if turn not in found:
                    low = turn & -turn
                    found[turn] = swap(ready[turn ^ low], "gy", low)
        if last:
            early, late = list(range(pieces)), []
            jobs = {turn: list(range(moment)) for turn in early}
            (terms,) = call(
                functools.partial(correlate, jobs, moment),
                [((len(jobs), 2, tile_x, tile_y, depth), F32)],
                ([residual], rates[: 4 * moment] + [found[turn] for turn in jobs]),
            )
            terms, vels = lax.optimization_barrier((terms, vels))
        fresh = [None, None]
        for side in range(2):
            arrays = [vels[side], sent[side], edges[side]]
            outs = [pair_shape]
            if not last:
                arrays += [old_halos[side], middles[side], middles[1 - side]]
                arrays += [lights[side], lames[side], shears[side], spots[side], amounts[side]]
                outs += [pair_shape, halo_shape, vel_shape, sent_shape]
            results = call(functools.partial(outer, side, moment, last), outs, ([], arrays))
            rates.append(results[0])
            if not last:
                edges[side], old_halos[side], fresh[side] = results[1:4]
                sent[side] = to_neighbour(results[4], side)
        vels = fresh

    jobs = {turn: [moments - 1] if turn in early else list(range(moments)) for turn in early + late}
    (terms,) = call(
        functools.partial(correlate, jobs, moments),
        [((pieces, 2, tile_x, tile_y, depth), F32)],
        ([residual], rates + [found[turn] for turn in jobs] + [terms]),
    )
    held = {turn: terms[at] for at, turn in enumerate(jobs)}
    if pieces > 1:
        keep = [turn for turn in held if not turn & 1]
        got = swap(jnp.stack([held[turn ^ 1] for turn in keep]), "gy", 1)
        held = {turn: held[turn] + got[at] for at, turn in enumerate(keep)}
    share = tile_x // groups
    result = 0.0
    for across_sta in reversed(range(groups)):
        for turn in reversed(list(held)):
            part = lax.dynamic_slice_in_dim(held[turn], (group ^ across_sta) * share, share, 1)
            if across_sta or turn:
                pairs = [
                    (a * pieces + b, (a ^ across_sta) * pieces + (b ^ turn))
                    for a in range(groups)
                    for b in range(pieces)
                ]
                part = lax.ppermute(part, ("sta", "gy"), pairs)
            result = result + part
    return result


def solution(mesh):
    in_specs = (
        P("sta", None, None, "gx", "gy", None),
        P("sta", None, None, "gx", "gy", None),
        P("gx", "gy", None),
        P(),
        P("sta", None, None),
        P("sta", None),
        P(),
        P(),
    )
    out_specs = P(None, ("gx", "sta"), "gy", None)
    return jax.shard_map(local, mesh=mesh, in_specs=in_specs, out_specs=out_specs, check_vma=False)
```

```python
import functools

import jax
import jax.numpy as jnp
from jax import lax
from jax.experimental import pallas as pl
from jax.experimental.pallas import tpu as pltpu
from jax.sharding import PartitionSpec as P

NEAR = 8.0
UNIT = 12.0
SUBLANES = 8
TIME_STEP = 0.25
AMPLITUDE = 4.0
KERNEL_SCALE = 0.0625
STIFFNESS = 0.3
REACH = 2
DEEP = 2 * REACH
ALONG_X = (0, 3, 4)
NEAR_ROWS = 1
PACKED = DEEP + NEAR_ROWS

VMEM = pl.BlockSpec(memory_space=pltpu.VMEM)
SMEM = pl.BlockSpec(memory_space=pltpu.SMEM)
HBM = pl.BlockSpec(memory_space=pltpu.HBM)
F32, BF16 = jnp.float32, jnp.bfloat16


def call(body, outs, ins, scratch=(), flops=1_000_000):
    scalars, arrays, *far = ins
    far = far[0] if far else []
    return list(pl.pallas_call(
        body,
        out_shape=[jax.ShapeDtypeStruct(shape, kind) for shape, kind in outs],
        in_specs=[SMEM] * len(scalars) + [VMEM] * len(arrays) + [HBM] * len(far),
        out_specs=[VMEM] * len(outs),
        scratch_shapes=list(scratch),
        compiler_params=pltpu.CompilerParams(vmem_limit_bytes=6 * 1024 * 1024),
        cost_estimate=pl.CostEstimate(flops=flops, bytes_accessed=2_000_000, transcendentals=0),
    )(*scalars, *arrays, *far))


def band(depth):
    row = lax.broadcasted_iota(jnp.int32, (depth, depth), 0)
    step = row - lax.broadcasted_iota(jnp.int32, (depth, depth), 1)
    parts = jnp.where(step == 1, NEAR, 0.0) - jnp.where(step == -1, NEAR, 0.0)
    parts = parts - jnp.where(step == 2, 1.0, 0.0) + jnp.where(step == -2, 1.0, 0.0)
    parts = parts.astype(BF16)
    return jnp.concatenate([parts, parts], 0)


def along_depth(rows):
    stacked = jnp.concatenate(rows, 0)
    high = stacked.astype(BF16)
    low = (stacked - high.astype(F32)).astype(BF16)
    split = jnp.concatenate([high, low], 1)
    result = jnp.dot(split, band(stacked.shape[1]), preferred_element_type=F32)
    size = rows[0].shape[0]
    return [result[at * size : (at + 1) * size] for at in range(len(rows))]


def along_y(row):
    count = row.shape[0] // SUBLANES
    at = lax.broadcasted_iota(jnp.int32, (SUBLANES, row.shape[1]), 0)
    planes = [row[SUBLANES * p : SUBLANES * (p + 1)] for p in range(count)]
    before = [jnp.where(at > 0, pltpu.roll(plane, 1, 0), 0.0) for plane in planes[-2:]]
    after = [jnp.where(at < SUBLANES - 1, pltpu.roll(plane, SUBLANES - 1, 0), 0.0) for plane in planes[:2]]
    spread = before + planes + after

    def shifted(by):
        return jnp.concatenate(spread[2 + by : 2 + by + count], 0)

    return shifted(1) - shifted(-1), shifted(2) - shifted(-2)


def across(rows, out, side):
    near, far = rows(out + 1) - rows(out - 1), rows(out + 2) - rows(out - 2)
    return (-near, -far) if side else (near, far)


def across_and_along(rows, out, side, row):
    near_y, far_y = along_y(row)
    near, far = rows(out + 1) - rows(out - 1), rows(out + 2) - rows(out - 2)
    if side:
        return NEAR * (near_y - near) - (far_y - far)
    return NEAR * (near_y + near) - (far_y + far)


def derivative(pair):
    return NEAR * pair[0] - pair[1]


MIRRORED_VEL = (0,)
MIRRORED_STRESS = (3, 4)


def position():
    slab, me = lax.axis_index("gx"), lax.axis_index("gy")
    return slab, me, (slab + me) % 2


def sign_of(flip):
    return 1.0 - 2.0 * flip.astype(F32)


def row_of(flip, side, out, tile_x):
    x = tile_x // 2 - 1 - out if side else tile_x // 2 + out
    return x + flip * (tile_x - 1 - 2 * x)


def interleave(me, tiles, comp, row, held):
    tile_y = tiles[0].shape[2]
    for turn, tile in enumerate(tiles):
        held[pl.ds(pl.multiple_of((me ^ turn) * tile_y, tile_y), tile_y), :] = tile[comp, row]
    count = held.shape[0] // SUBLANES
    return jnp.concatenate([held[pl.ds(p, SUBLANES, stride=count), :] for p in range(count)], 0)


def assemble(*refs):
    count = len(refs) - 11
    tiles, sides, held = refs[:count], (refs[count : count + 5], refs[count + 5 : -1]), refs[-1]
    tile_x = tiles[0].shape[1]
    _, me, flip = position()
    sign = sign_of(flip)
    face_comps = tuple(3 + comp for comp in ALONG_X) + (9,)
    for side, (vel, middle, edge, cells, face) in enumerate(sides):
        for out in range(DEEP):
            row = row_of(flip, side, out, tile_x)
            part, at = (middle, out) if out < REACH else (edge, out - REACH)
            for comp in range(10):
                value = interleave(me, tiles, comp, row, held.at[(out * 10 + comp) % held.shape[0]])
                if comp in MIRRORED_VEL or comp - 3 in MIRRORED_STRESS:
                    value = sign * value
                if comp < 3:
                    vel[comp, out] = value
                elif comp < 9:
                    part[comp - 3, at] = value
                else:
                    cells[out] = value
                if out >= REACH and comp in face_comps:
                    face[face_comps.index(comp), out - REACH] = value


def push(side, spots, amount, stress_row, vel, light, vel_out, sent):
    rows = [functools.partial(stress_row, comp) for comp in range(6)]
    deep = along_depth([rows[comp](out) for out in range(DEEP) for comp in (4, 5, 2)])
    for out in range(DEEP):
        force_x = across_and_along(rows[0], out, side, rows[3](out)) + deep[3 * out]
        force_y = across_and_along(rows[3], out, side, rows[1](out)) + deep[3 * out + 1]
        force_z = across_and_along(rows[4], out, side, rows[5](out)) + deep[3 * out + 2]
        force_z = force_z + amount * spots[out]
        near = DEEP - 1 - out
        for comp, force in enumerate((force_x, force_y, force_z)):
            fresh = vel[comp, out] + light[out] * force
            vel_out[comp, out] = fresh
            if comp in MIRRORED_VEL:
                fresh = -fresh
            high = fresh.astype(BF16)
            if near < NEAR_ROWS:
                sent[comp * PACKED + 2 * near] = high
                sent[comp * PACKED + 2 * near + 1] = (fresh - high.astype(F32)).astype(BF16)
            else:
                sent[comp * PACKED + NEAR_ROWS + near] = high


def from_halo(halo, comp, near):
    if near < NEAR_ROWS:
        at = comp * PACKED + 2 * near
        return halo[at].astype(F32) + halo[at + 1].astype(F32)
    return halo[comp * PACKED + NEAR_ROWS + near].astype(F32)


def first(side, table, residual, rec_cell, vel, middle, other, edge, cells, halo, *outs):
    vel_out, sent, light, lame, shear, halo_out, spots, amounts = outs
    size_y, depth = vel.shape[2:]
    planes = size_y // SUBLANES
    slab, me, flip = position()
    cell = rec_cell[0, me]
    spot_x, spot_y = cell // size_y - slab * (2 * DEEP), cell % size_y
    spot_x = spot_x + flip * (2 * DEEP - 1 - 2 * spot_x)
    spot_y = (spot_y % planes) * SUBLANES + spot_y // planes
    at_spot = (lax.broadcasted_iota(jnp.int32, (size_y, depth), 0) == spot_y) & (
        lax.broadcasted_iota(jnp.int32, (size_y, depth), 1) == 0
    )
    for out in range(DEEP):
        here = spot_x == (DEEP - 1 - out if side else DEEP + out)
        spots[out] = jnp.where(at_spot, jnp.where(here, UNIT * AMPLITUDE, 0.0), 0.0)
    for moment in range(residual.shape[2]):
        amounts[moment] = jnp.full((size_y, depth), residual[0, me, moment], F32)
    _, inside = partner(slab, me, lax.axis_size("gx"), side)
    count = table.shape[0]
    for out in range(DEEP + REACH):
        if out < DEEP:
            number, share = cells[out], 1.0
        else:
            number = halo[len(ALONG_X), REACH - 1 - (out - DEEP)]
            share = jnp.where(inside, 1.0, 0.0)
        parts = [jnp.full(number.shape, table[0, c], F32) for c in range(3)]
        for m in range(1, count):
            hit = number == float(m)
            parts = [jnp.where(hit, table[m, c], parts[c]) for c in range(3)]
        lame[out] = (TIME_STEP * STIFFNESS / UNIT * share) * parts[1]
        shear[out] = (TIME_STEP * STIFFNESS / UNIT * share) * parts[2]
        if out < DEEP:
            light[out] = (TIME_STEP / UNIT) / parts[0]
    for at in range(len(ALONG_X)):
        for near in range(REACH):
            value = halo[at, REACH - 1 - near]
            halo_out[at, near] = -value if ALONG_X[at] in MIRRORED_STRESS else value
    push(side, spots, amounts[0], stress_rows(middle, other, edge, halo_out), vel, light, vel_out, sent)


def stress_rows(middle, other, edge, halo):
    def row(comp, out):
        if out < 0:
            return other[comp, -1 - out]
        if out < REACH:
            return middle[comp, out]
        if out < DEEP:
            return edge[comp, out - REACH]
        return halo[ALONG_X.index(comp), out - DEEP]

    return row


def strain_rates(vx, vy, vz, side, first_out, last_out, full_out):
    outs = range(first_out, last_out)
    wanted = [(vel, out) for out in outs for vel in (vx, vz)] + [(vy, out) for out in outs if out < full_out]
    deep = along_depth([vel(out) for vel, out in wanted])
    deep = {key: value for key, value in zip(wanted, deep)}
    for out in outs:
        rates = [
            derivative(across(vx, out, side)),
            derivative(along_y(vy(out))),
            deep[vz, out],
            across_and_along(vy, out, side, vx(out)),
            deep[vx, out] + derivative(across(vz, out, side)),
        ]
        if out < full_out:
            rates.append(deep[vy, out] + derivative(along_y(vz(out))))
        yield out, rates


def store(target, at, rates):
    count = rates[0].shape[0] // SUBLANES
    for comp, rate in enumerate(rates):
        for p in range(count):
            spot = pl.ds(p, SUBLANES, stride=count)
            target[comp, at, spot, :] = rate[SUBLANES * p : SUBLANES * (p + 1)]


def renew(rates, lame, shear, before):
    bulk = lame * (rates[0] + rates[1] + rates[2])
    twice = shear + shear
    return {
        comp: old + (bulk + twice * rates[comp] if comp < 3 else shear * rates[comp])
        for comp, old in before.items()
    }


def outer(side, moment, last, vel, halo, edge, *refs):
    if last:
        (rates_out,) = refs
    else:
        old_halo, middle, other, light, lame, shear, spots, amounts, rates_out, edge_out, halo_out, vel_out, sent = refs

    def rows(comp):
        return lambda out: vel[comp, out] if out < DEEP else from_halo(halo, comp, out - DEEP)

    until = DEEP if last else DEEP + REACH
    for out, rates in strain_rates(rows(0), rows(1), rows(2), side, REACH, until, DEEP):
        own = out < DEEP
        if own:
            store(rates_out, out - REACH, rates)
        if last:
            continue
        if own:
            fresh = renew(rates, lame[out], shear[out], {comp: edge[comp, out - REACH] for comp in range(6)})
            for comp, value in fresh.items():
                edge_out[comp, out - REACH] = value
        else:
            before = {comp: old_halo[at, out - DEEP] for at, comp in enumerate(ALONG_X)}
            fresh = renew(rates, lame[out], shear[out], before)
            for at, comp in enumerate(ALONG_X):
                halo_out[at, out - DEEP] = fresh[comp]
    if not last:
        rows = stress_rows(middle, other, edge_out, halo_out)
        push(side, spots, amounts[moment + 1], rows, vel, light, vel_out, sent)


def inner(last, *refs):
    vels = refs[:2]
    if last:
        rates_out = refs[2:]
    else:
        middles, lames, shears = refs[2:4], refs[4:6], refs[6:8]
        rates_out, middles_out = refs[8:10], refs[10:12]
    for side in range(2):

        def rows(comp):
            return lambda out: vels[side][comp, out] if out >= 0 else vels[1 - side][comp, -1 - out]

        for out, rates in strain_rates(rows(0), rows(1), rows(2), side, 0, REACH, REACH):
            store(rates_out[side], out, rates)
            if not last:
                before = {comp: middles[side][comp, out] for comp in range(6)}
                fresh = renew(rates, lames[side][out], shears[side][out], before)
                for comp, value in fresh.items():
                    middles_out[side][comp, out] = value


def correlate(jobs, moments, residual, *refs):
    rates, refs = refs[: 4 * moments], refs[4 * moments :]
    terms, slots, arrived = refs[-3:]
    sources, before = refs[-3 - len(jobs) : -3], refs[: -3 - len(jobs)]
    tile_x, tile_y = sources[0].shape[2:4]
    _, me, flip = position()
    sign = sign_of(flip)
    steps = sorted({moment for wanted in jobs.values() for moment in wanted})
    work = {step: [job for job, turn in enumerate(jobs) if step in jobs[turn]] for step in steps}

    def fetch(at, job):
        slot = at % 2
        return pltpu.make_async_copy(sources[job].at[steps[at]], slots.at[slot, job], arrived.at[slot, job])

    for job in work[steps[0]]:
        fetch(0, job).start()
    done = set()
    for at, moment in enumerate(steps):
        if at + 1 < len(steps):
            for job in work[steps[at + 1]]:
                fetch(at + 1, job).start()
        weight = (KERNEL_SCALE / UNIT) * residual[0, me, moment]
        for job in work[moment]:
            fetch(at, job).wait()
            turn = list(jobs)[job]
            spot = pl.ds(pl.multiple_of((me ^ turn) * tile_y, tile_y), tile_y)
            for side in range(2):
                for out in range(DEEP):
                    row = row_of(flip, side, out, tile_x)
                    held = rates[4 * moment + 2 * (out // REACH) + side]
                    rate = [held[c, out % REACH, spot, :] for c in range(6)]
                    source = [slots[at % 2, job, c, row] for c in range(6)]
                    bulk = (source[0] + source[1] + source[2]) * (rate[0] + rate[1] + rate[2])
                    diag = source[0] * rate[0] + source[1] * rate[1] + source[2] * rate[2]
                    off = sign * (source[3] * rate[3] + source[4] * rate[4]) + source[5] * rate[5]
                    lam, mu = weight * bulk, (2.0 * weight) * (diag + off)
                    if job in done:
                        lam, mu = terms[job, 0, row] + lam, terms[job, 1, row] + mu
                    elif before and job < before[0].shape[0]:
                        lam, mu = before[0][job, 0, row] + lam, before[0][job, 1, row] + mu
                    terms[job, 0, row] = lam
                    terms[job, 1, row] = mu
            done.add(job)


def correlated(jobs, moments, residual, rates, found, before):
    one = found[0].shape[1:]
    (terms,) = call(
        functools.partial(correlate, jobs, moments),
        [((len(jobs), 2) + one[1:], F32)],
        ([residual], rates + before, [found[turn] for turn in jobs]),
        [pltpu.VMEM((2, len(jobs)) + one, F32), pltpu.SemaphoreType.DMA((2, len(jobs)))],
    )
    return terms


def swap(array, axis, turn):
    count = lax.axis_size(axis)
    return lax.ppermute(array, axis, [(i, i ^ turn) for i in range(count)])


def partner(slab, piece, slabs, side):
    other = slab + 1 - 2 * ((slab + piece + side) % 2)
    return other, (other >= 0) & (other < slabs)


def to_neighbour(face, side):
    slabs, pieces = lax.axis_size("gx"), lax.axis_size("gy")
    pairs = []
    for slab in range(slabs):
        for piece in range(pieces):
            other, inside = partner(slab, piece, slabs, side)
            if inside:
                pairs.append((slab * pieces + piece, other * pieces + piece))
    return lax.ppermute(face, ("gx", "gy"), pairs)


def local(rec_state, source_strain, material, material_table, residual, rec_cell, listed, src_pick):
    state = rec_state[0]
    receivers, _, tile_x, tile_y, depth = state.shape
    pieces, slabs, groups = lax.axis_size("gy"), lax.axis_size("gx"), lax.axis_size("sta")
    assert receivers == pieces and tile_x == 2 * DEEP
    assert pieces & (pieces - 1) == 0 and groups & (groups - 1) == 0
    size_y = pieces * tile_y
    group, me = lax.axis_index("sta"), lax.axis_index("gy")
    moments = residual.shape[2]

    numbers = material.astype(F32)[None]
    order = sorted(range(pieces), reverse=True)
    picked = {turn: lax.dynamic_index_in_dim(state, me ^ turn, 0, keepdims=False) for turn in order}
    own, picked = lax.optimization_barrier((source_strain[0], picked))
    chunks = {turn: jnp.concatenate([picked[turn], numbers], 0) for turn in order}
    chunks = [swap(chunks[turn], "gy", turn) if turn else chunks[turn] for turn in range(pieces)]
    strains = [swap(own, "sta", turn) if turn else own for turn in range(groups)]

    def shape(*lead, kind=F32):
        return lead + (size_y, depth), kind

    vel_shape, pair_shape = shape(3, DEEP), shape(6, REACH)
    halo_shape, sent_shape = shape(3, REACH), shape(3 * PACKED, kind=BF16)

    results = call(
        assemble,
        [vel_shape, pair_shape, pair_shape, shape(DEEP), shape(4, REACH)] * 2,
        ([], chunks),
        [pltpu.VMEM((8, size_y, depth), F32)],
    )
    vels, middles, edges, cells, faces = ([results[at], results[5 + at]] for at in range(5))
    halos = [to_neighbour(faces[side], side) for side in range(2)]

    strains, cells = lax.optimization_barrier((strains, cells))
    weights = lax.dynamic_slice_in_dim(listed, group, 1, 2)[:, :, 0].astype(F32)
    combined = 0.0
    for turn in range(groups):
        factor = jnp.sum(weights * (src_pick == (group ^ turn)).astype(F32), 0)
        combined = combined + factor[:, None, None, None, None] * strains[turn].astype(F32)
    combined, halos = lax.optimization_barrier((combined, halos))
    found = {turn: swap(combined, "gy", turn) for turn in range(pieces - 1, 0, -1) if turn & (turn - 1) == 0}
    found[0] = combined

    sent, lights, lames, shears, old_halos, spots, amounts = ([None, None] for _ in range(7))
    fresh = [None, None]
    for side in range(2):
        results = call(
            functools.partial(first, side),
            [vel_shape, sent_shape, shape(DEEP), shape(DEEP + REACH), shape(DEEP + REACH), halo_shape]
            + [shape(DEEP), shape(moments)],
            (
                [material_table, residual, rec_cell],
                [vels[side], middles[side], middles[1 - side], edges[side], cells[side], halos[side]],
            ),
        )
        fresh[side], sent[side], lights[side], lames[side], shears[side], old_halos[side] = results[:6]
        spots[side], amounts[side] = results[6:]
        sent[side] = to_neighbour(sent[side], side)
    vels = fresh

    rates = []
    for moment in range(moments):
        last = moment == moments - 1
        results = call(
            functools.partial(inner, last),
            [pair_shape] * (2 if last else 4),
            ([], vels if last else vels + middles + lames + shears),
        )
        rates += results[:2]
        if not last:
            middles = results[2:]
        if moment == 3 * moments // 4:
            ready, rates[-1] = lax.optimization_barrier((found, rates[-1]))
            for turn in range(pieces):
                if turn not in found:
                    low = turn & -turn
                    found[turn] = swap(ready[turn ^ low], "gy", low)
        if last:
            early, late = list(range(pieces)), []
            jobs = {turn: list(range(moment)) for turn in early}
            terms = correlated(jobs, moment, residual, rates[: 4 * moment], found, [])
            terms, vels = lax.optimization_barrier((terms, vels))
        fresh = [None, None]
        for side in range(2):
            arrays = [vels[side], sent[side], edges[side]]
            outs = [pair_shape]
            if not last:
                arrays += [old_halos[side], middles[side], middles[1 - side]]
                arrays += [lights[side], lames[side], shears[side], spots[side], amounts[side]]
                outs += [pair_shape, halo_shape, vel_shape, sent_shape]
            results = call(functools.partial(outer, side, moment, last), outs, ([], arrays))
            rates.append(results[0])
            if not last:
                edges[side], old_halos[side], fresh[side] = results[1:4]
                sent[side] = to_neighbour(results[4], side)
        vels = fresh

    jobs = {turn: [moments - 1] if turn in early else list(range(moments)) for turn in early + late}
    terms = correlated(jobs, moments, residual, rates, found, [terms])
    held = {turn: terms[at] for at, turn in enumerate(jobs)}
    if pieces > 1:
        keep = [turn for turn in held if not turn & 1]
        got = swap(jnp.stack([held[turn ^ 1] for turn in keep]), "gy", 1)
        held = {turn: held[turn] + got[at] for at, turn in enumerate(keep)}
    share = tile_x // groups
    result = 0.0
    for across_sta in reversed(range(groups)):
        for turn in reversed(list(held)):
            part = lax.dynamic_slice_in_dim(held[turn], (group ^ across_sta) * share, share, 1)
            if across_sta or turn:
                pairs = [
                    (a * pieces + b, (a ^ across_sta) * pieces + (b ^ turn))
                    for a in range(groups)
                    for b in range(pieces)
                ]
                part = lax.ppermute(part, ("sta", "gy"), pairs)
            result = result + part
    return result


def solution(mesh):
    in_specs = (
        P("sta", None, None, "gx", "gy", None),
        P("sta", None, None, "gx", "gy", None),
        P("gx", "gy", None),
        P(),
        P("sta", None, None),
        P("sta", None),
        P(),
        P(),
    )
    out_specs = P(None, ("gx", "sta"), "gy", None)
    return jax.shard_map(local, mesh=mesh, in_specs=in_specs, out_specs=out_specs, check_vma=False)
```

```python
import functools

import jax
import jax.numpy as jnp
from jax import lax
from jax.experimental import pallas as pl
from jax.experimental.pallas import tpu as pltpu
from jax.sharding import PartitionSpec as P

NEAR = 8.0
UNIT = 12.0
SUBLANES = 8
TIME_STEP = 0.25
AMPLITUDE = 4.0
KERNEL_SCALE = 0.0625
STIFFNESS = 0.3
REACH = 2
DEEP = 2 * REACH
ALONG_X = (0, 3, 4)
NEAR_ROWS = 1
PACKED = DEEP + NEAR_ROWS

VMEM = pl.BlockSpec(memory_space=pltpu.VMEM)
SMEM = pl.BlockSpec(memory_space=pltpu.SMEM)
F32, BF16 = jnp.float32, jnp.bfloat16


def call(body, outs, ins, scratch=(), flops=1_000_000):
    scalars, arrays = ins
    return list(pl.pallas_call(
        body,
        out_shape=[jax.ShapeDtypeStruct(shape, kind) for shape, kind in outs],
        in_specs=[SMEM] * len(scalars) + [VMEM] * len(arrays),
        out_specs=[VMEM] * len(outs),
        scratch_shapes=list(scratch),
        compiler_params=pltpu.CompilerParams(vmem_limit_bytes=6 * 1024 * 1024),
        cost_estimate=pl.CostEstimate(flops=flops, bytes_accessed=2_000_000, transcendentals=0),
    )(*scalars, *arrays))


def band(depth):
    row = lax.broadcasted_iota(jnp.int32, (depth, depth), 0)
    step = row - lax.broadcasted_iota(jnp.int32, (depth, depth), 1)
    parts = jnp.where(step == 1, NEAR, 0.0) - jnp.where(step == -1, NEAR, 0.0)
    parts = parts - jnp.where(step == 2, 1.0, 0.0) + jnp.where(step == -2, 1.0, 0.0)
    parts = parts.astype(BF16)
    return jnp.concatenate([parts, parts], 0)


def along_depth(rows):
    stacked = jnp.concatenate(rows, 0)
    high = stacked.astype(BF16)
    low = (stacked - high.astype(F32)).astype(BF16)
    split = jnp.concatenate([high, low], 1)
    result = jnp.dot(split, band(stacked.shape[1]), preferred_element_type=F32)
    size = rows[0].shape[0]
    return [result[at * size : (at + 1) * size] for at in range(len(rows))]


def along_y(row):
    count = row.shape[0] // SUBLANES
    at = lax.broadcasted_iota(jnp.int32, (SUBLANES, row.shape[1]), 0)
    planes = [row[SUBLANES * p : SUBLANES * (p + 1)] for p in range(count)]
    before = [jnp.where(at > 0, pltpu.roll(plane, 1, 0), 0.0) for plane in planes[-2:]]
    after = [jnp.where(at < SUBLANES - 1, pltpu.roll(plane, SUBLANES - 1, 0), 0.0) for plane in planes[:2]]
    spread = before + planes + after

    def shifted(by):
        return jnp.concatenate(spread[2 + by : 2 + by + count], 0)

    return shifted(1) - shifted(-1), shifted(2) - shifted(-2)


def across(rows, out, side):
    near, far = rows(out + 1) - rows(out - 1), rows(out + 2) - rows(out - 2)
    return (-near, -far) if side else (near, far)


def across_and_along(rows, out, side, row):
    near_y, far_y = along_y(row)
    near, far = rows(out + 1) - rows(out - 1), rows(out + 2) - rows(out - 2)
    if side:
        return NEAR * (near_y - near) - (far_y - far)
    return NEAR * (near_y + near) - (far_y + far)


def derivative(pair):
    return NEAR * pair[0] - pair[1]


MIRRORED_VEL = (0,)
MIRRORED_STRESS = (3, 4)


def position():
    slab, me = lax.axis_index("gx"), lax.axis_index("gy")
    return slab, me, (slab + me) % 2


def sign_of(flip):
    return 1.0 - 2.0 * flip.astype(F32)


def row_of(flip, side, out, tile_x):
    x = tile_x // 2 - 1 - out if side else tile_x // 2 + out
    return x + flip * (tile_x - 1 - 2 * x)


def interleave(me, tiles, comp, row, held):
    tile_y = tiles[0].shape[2]
    for turn, tile in enumerate(tiles):
        held[pl.ds(pl.multiple_of((me ^ turn) * tile_y, tile_y), tile_y), :] = tile[comp, row]
    count = held.shape[0] // SUBLANES
    return jnp.concatenate([held[pl.ds(p, SUBLANES, stride=count), :] for p in range(count)], 0)


def assemble(*refs):
    count = len(refs) - 11
    tiles, sides, held = refs[:count], (refs[count : count + 5], refs[count + 5 : -1]), refs[-1]
    tile_x = tiles[0].shape[1]
    _, me, flip = position()
    sign = sign_of(flip)
    face_comps = tuple(3 + comp for comp in ALONG_X) + (9,)
    for side, (vel, middle, edge, cells, face) in enumerate(sides):
        for out in range(DEEP):
            row = row_of(flip, side, out, tile_x)
            part, at = (middle, out) if out < REACH else (edge, out - REACH)
            for comp in range(10):
                value = interleave(me, tiles, comp, row, held.at[(out * 10 + comp) % held.shape[0]])
                if comp in MIRRORED_VEL or comp - 3 in MIRRORED_STRESS:
                    value = sign * value
                if comp < 3:
                    vel[comp, out] = value
                elif comp < 9:
                    part[comp - 3, at] = value
                else:
                    cells[out] = value
                if out >= REACH and comp in face_comps:
                    face[face_comps.index(comp), out - REACH] = value


def push(side, spots, amount, stress_row, vel, light, vel_out, sent):
    rows = [functools.partial(stress_row, comp) for comp in range(6)]
    deep = along_depth([rows[comp](out) for out in range(DEEP) for comp in (4, 5, 2)])
    for out in range(DEEP):
        force_x = across_and_along(rows[0], out, side, rows[3](out)) + deep[3 * out]
        force_y = across_and_along(rows[3], out, side, rows[1](out)) + deep[3 * out + 1]
        force_z = across_and_along(rows[4], out, side, rows[5](out)) + deep[3 * out + 2]
        force_z = force_z + amount * spots[out]
        near = DEEP - 1 - out
        for comp, force in enumerate((force_x, force_y, force_z)):
            fresh = vel[comp, out] + light[out] * force
            vel_out[comp, out] = fresh
            if comp in MIRRORED_VEL:
                fresh = -fresh
            high = fresh.astype(BF16)
            if near < NEAR_ROWS:
                sent[comp * PACKED + 2 * near] = high
                sent[comp * PACKED + 2 * near + 1] = (fresh - high.astype(F32)).astype(BF16)
            else:
                sent[comp * PACKED + NEAR_ROWS + near] = high


def from_halo(halo, comp, near):
    if near < NEAR_ROWS:
        at = comp * PACKED + 2 * near
        return halo[at].astype(F32) + halo[at + 1].astype(F32)
    return halo[comp * PACKED + NEAR_ROWS + near].astype(F32)


def first(side, table, residual, rec_cell, vel, middle, other, edge, cells, halo, *outs):
    vel_out, sent, light, lame, shear, halo_out, spots, amounts = outs
    size_y, depth = vel.shape[2:]
    planes = size_y // SUBLANES
    slab, me, flip = position()
    cell = rec_cell[0, me]
    spot_x, spot_y = cell // size_y - slab * (2 * DEEP), cell % size_y
    spot_x = spot_x + flip * (2 * DEEP - 1 - 2 * spot_x)
    spot_y = (spot_y % planes) * SUBLANES + spot_y // planes
    at_spot = (lax.broadcasted_iota(jnp.int32, (size_y, depth), 0) == spot_y) & (
        lax.broadcasted_iota(jnp.int32, (size_y, depth), 1) == 0
    )
    for out in range(DEEP):
        here = spot_x == (DEEP - 1 - out if side else DEEP + out)
        spots[out] = jnp.where(at_spot, jnp.where(here, UNIT * AMPLITUDE, 0.0), 0.0)
    for moment in range(residual.shape[2]):
        amounts[moment] = jnp.full((size_y, depth), residual[0, me, moment], F32)
    _, inside = partner(slab, me, lax.axis_size("gx"), side)
    count = table.shape[0]
    for out in range(DEEP + REACH):
        if out < DEEP:
            number, share = cells[out], 1.0
        else:
            number = halo[len(ALONG_X), REACH - 1 - (out - DEEP)]
            share = jnp.where(inside, 1.0, 0.0)
        parts = [jnp.full(number.shape, table[0, c], F32) for c in range(3)]
        for m in range(1, count):
            hit = number == float(m)
            parts = [jnp.where(hit, table[m, c], parts[c]) for c in range(3)]
        lame[out] = (TIME_STEP * STIFFNESS / UNIT * share) * parts[1]
        shear[out] = (TIME_STEP * STIFFNESS / UNIT * share) * parts[2]
        if out < DEEP:
            light[out] = (TIME_STEP / UNIT) / parts[0]
    for at in range(len(ALONG_X)):
        for near in range(REACH):
            value = halo[at, REACH - 1 - near]
            halo_out[at, near] = -value if ALONG_X[at] in MIRRORED_STRESS else value
    push(side, spots, amounts[0], stress_rows(middle, other, edge, halo_out), vel, light, vel_out, sent)


def stress_rows(middle, other, edge, halo):
    def row(comp, out):
        if out < 0:
            return other[comp, -1 - out]
        if out < REACH:
            return middle[comp, out]
        if out < DEEP:
            return edge[comp, out - REACH]
        return halo[ALONG_X.index(comp), out - DEEP]

    return row


def strain_rates(vx, vy, vz, side, first_out, last_out, full_out):
    outs = range(first_out, last_out)
    wanted = [(vel, out) for out in outs for vel in (vx, vz)] + [(vy, out) for out in outs if out < full_out]
    deep = along_depth([vel(out) for vel, out in wanted])
    deep = {key: value for key, value in zip(wanted, deep)}
    for out in outs:
        rates = [
            derivative(across(vx, out, side)),
            derivative(along_y(vy(out))),
            deep[vz, out],
            across_and_along(vy, out, side, vx(out)),
            deep[vx, out] + derivative(across(vz, out, side)),
        ]
        if out < full_out:
            rates.append(deep[vy, out] + derivative(along_y(vz(out))))
        yield out, rates


def store(target, at, rates):
    count = rates[0].shape[0] // SUBLANES
    for comp, rate in enumerate(rates):
        for p in range(count):
            spot = pl.ds(p, SUBLANES, stride=count)
            target[comp, at, spot, :] = rate[SUBLANES * p : SUBLANES * (p + 1)]


def renew(rates, lame, shear, before):
    bulk = lame * (rates[0] + rates[1] + rates[2])
    twice = shear + shear
    return {
        comp: old + (bulk + twice * rates[comp] if comp < 3 else shear * rates[comp])
        for comp, old in before.items()
    }


def outer(side, moment, last, vel, halo, edge, *refs):
    if last:
        (rates_out,) = refs
    else:
        old_halo, middle, other, light, lame, shear, spots, amounts, rates_out, edge_out, halo_out, vel_out, sent = refs

    def rows(comp):
        return lambda out: vel[comp, out] if out < DEEP else from_halo(halo, comp, out - DEEP)

    until = DEEP if last else DEEP + REACH
    for out, rates in strain_rates(rows(0), rows(1), rows(2), side, REACH, until, DEEP):
        own = out < DEEP
        if own:
            store(rates_out, out - REACH, rates)
        if last:
            continue
        if own:
            fresh = renew(rates, lame[out], shear[out], {comp: edge[comp, out - REACH] for comp in range(6)})
            for comp, value in fresh.items():
                edge_out[comp, out - REACH] = value
        else:
            before = {comp: old_halo[at, out - DEEP] for at, comp in enumerate(ALONG_X)}
            fresh = renew(rates, lame[out], shear[out], before)
            for at, comp in enumerate(ALONG_X):
                halo_out[at, out - DEEP] = fresh[comp]
    if not last:
        rows = stress_rows(middle, other, edge_out, halo_out)
        push(side, spots, amounts[moment + 1], rows, vel, light, vel_out, sent)


def inner(last, *refs):
    vels = refs[:2]
    if last:
        rates_out = refs[2:]
    else:
        middles, lames, shears = refs[2:4], refs[4:6], refs[6:8]
        rates_out, middles_out = refs[8:10], refs[10:12]
    for side in range(2):

        def rows(comp):
            return lambda out: vels[side][comp, out] if out >= 0 else vels[1 - side][comp, -1 - out]

        for out, rates in strain_rates(rows(0), rows(1), rows(2), side, 0, REACH, REACH):
            store(rates_out[side], out, rates)
            if not last:
                before = {comp: middles[side][comp, out] for comp in range(6)}
                fresh = renew(rates, lames[side][out], shears[side][out], before)
                for comp, value in fresh.items():
                    middles_out[side][comp, out] = value


def correlate(jobs, moments, residual, *refs):
    count = 4 * moments
    rates, sources, before, terms = refs[:count], refs[count : count + len(jobs)], refs[count + len(jobs) : -1], refs[-1]
    tile_x, tile_y = sources[0].shape[2:4]
    _, me, flip = position()
    sign = sign_of(flip)
    for job, turn in enumerate(jobs):
        spot = pl.ds(pl.multiple_of((me ^ turn) * tile_y, tile_y), tile_y)
        for side in range(2):
            for out in range(DEEP):
                row = row_of(flip, side, out, tile_x)
                lam = mu = 0.0
                if before and job < before[0].shape[0]:
                    lam, mu = before[0][job, 0, row], before[0][job, 1, row]
                for moment in jobs[turn]:
                    weight = (KERNEL_SCALE / UNIT) * residual[0, me, moment]
                    held = rates[4 * moment + 2 * (out // REACH) + side]
                    rate = [held[c, out % REACH, spot, :] for c in range(6)]
                    source = [sources[job][moment, c, row] for c in range(6)]
                    bulk = (source[0] + source[1] + source[2]) * (rate[0] + rate[1] + rate[2])
                    diag = source[0] * rate[0] + source[1] * rate[1] + source[2] * rate[2]
                    off = sign * (source[3] * rate[3] + source[4] * rate[4]) + source[5] * rate[5]
                    lam = lam + weight * bulk
                    mu = mu + (2.0 * weight) * (diag + off)
                terms[job, 0, row] = lam
                terms[job, 1, row] = mu


def combine(groups, listed, src_pick, *refs):
    strains, out = refs[:groups], refs[groups]
    group = lax.axis_index("sta")
    moments, comps = out.shape[:2]
    for moment in range(moments):
        factors = []
        for turn in range(groups):
            factor = 0
            for at in range(src_pick.shape[0]):
                factor += jnp.where(src_pick[at, moment] == (group ^ turn), listed[at, moment, group], 0)
            factors.append(factor.astype(F32))
        for comp in range(comps):
            total = 0.0
            for factor, strain in zip(factors, strains):
                total = total + factor * strain[moment, comp].astype(F32)
            out[moment, comp] = total


def swap(array, axis, turn):
    count = lax.axis_size(axis)
    return lax.ppermute(array, axis, [(i, i ^ turn) for i in range(count)])


def partner(slab, piece, slabs, side):
    other = slab + 1 - 2 * ((slab + piece + side) % 2)
    return other, (other >= 0) & (other < slabs)


def to_neighbour(face, side):
    slabs, pieces = lax.axis_size("gx"), lax.axis_size("gy")
    pairs = []
    for slab in range(slabs):
        for piece in range(pieces):
            other, inside = partner(slab, piece, slabs, side)
            if inside:
                pairs.append((slab * pieces + piece, other * pieces + piece))
    return lax.ppermute(face, ("gx", "gy"), pairs)


def local(rec_state, source_strain, material, material_table, residual, rec_cell, listed, src_pick):
    state = rec_state[0]
    receivers, _, tile_x, tile_y, depth = state.shape
    pieces, slabs, groups = lax.axis_size("gy"), lax.axis_size("gx"), lax.axis_size("sta")
    assert receivers == pieces and tile_x == 2 * DEEP
    assert pieces & (pieces - 1) == 0 and groups & (groups - 1) == 0
    size_y = pieces * tile_y
    group, me = lax.axis_index("sta"), lax.axis_index("gy")
    moments = residual.shape[2]

    numbers = material.astype(F32)[None]
    order = sorted(range(pieces), reverse=True)
    picked = {turn: lax.dynamic_index_in_dim(state, me ^ turn, 0, keepdims=False) for turn in order}
    own = source_strain[0].reshape(source_strain.shape[1:3] + (tile_x * tile_y, depth))
    own, picked = lax.optimization_barrier((own, picked))
    chunks = {turn: jnp.concatenate([picked[turn], numbers], 0) for turn in order}
    chunks = [swap(chunks[turn], "gy", turn) if turn else chunks[turn] for turn in range(pieces)]
    strains = [swap(own, "sta", turn) if turn else own for turn in range(groups)]

    def shape(*lead, kind=F32):
        return lead + (size_y, depth), kind

    vel_shape, pair_shape = shape(3, DEEP), shape(6, REACH)
    halo_shape, sent_shape = shape(3, REACH), shape(3 * PACKED, kind=BF16)

    results = call(
        assemble,
        [vel_shape, pair_shape, pair_shape, shape(DEEP), shape(4, REACH)] * 2,
        ([], chunks),
        [pltpu.VMEM((8, size_y, depth), F32)],
    )
    vels, middles, edges, cells, faces = ([results[at], results[5 + at]] for at in range(5))
    halos = [to_neighbour(faces[side], side) for side in range(2)]

    strains, cells = lax.optimization_barrier((strains, cells))
    (combined,) = call(
        functools.partial(combine, groups), [(own.shape, F32)], ([listed, src_pick], strains)
    )
    combined = combined.reshape(own.shape[:2] + (tile_x, tile_y, depth))
    combined, halos = lax.optimization_barrier((combined, halos))
    found = {turn: swap(combined, "gy", turn) for turn in range(pieces - 1, 0, -1) if turn & (turn - 1) == 0}
    found[0] = combined

    sent, lights, lames, shears, old_halos, spots, amounts = ([None, None] for _ in range(7))
    fresh = [None, None]
    for side in range(2):
        results = call(
            functools.partial(first, side),
            [vel_shape, sent_shape, shape(DEEP), shape(DEEP + REACH), shape(DEEP + REACH), halo_shape]
            + [shape(DEEP), shape(moments)],
            (
                [material_table, residual, rec_cell],
                [vels[side], middles[side], middles[1 - side], edges[side], cells[side], halos[side]],
            ),
        )
        fresh[side], sent[side], lights[side], lames[side], shears[side], old_halos[side] = results[:6]
        spots[side], amounts[side] = results[6:]
        sent[side] = to_neighbour(sent[side], side)
    vels = fresh

    rates = []
    for moment in range(moments):
        last = moment == moments - 1
        results = call(
            functools.partial(inner, last),
            [pair_shape] * (2 if last else 4),
            ([], vels if last else vels + middles + lames + shears),
        )
        rates += results[:2]
        if not last:
            middles = results[2:]
        if moment == 3 * moments // 4:
            ready, rates[-1] = lax.optimization_barrier((found, rates[-1]))
            for turn in range(pieces):
                if turn not in found:
                    low = turn & -turn
                    found[turn] = swap(ready[turn ^ low], "gy", low)
        if last:
            early, late = list(range(pieces)), []
            jobs = {turn: list(range(moment)) for turn in early}
            (terms,) = call(
                functools.partial(correlate, jobs, moment),
                [((len(jobs), 2, tile_x, tile_y, depth), F32)],
                ([residual], rates[: 4 * moment] + [found[turn] for turn in jobs]),
            )
            terms, vels = lax.optimization_barrier((terms, vels))
        fresh = [None, None]
        for side in range(2):
            arrays = [vels[side], sent[side], edges[side]]
            outs = [pair_shape]
            if not last:
                arrays += [old_halos[side], middles[side], middles[1 - side]]
                arrays += [lights[side], lames[side], shears[side], spots[side], amounts[side]]
                outs += [pair_shape, halo_shape, vel_shape, sent_shape]
            results = call(functools.partial(outer, side, moment, last), outs, ([], arrays))
            rates.append(results[0])
            if not last:
                edges[side], old_halos[side], fresh[side] = results[1:4]
                sent[side] = to_neighbour(results[4], side)
        vels = fresh

    jobs = {turn: [moments - 1] if turn in early else list(range(moments)) for turn in early + late}
    (terms,) = call(
        functools.partial(correlate, jobs, moments),
        [((pieces, 2, tile_x, tile_y, depth), F32)],
        ([residual], rates + [found[turn] for turn in jobs] + [terms]),
    )
    held = {turn: terms[at] for at, turn in enumerate(jobs)}
    if pieces > 1:
        keep = [turn for turn in held if not turn & 1]
        got = swap(jnp.stack([held[turn ^ 1] for turn in keep]), "gy", 1)
        held = {turn: held[turn] + got[at] for at, turn in enumerate(keep)}
    share = tile_x // groups
    result = 0.0
    for across_sta in reversed(range(groups)):
        for turn in reversed(list(held)):
            part = lax.dynamic_slice_in_dim(held[turn], (group ^ across_sta) * share, share, 1)
            if across_sta or turn:
                pairs = [
                    (a * pieces + b, (a ^ across_sta) * pieces + (b ^ turn))
                    for a in range(groups)
                    for b in range(pieces)
                ]
                part = lax.ppermute(part, ("sta", "gy"), pairs)
            result = result + part
    return result


def solution(mesh):
    in_specs = (
        P("sta", None, None, "gx", "gy", None),
        P("sta", None, None, "gx", "gy", None),
        P("gx", "gy", None),
        P(),
        P("sta", None, None),
        P("sta", None),
        P(),
        P(),
    )
    out_specs = P(None, ("gx", "sta"), "gy", None)
    return jax.shard_map(local, mesh=mesh, in_specs=in_specs, out_specs=out_specs, check_vma=False)
```

```python
import functools

import jax
import jax.numpy as jnp
from jax import lax
from jax.experimental import pallas as pl
from jax.experimental.pallas import tpu as pltpu
from jax.sharding import PartitionSpec as P

NEAR = 8.0
UNIT = 12.0
SUBLANES = 8
TIME_STEP = 0.25
AMPLITUDE = 4.0
KERNEL_SCALE = 0.0625
STIFFNESS = 0.3
REACH = 2
DEEP = 2 * REACH
ALONG_X = (0, 3, 4)
NEAR_ROWS = 1
PACKED = DEEP + NEAR_ROWS

VMEM = pl.BlockSpec(memory_space=pltpu.VMEM)
SMEM = pl.BlockSpec(memory_space=pltpu.SMEM)
F32, BF16 = jnp.float32, jnp.bfloat16


def call(body, outs, ins, scratch=(), flops=8_000_000_000):
    scalars, arrays = ins
    return list(pl.pallas_call(
        body,
        out_shape=[jax.ShapeDtypeStruct(shape, kind) for shape, kind in outs],
        in_specs=[SMEM] * len(scalars) + [VMEM] * len(arrays),
        out_specs=[VMEM] * len(outs),
        scratch_shapes=list(scratch),
        compiler_params=pltpu.CompilerParams(vmem_limit_bytes=6 * 1024 * 1024),
        cost_estimate=pl.CostEstimate(flops=flops, bytes_accessed=2_000_000, transcendentals=0),
    )(*scalars, *arrays))


def band(depth):
    row = lax.broadcasted_iota(jnp.int32, (depth, depth), 0)
    step = row - lax.broadcasted_iota(jnp.int32, (depth, depth), 1)
    parts = jnp.where(step == 1, NEAR, 0.0) - jnp.where(step == -1, NEAR, 0.0)
    parts = parts - jnp.where(step == 2, 1.0, 0.0) + jnp.where(step == -2, 1.0, 0.0)
    parts = parts.astype(BF16)
    return jnp.concatenate([parts, parts], 0)


def along_depth(rows):
    stacked = jnp.concatenate(rows, 0)
    high = stacked.astype(BF16)
    low = (stacked - high.astype(F32)).astype(BF16)
    split = jnp.concatenate([high, low], 1)
    result = jnp.dot(split, band(stacked.shape[1]), preferred_element_type=F32)
    size = rows[0].shape[0]
    return [result[at * size : (at + 1) * size] for at in range(len(rows))]


def along_y(row):
    count = row.shape[0] // SUBLANES
    at = lax.broadcasted_iota(jnp.int32, (SUBLANES, row.shape[1]), 0)
    planes = [row[SUBLANES * p : SUBLANES * (p + 1)] for p in range(count)]
    before = [jnp.where(at > 0, pltpu.roll(plane, 1, 0), 0.0) for plane in planes[-2:]]
    after = [jnp.where(at < SUBLANES - 1, pltpu.roll(plane, SUBLANES - 1, 0), 0.0) for plane in planes[:2]]
    spread = before + planes + after

    def shifted(by):
        return jnp.concatenate(spread[2 + by : 2 + by + count], 0)

    return shifted(1) - shifted(-1), shifted(2) - shifted(-2)


def across(rows, out, side):
    near, far = rows(out + 1) - rows(out - 1), rows(out + 2) - rows(out - 2)
    return (-near, -far) if side else (near, far)


def across_and_along(rows, out, side, row):
    near_y, far_y = along_y(row)
    near, far = rows(out + 1) - rows(out - 1), rows(out + 2) - rows(out - 2)
    if side:
        return NEAR * (near_y - near) - (far_y - far)
    return NEAR * (near_y + near) - (far_y + far)


def derivative(pair):
    return NEAR * pair[0] - pair[1]


MIRRORED_VEL = (0,)
MIRRORED_STRESS = (3, 4)


def position():
    slab, me = lax.axis_index("gx"), lax.axis_index("gy")
    return slab, me, (slab + me) % 2


def sign_of(flip):
    return 1.0 - 2.0 * flip.astype(F32)


def row_of(flip, side, out, tile_x):
    x = tile_x // 2 - 1 - out if side else tile_x // 2 + out
    return x + flip * (tile_x - 1 - 2 * x)


def interleave(me, tiles, comp, row, held):
    tile_y = tiles[0].shape[2]
    for turn, tile in enumerate(tiles):
        held[pl.ds(pl.multiple_of((me ^ turn) * tile_y, tile_y), tile_y), :] = tile[comp, row]
    count = held.shape[0] // SUBLANES
    return jnp.concatenate([held[pl.ds(p, SUBLANES, stride=count), :] for p in range(count)], 0)


def assemble(*refs):
    count = len(refs) - 11
    tiles, sides, held = refs[:count], (refs[count : count + 5], refs[count + 5 : -1]), refs[-1]
    tile_x = tiles[0].shape[1]
    _, me, flip = position()
    sign = sign_of(flip)
    face_comps = tuple(3 + comp for comp in ALONG_X) + (9,)
    for side, (vel, middle, edge, cells, face) in enumerate(sides):
        for out in range(DEEP):
            row = row_of(flip, side, out, tile_x)
            part, at = (middle, out) if out < REACH else (edge, out - REACH)
            for comp in range(10):
                value = interleave(me, tiles, comp, row, held.at[(out * 10 + comp) % held.shape[0]])
                if comp in MIRRORED_VEL or comp - 3 in MIRRORED_STRESS:
                    value = sign * value
                if comp < 3:
                    vel[comp, out] = value
                elif comp < 9:
                    part[comp - 3, at] = value
                else:
                    cells[out] = value
                if out >= REACH and comp in face_comps:
                    face[face_comps.index(comp), out - REACH] = value


def push(side, spots, amount, stress_row, vel, light, vel_out, sent):
    rows = [functools.partial(stress_row, comp) for comp in range(6)]
    deep = along_depth([rows[comp](out) for out in range(DEEP) for comp in (4, 5, 2)])
    for out in range(DEEP):
        force_x = across_and_along(rows[0], out, side, rows[3](out)) + deep[3 * out]
        force_y = across_and_along(rows[3], out, side, rows[1](out)) + deep[3 * out + 1]
        force_z = across_and_along(rows[4], out, side, rows[5](out)) + deep[3 * out + 2]
        force_z = force_z + amount * spots[out]
        near = DEEP - 1 - out
        for comp, force in enumerate((force_x, force_y, force_z)):
            fresh = vel[comp, out] + light[out] * force
            vel_out[comp, out] = fresh
            if comp in MIRRORED_VEL:
                fresh = -fresh
            high = fresh.astype(BF16)
            if near < NEAR_ROWS:
                sent[comp * PACKED + 2 * near] = high
                sent[comp * PACKED + 2 * near + 1] = (fresh - high.astype(F32)).astype(BF16)
            else:
                sent[comp * PACKED + NEAR_ROWS + near] = high


def from_halo(halo, comp, near):
    if near < NEAR_ROWS:
        at = comp * PACKED + 2 * near
        return halo[at].astype(F32) + halo[at + 1].astype(F32)
    return halo[comp * PACKED + NEAR_ROWS + near].astype(F32)


def first(side, table, residual, rec_cell, vel, middle, other, edge, cells, halo, *outs):
    vel_out, sent, light, lame, shear, halo_out, spots, amounts = outs
    size_y, depth = vel.shape[2:]
    planes = size_y // SUBLANES
    slab, me, flip = position()
    cell = rec_cell[0, me]
    spot_x, spot_y = cell // size_y - slab * (2 * DEEP), cell % size_y
    spot_x = spot_x + flip * (2 * DEEP - 1 - 2 * spot_x)
    spot_y = (spot_y % planes) * SUBLANES + spot_y // planes
    at_spot = (lax.broadcasted_iota(jnp.int32, (size_y, depth), 0) == spot_y) & (
        lax.broadcasted_iota(jnp.int32, (size_y, depth), 1) == 0
    )
    for out in range(DEEP):
        here = spot_x == (DEEP - 1 - out if side else DEEP + out)
        spots[out] = jnp.where(at_spot, jnp.where(here, UNIT * AMPLITUDE, 0.0), 0.0)
    for moment in range(residual.shape[2]):
        amounts[moment] = jnp.full((size_y, depth), residual[0, me, moment], F32)
    _, inside = partner(slab, me, lax.axis_size("gx"), side)
    count = table.shape[0]
    for out in range(DEEP + REACH):
        if out < DEEP:
            number, share = cells[out], 1.0
        else:
            number = halo[len(ALONG_X), REACH - 1 - (out - DEEP)]
            share = jnp.where(inside, 1.0, 0.0)
        parts = [jnp.full(number.shape, table[0, c], F32) for c in range(3)]
        for m in range(1, count):
            hit = number == float(m)
            parts = [jnp.where(hit, table[m, c], parts[c]) for c in range(3)]
        lame[out] = (TIME_STEP * STIFFNESS / UNIT * share) * parts[1]
        shear[out] = (TIME_STEP * STIFFNESS / UNIT * share) * parts[2]
        if out < DEEP:
            light[out] = (TIME_STEP / UNIT) / parts[0]
    for at in range(len(ALONG_X)):
        for near in range(REACH):
            value = halo[at, REACH - 1 - near]
            halo_out[at, near] = -value if ALONG_X[at] in MIRRORED_STRESS else value
    push(side, spots, amounts[0], stress_rows(middle, other, edge, halo_out), vel, light, vel_out, sent)


def stress_rows(middle, other, edge, halo):
    def row(comp, out):
        if out < 0:
            return other[comp, -1 - out]
        if out < REACH:
            return middle[comp, out]
        if out < DEEP:
            return edge[comp, out - REACH]
        return halo[ALONG_X.index(comp), out - DEEP]

    return row


def strain_rates(vx, vy, vz, side, first_out, last_out, full_out):
    outs = range(first_out, last_out)
    wanted = [(vel, out) for out in outs for vel in (vx, vz)] + [(vy, out) for out in outs if out < full_out]
    deep = along_depth([vel(out) for vel, out in wanted])
    deep = {key: value for key, value in zip(wanted, deep)}
    for out in outs:
        rates = [
            derivative(across(vx, out, side)),
            derivative(along_y(vy(out))),
            deep[vz, out],
            across_and_along(vy, out, side, vx(out)),
            deep[vx, out] + derivative(across(vz, out, side)),
        ]
        if out < full_out:
            rates.append(deep[vy, out] + derivative(along_y(vz(out))))
        yield out, rates


def store(target, at, rates):
    count = rates[0].shape[0] // SUBLANES
    for comp, rate in enumerate(rates):
        for p in range(count):
            spot = pl.ds(p, SUBLANES, stride=count)
            target[comp, at, spot, :] = rate[SUBLANES * p : SUBLANES * (p + 1)]


def renew(rates, lame, shear, before):
    bulk = lame * (rates[0] + rates[1] + rates[2])
    twice = shear + shear
    return {
        comp: old + (bulk + twice * rates[comp] if comp < 3 else shear * rates[comp])
        for comp, old in before.items()
    }


def outer(side, moment, last, vel, halo, edge, *refs):
    if last:
        (rates_out,) = refs
    else:
        old_halo, middle, other, light, lame, shear, spots, amounts, rates_out, edge_out, halo_out, vel_out, sent = refs

    def rows(comp):
        return lambda out: vel[comp, out] if out < DEEP else from_halo(halo, comp, out - DEEP)

    until = DEEP if last else DEEP + REACH
    for out, rates in strain_rates(rows(0), rows(1), rows(2), side, REACH, until, DEEP):
        own = out < DEEP
        if own:
            store(rates_out, out - REACH, rates)
        if last:
            continue
        if own:
            fresh = renew(rates, lame[out], shear[out], {comp: edge[comp, out - REACH] for comp in range(6)})
            for comp, value in fresh.items():
                edge_out[comp, out - REACH] = value
        else:
            before = {comp: old_halo[at, out - DEEP] for at, comp in enumerate(ALONG_X)}
            fresh = renew(rates, lame[out], shear[out], before)
            for at, comp in enumerate(ALONG_X):
                halo_out[at, out - DEEP] = fresh[comp]
    if not last:
        rows = stress_rows(middle, other, edge_out, halo_out)
        push(side, spots, amounts[moment + 1], rows, vel, light, vel_out, sent)


def inner(last, *refs):
    vels = refs[:2]
    if last:
        rates_out = refs[2:]
    else:
        middles, lames, shears = refs[2:4], refs[4:6], refs[6:8]
        rates_out, middles_out = refs[8:10], refs[10:12]
    for side in range(2):

        def rows(comp):
            return lambda out: vels[side][comp, out] if out >= 0 else vels[1 - side][comp, -1 - out]

        for out, rates in strain_rates(rows(0), rows(1), rows(2), side, 0, REACH, REACH):
            store(rates_out[side], out, rates)
            if not last:
                before = {comp: middles[side][comp, out] for comp in range(6)}
                fresh = renew(rates, lames[side][out], shears[side][out], before)
                for comp, value in fresh.items():
                    middles_out[side][comp, out] = value


def correlate(jobs, moments, residual, *refs):
    count = 4 * moments
    rates, sources, before, terms = refs[:count], refs[count : count + len(jobs)], refs[count + len(jobs) : -1], refs[-1]
    tile_x, tile_y = sources[0].shape[2:4]
    _, me, flip = position()
    sign = sign_of(flip)
    for job, turn in enumerate(jobs):
        spot = pl.ds(pl.multiple_of((me ^ turn) * tile_y, tile_y), tile_y)
        for side in range(2):
            for out in range(DEEP):
                row = row_of(flip, side, out, tile_x)
                lam = mu = 0.0
                if before and job < before[0].shape[0]:
                    lam, mu = before[0][job, 0, row], before[0][job, 1, row]
                for moment in jobs[turn]:
                    weight = (KERNEL_SCALE / UNIT) * residual[0, me, moment]
                    held = rates[4 * moment + 2 * (out // REACH) + side]
                    rate = [held[c, out % REACH, spot, :] for c in range(6)]
                    source = [sources[job][moment, c, row] for c in range(6)]
                    bulk = (source[0] + source[1] + source[2]) * (rate[0] + rate[1] + rate[2])
                    diag = source[0] * rate[0] + source[1] * rate[1] + source[2] * rate[2]
                    off = sign * (source[3] * rate[3] + source[4] * rate[4]) + source[5] * rate[5]
                    lam = lam + weight * bulk
                    mu = mu + (2.0 * weight) * (diag + off)
                terms[job, 0, row] = lam
                terms[job, 1, row] = mu


def swap(array, axis, turn):
    count = lax.axis_size(axis)
    return lax.ppermute(array, axis, [(i, i ^ turn) for i in range(count)])


def partner(slab, piece, slabs, side):
    other = slab + 1 - 2 * ((slab + piece + side) % 2)
    return other, (other >= 0) & (other < slabs)


def to_neighbour(face, side):
    slabs, pieces = lax.axis_size("gx"), lax.axis_size("gy")
    pairs = []
    for slab in range(slabs):
        for piece in range(pieces):
            other, inside = partner(slab, piece, slabs, side)
            if inside:
                pairs.append((slab * pieces + piece, other * pieces + piece))
    return lax.ppermute(face, ("gx", "gy"), pairs)


def local(rec_state, source_strain, material, material_table, residual, rec_cell, listed, src_pick):
    state = rec_state[0]
    receivers, _, tile_x, tile_y, depth = state.shape
    pieces, slabs, groups = lax.axis_size("gy"), lax.axis_size("gx"), lax.axis_size("sta")
    assert receivers == pieces and tile_x == 2 * DEEP
    assert pieces & (pieces - 1) == 0 and groups & (groups - 1) == 0
    size_y = pieces * tile_y
    group, me = lax.axis_index("sta"), lax.axis_index("gy")
    moments = residual.shape[2]

    numbers = material.astype(F32)[None]
    order = sorted(range(pieces), reverse=True)
    picked = {turn: lax.dynamic_index_in_dim(state, me ^ turn, 0, keepdims=False) for turn in order}
    own, picked = lax.optimization_barrier((source_strain[0], picked))
    chunks = {turn: jnp.concatenate([picked[turn], numbers], 0) for turn in order}
    chunks = [swap(chunks[turn], "gy", turn) if turn else chunks[turn] for turn in range(pieces)]
    strains = [swap(own, "sta", turn) if turn else own for turn in range(groups)]

    def shape(*lead, kind=F32):
        return lead + (size_y, depth), kind

    vel_shape, pair_shape = shape(3, DEEP), shape(6, REACH)
    halo_shape, sent_shape = shape(3, REACH), shape(3 * PACKED, kind=BF16)

    results = call(
        assemble,
        [vel_shape, pair_shape, pair_shape, shape(DEEP), shape(4, REACH)] * 2,
        ([], chunks),
        [pltpu.VMEM((8, size_y, depth), F32)],
    )
    vels, middles, edges, cells, faces = ([results[at], results[5 + at]] for at in range(5))
    halos = [to_neighbour(faces[side], side) for side in range(2)]

    strains, cells = lax.optimization_barrier((strains, cells))
    weights = lax.dynamic_slice_in_dim(listed, group, 1, 2)[:, :, 0].astype(F32)
    combined = 0.0
    for turn in range(groups):
        factor = jnp.sum(weights * (src_pick == (group ^ turn)).astype(F32), 0)
        combined = combined + factor[:, None, None, None, None] * strains[turn].astype(F32)
    sent, lights, lames, shears, old_halos, spots, amounts = ([None, None] for _ in range(7))
    fresh = [None, None]
    for side in range(2):
        results = call(
            functools.partial(first, side),
            [vel_shape, sent_shape, shape(DEEP), shape(DEEP + REACH), shape(DEEP + REACH), halo_shape]
            + [shape(DEEP), shape(moments)],
            (
                [material_table, residual, rec_cell],
                [vels[side], middles[side], middles[1 - side], edges[side], cells[side], halos[side]],
            ),
        )
        fresh[side], sent[side], lights[side], lames[side], shears[side], old_halos[side] = results[:6]
        spots[side], amounts[side] = results[6:]
        sent[side] = to_neighbour(sent[side], side)
    vels = fresh

    found, rates = {0: combined}, []
    exchanges = {0: [pieces // 2], 1: [w for w in range(1, pieces // 2) if w & (w - 1) == 0]}
    rest = [turn for turn in range(pieces) if turn & (turn - 1)]
    for moment in range(moments):
        last = moment == moments - 1
        results = call(
            functools.partial(inner, last),
            [pair_shape] * (2 if last else 4),
            ([], vels if last else vels + middles + lames + shears),
        )
        rates += results[:2]
        if not last:
            middles = results[2:]
        if moment in exchanges:
            ready, rates[-1] = lax.optimization_barrier((combined, rates[-1]))
            for turn in exchanges[moment]:
                found[turn] = swap(ready, "gy", turn)
        if moment == 3 * moments // 4:
            found, rates[-1] = lax.optimization_barrier((found, rates[-1]))
            for turn in rest:
                low = turn & -turn
                found[turn] = swap(found[turn ^ low], "gy", low)
        if last:
            early, late = [turn for turn in range(pieces) if turn not in rest], rest
            jobs = {turn: list(range(moment)) for turn in early}
            (terms,) = call(
                functools.partial(correlate, jobs, moment),
                [((len(jobs), 2, tile_x, tile_y, depth), F32)],
                ([residual], rates[: 4 * moment] + [found[turn] for turn in jobs]),
            )
            terms, vels = lax.optimization_barrier((terms, vels))
        fresh = [None, None]
        for side in range(2):
            arrays = [vels[side], sent[side], edges[side]]
            outs = [pair_shape]
            if not last:
                arrays += [old_halos[side], middles[side], middles[1 - side]]
                arrays += [lights[side], lames[side], shears[side], spots[side], amounts[side]]
                outs += [pair_shape, halo_shape, vel_shape, sent_shape]
            results = call(functools.partial(outer, side, moment, last), outs, ([], arrays))
            rates.append(results[0])
            if not last:
                edges[side], old_halos[side], fresh[side] = results[1:4]
                sent[side] = to_neighbour(results[4], side)
        vels = fresh

    jobs = {turn: [moments - 1] if turn in early else list(range(moments)) for turn in early + late}
    (terms,) = call(
        functools.partial(correlate, jobs, moments),
        [((pieces, 2, tile_x, tile_y, depth), F32)],
        ([residual], rates + [found[turn] for turn in jobs] + [terms]),
    )
    held = {turn: terms[at] for at, turn in enumerate(jobs)}
    if pieces > 1:
        keep = [turn for turn in held if not turn & 1]
        got = swap(jnp.stack([held[turn ^ 1] for turn in keep]), "gy", 1)
        held = {turn: held[turn] + got[at] for at, turn in enumerate(keep)}
    share = tile_x // groups
    result = 0.0
    for across_sta in reversed(range(groups)):
        for turn in reversed(list(held)):
            part = lax.dynamic_slice_in_dim(held[turn], (group ^ across_sta) * share, share, 1)
            if across_sta or turn:
                pairs = [
                    (a * pieces + b, (a ^ across_sta) * pieces + (b ^ turn))
                    for a in range(groups)
                    for b in range(pieces)
                ]
                part = lax.ppermute(part, ("sta", "gy"), pairs)
            result = result + part
    return result


def solution(mesh):
    in_specs = (
        P("sta", None, None, "gx", "gy", None),
        P("sta", None, None, "gx", "gy", None),
        P("gx", "gy", None),
        P(),
        P("sta", None, None),
        P("sta", None),
        P(),
        P(),
    )
    out_specs = P(None, ("gx", "sta"), "gy", None)
    return jax.shard_map(local, mesh=mesh, in_specs=in_specs, out_specs=out_specs, check_vma=False)
```

```python
import functools

import jax
import jax.numpy as jnp
from jax import lax
from jax.experimental import pallas as pl
from jax.experimental.pallas import tpu as pltpu
from jax.sharding import PartitionSpec as P

NEAR = 8.0
UNIT = 12.0
SUBLANES = 8
TIME_STEP = 0.25
AMPLITUDE = 4.0
KERNEL_SCALE = 0.0625
STIFFNESS = 0.3
REACH = 2
DEEP = 2 * REACH
ALONG_X = (0, 3, 4)
NEAR_ROWS = 1
PACKED = DEEP + NEAR_ROWS

VMEM = pl.BlockSpec(memory_space=pltpu.VMEM)
SMEM = pl.BlockSpec(memory_space=pltpu.SMEM)
F32, BF16 = jnp.float32, jnp.bfloat16


def call(body, outs, ins, scratch=(), flops=8_000_000_000):
    scalars, arrays = ins
    return list(pl.pallas_call(
        body,
        out_shape=[jax.ShapeDtypeStruct(shape, kind) for shape, kind in outs],
        in_specs=[SMEM] * len(scalars) + [VMEM] * len(arrays),
        out_specs=[VMEM] * len(outs),
        scratch_shapes=list(scratch),
        compiler_params=pltpu.CompilerParams(vmem_limit_bytes=6 * 1024 * 1024),
        cost_estimate=pl.CostEstimate(flops=flops, bytes_accessed=2_000_000, transcendentals=0),
    )(*scalars, *arrays))


def band(depth):
    row = lax.broadcasted_iota(jnp.int32, (depth, depth), 0)
    step = row - lax.broadcasted_iota(jnp.int32, (depth, depth), 1)
    parts = jnp.where(step == 1, NEAR, 0.0) - jnp.where(step == -1, NEAR, 0.0)
    parts = parts - jnp.where(step == 2, 1.0, 0.0) + jnp.where(step == -2, 1.0, 0.0)
    parts = parts.astype(BF16)
    return jnp.concatenate([parts, parts], 0)


def along_depth(rows):
    stacked = jnp.concatenate(rows, 0)
    high = stacked.astype(BF16)
    low = (stacked - high.astype(F32)).astype(BF16)
    split = jnp.concatenate([high, low], 1)
    result = jnp.dot(split, band(stacked.shape[1]), preferred_element_type=F32)
    size = rows[0].shape[0]
    return [result[at * size : (at + 1) * size] for at in range(len(rows))]


def along_y(row):
    count = row.shape[0] // SUBLANES
    at = lax.broadcasted_iota(jnp.int32, (SUBLANES, row.shape[1]), 0)
    planes = [row[SUBLANES * p : SUBLANES * (p + 1)] for p in range(count)]
    before = [jnp.where(at > 0, pltpu.roll(plane, 1, 0), 0.0) for plane in planes[-2:]]
    after = [jnp.where(at < SUBLANES - 1, pltpu.roll(plane, SUBLANES - 1, 0), 0.0) for plane in planes[:2]]
    spread = before + planes + after

    def shifted(by):
        return jnp.concatenate(spread[2 + by : 2 + by + count], 0)

    return shifted(1) - shifted(-1), shifted(2) - shifted(-2)


def across(rows, out, side):
    near, far = rows(out + 1) - rows(out - 1), rows(out + 2) - rows(out - 2)
    return (-near, -far) if side else (near, far)


def across_and_along(rows, out, side, row):
    near_y, far_y = along_y(row)
    near, far = rows(out + 1) - rows(out - 1), rows(out + 2) - rows(out - 2)
    if side:
        return NEAR * (near_y - near) - (far_y - far)
    return NEAR * (near_y + near) - (far_y + far)


def derivative(pair):
    return NEAR * pair[0] - pair[1]


MIRRORED_VEL = (0,)
MIRRORED_STRESS = (3, 4)


def position():
    slab, me = lax.axis_index("gx"), lax.axis_index("gy")
    return slab, me, (slab + me) % 2


def sign_of(flip):
    return 1.0 - 2.0 * flip.astype(F32)


def row_of(flip, side, out, tile_x):
    x = tile_x // 2 - 1 - out if side else tile_x // 2 + out
    return x + flip * (tile_x - 1 - 2 * x)


def interleave(me, tiles, comp, row, held):
    tile_y = tiles[0].shape[2]
    for turn, tile in enumerate(tiles):
        held[pl.ds(pl.multiple_of((me ^ turn) * tile_y, tile_y), tile_y), :] = tile[comp, row]
    count = held.shape[0] // SUBLANES
    return jnp.concatenate([held[pl.ds(p, SUBLANES, stride=count), :] for p in range(count)], 0)


def assemble(*refs):
    count = len(refs) - 11
    tiles, sides, held = refs[:count], (refs[count : count + 5], refs[count + 5 : -1]), refs[-1]
    tile_x = tiles[0].shape[1]
    _, me, flip = position()
    sign = sign_of(flip)
    face_comps = tuple(3 + comp for comp in ALONG_X) + (9,)
    for side, (vel, middle, edge, cells, face) in enumerate(sides):
        for out in range(DEEP):
            row = row_of(flip, side, out, tile_x)
            part, at = (middle, out) if out < REACH else (edge, out - REACH)
            for comp in range(10):
                value = interleave(me, tiles, comp, row, held.at[(out * 10 + comp) % held.shape[0]])
                if comp in MIRRORED_VEL or comp - 3 in MIRRORED_STRESS:
                    value = sign * value
                if comp < 3:
                    vel[comp, out] = value
                elif comp < 9:
                    part[comp - 3, at] = value
                else:
                    cells[out] = value
                if out >= REACH and comp in face_comps:
                    face[face_comps.index(comp), out - REACH] = value


def push(side, spots, amount, stress_row, vel, light, vel_out, sent):
    rows = [functools.partial(stress_row, comp) for comp in range(6)]
    deep = along_depth([rows[comp](out) for out in range(DEEP) for comp in (4, 5, 2)])
    for out in range(DEEP):
        force_x = across_and_along(rows[0], out, side, rows[3](out)) + deep[3 * out]
        force_y = across_and_along(rows[3], out, side, rows[1](out)) + deep[3 * out + 1]
        force_z = across_and_along(rows[4], out, side, rows[5](out)) + deep[3 * out + 2]
        force_z = force_z + amount * spots[out]
        near = DEEP - 1 - out
        for comp, force in enumerate((force_x, force_y, force_z)):
            fresh = vel[comp, out] + light[out] * force
            vel_out[comp, out] = fresh
            if comp in MIRRORED_VEL:
                fresh = -fresh
            high = fresh.astype(BF16)
            if near < NEAR_ROWS:
                sent[comp * PACKED + 2 * near] = high
                sent[comp * PACKED + 2 * near + 1] = (fresh - high.astype(F32)).astype(BF16)
            else:
                sent[comp * PACKED + NEAR_ROWS + near] = high


def from_halo(halo, comp, near):
    if near < NEAR_ROWS:
        at = comp * PACKED + 2 * near
        return halo[at].astype(F32) + halo[at + 1].astype(F32)
    return halo[comp * PACKED + NEAR_ROWS + near].astype(F32)


def first(side, table, residual, rec_cell, vel, middle, other, edge, cells, halo, *outs):
    vel_out, sent, light, lame, shear, halo_out, spots, amounts = outs
    size_y, depth = vel.shape[2:]
    planes = size_y // SUBLANES
    slab, me, flip = position()
    cell = rec_cell[0, me]
    spot_x, spot_y = cell // size_y - slab * (2 * DEEP), cell % size_y
    spot_x = spot_x + flip * (2 * DEEP - 1 - 2 * spot_x)
    spot_y = (spot_y % planes) * SUBLANES + spot_y // planes
    at_spot = (lax.broadcasted_iota(jnp.int32, (size_y, depth), 0) == spot_y) & (
        lax.broadcasted_iota(jnp.int32, (size_y, depth), 1) == 0
    )
    for out in range(DEEP):
        here = spot_x == (DEEP - 1 - out if side else DEEP + out)
        spots[out] = jnp.where(at_spot, jnp.where(here, UNIT * AMPLITUDE, 0.0), 0.0)
    for moment in range(residual.shape[2]):
        amounts[moment] = jnp.full((size_y, depth), residual[0, me, moment], F32)
    _, inside = partner(slab, me, lax.axis_size("gx"), side)
    count = table.shape[0]
    for out in range(DEEP + REACH):
        if out < DEEP:
            number, share = cells[out], 1.0
        else:
            number = halo[len(ALONG_X), REACH - 1 - (out - DEEP)]
            share = jnp.where(inside, 1.0, 0.0)
        parts = [jnp.full(number.shape, table[0, c], F32) for c in range(3)]
        for m in range(1, count):
            hit = number == float(m)
            parts = [jnp.where(hit, table[m, c], parts[c]) for c in range(3)]
        lame[out] = (TIME_STEP * STIFFNESS / UNIT * share) * parts[1]
        shear[out] = (TIME_STEP * STIFFNESS / UNIT * share) * parts[2]
        if out < DEEP:
            light[out] = (TIME_STEP / UNIT) / parts[0]
    for at in range(len(ALONG_X)):
        for near in range(REACH):
            value = halo[at, REACH - 1 - near]
            halo_out[at, near] = -value if ALONG_X[at] in MIRRORED_STRESS else value
    push(side, spots, amounts[0], stress_rows(middle, other, edge, halo_out), vel, light, vel_out, sent)


def stress_rows(middle, other, edge, halo):
    def row(comp, out):
        if out < 0:
            return other[comp, -1 - out]
        if out < REACH:
            return middle[comp, out]
        if out < DEEP:
            return edge[comp, out - REACH]
        return halo[ALONG_X.index(comp), out - DEEP]

    return row


def strain_rates(vx, vy, vz, side, first_out, last_out, full_out):
    outs = range(first_out, last_out)
    wanted = [(vel, out) for out in outs for vel in (vx, vz)] + [(vy, out) for out in outs if out < full_out]
    deep = along_depth([vel(out) for vel, out in wanted])
    deep = {key: value for key, value in zip(wanted, deep)}
    for out in outs:
        rates = [
            derivative(across(vx, out, side)),
            derivative(along_y(vy(out))),
            deep[vz, out],
            across_and_along(vy, out, side, vx(out)),
            deep[vx, out] + derivative(across(vz, out, side)),
        ]
        if out < full_out:
            rates.append(deep[vy, out] + derivative(along_y(vz(out))))
        yield out, rates


def store(target, at, rates):
    count = rates[0].shape[0] // SUBLANES
    for comp, rate in enumerate(rates):
        for p in range(count):
            spot = pl.ds(p, SUBLANES, stride=count)
            target[comp, at, spot, :] = rate[SUBLANES * p : SUBLANES * (p + 1)]


def renew(rates, lame, shear, before):
    bulk = lame * (rates[0] + rates[1] + rates[2])
    twice = shear + shear
    return {
        comp: old + (bulk + twice * rates[comp] if comp < 3 else shear * rates[comp])
        for comp, old in before.items()
    }


def outer(side, moment, last, vel, halo, edge, *refs):
    if last:
        (rates_out,) = refs
    else:
        old_halo, middle, other, light, lame, shear, spots, amounts, rates_out, edge_out, halo_out, vel_out, sent = refs

    def rows(comp):
        return lambda out: vel[comp, out] if out < DEEP else from_halo(halo, comp, out - DEEP)

    until = DEEP if last else DEEP + REACH
    for out, rates in strain_rates(rows(0), rows(1), rows(2), side, REACH, until, DEEP):
        own = out < DEEP
        if own:
            store(rates_out, out - REACH, rates)
        if last:
            continue
        if own:
            fresh = renew(rates, lame[out], shear[out], {comp: edge[comp, out - REACH] for comp in range(6)})
            for comp, value in fresh.items():
                edge_out[comp, out - REACH] = value
        else:
            before = {comp: old_halo[at, out - DEEP] for at, comp in enumerate(ALONG_X)}
            fresh = renew(rates, lame[out], shear[out], before)
            for at, comp in enumerate(ALONG_X):
                halo_out[at, out - DEEP] = fresh[comp]
    if not last:
        rows = stress_rows(middle, other, edge_out, halo_out)
        push(side, spots, amounts[moment + 1], rows, vel, light, vel_out, sent)


def inner(last, *refs):
    vels = refs[:2]
    if last:
        rates_out = refs[2:]
    else:
        middles, lames, shears = refs[2:4], refs[4:6], refs[6:8]
        rates_out, middles_out = refs[8:10], refs[10:12]
    for side in range(2):

        def rows(comp):
            return lambda out: vels[side][comp, out] if out >= 0 else vels[1 - side][comp, -1 - out]

        for out, rates in strain_rates(rows(0), rows(1), rows(2), side, 0, REACH, REACH):
            store(rates_out[side], out, rates)
            if not last:
                before = {comp: middles[side][comp, out] for comp in range(6)}
                fresh = renew(rates, lames[side][out], shears[side][out], before)
                for comp, value in fresh.items():
                    middles_out[side][comp, out] = value


def correlate(jobs, moments, residual, *refs):
    count = 4 * moments
    rates, sources, before, terms = refs[:count], refs[count : count + len(jobs)], refs[count + len(jobs) : -1], refs[-1]
    tile_x, tile_y = sources[0].shape[2:4]
    _, me, flip = position()
    sign = sign_of(flip)
    for job, turn in enumerate(jobs):
        spot = pl.ds(pl.multiple_of((me ^ turn) * tile_y, tile_y), tile_y)
        for side in range(2):
            for out in range(DEEP):
                row = row_of(flip, side, out, tile_x)
                lam = mu = 0.0
                if before and job < before[0].shape[0]:
                    lam, mu = before[0][job, 0, row], before[0][job, 1, row]
                for moment in jobs[turn]:
                    weight = (KERNEL_SCALE / UNIT) * residual[0, me, moment]
                    held = rates[4 * moment + 2 * (out // REACH) + side]
                    rate = [held[c, out % REACH, spot, :] for c in range(6)]
                    source = [sources[job][moment, c, row] for c in range(6)]
                    bulk = (source[0] + source[1] + source[2]) * (rate[0] + rate[1] + rate[2])
                    diag = source[0] * rate[0] + source[1] * rate[1] + source[2] * rate[2]
                    off = sign * (source[3] * rate[3] + source[4] * rate[4]) + source[5] * rate[5]
                    lam = lam + weight * bulk
                    mu = mu + (2.0 * weight) * (diag + off)
                terms[job, 0, row] = lam
                terms[job, 1, row] = mu


def combine(groups, listed, src_pick, *refs):
    strains, out = refs[:groups], refs[groups]
    group = lax.axis_index("sta")
    moments, comps = out.shape[:2]
    for moment in range(moments):
        factors = []
        for turn in range(groups):
            factor = 0
            for at in range(src_pick.shape[0]):
                factor += jnp.where(src_pick[at, moment] == (group ^ turn), listed[at, moment, group], 0)
            factors.append(factor.astype(F32))
        for comp in range(comps):
            total = 0.0
            for factor, strain in zip(factors, strains):
                total = total + factor * strain[moment, comp].astype(F32)
            out[moment, comp] = total


def swap(array, axis, turn):
    count = lax.axis_size(axis)
    return lax.ppermute(array, axis, [(i, i ^ turn) for i in range(count)])


def partner(slab, piece, slabs, side):
    other = slab + 1 - 2 * ((slab + piece + side) % 2)
    return other, (other >= 0) & (other < slabs)


def to_neighbour(face, side):
    slabs, pieces = lax.axis_size("gx"), lax.axis_size("gy")
    pairs = []
    for slab in range(slabs):
        for piece in range(pieces):
            other, inside = partner(slab, piece, slabs, side)
            if inside:
                pairs.append((slab * pieces + piece, other * pieces + piece))
    return lax.ppermute(face, ("gx", "gy"), pairs)


def local(rec_state, source_strain, material, material_table, residual, rec_cell, listed, src_pick):
    state = rec_state[0]
    receivers, _, tile_x, tile_y, depth = state.shape
    pieces, slabs, groups = lax.axis_size("gy"), lax.axis_size("gx"), lax.axis_size("sta")
    assert receivers == pieces and tile_x == 2 * DEEP
    assert pieces & (pieces - 1) == 0 and groups & (groups - 1) == 0
    size_y = pieces * tile_y
    group, me = lax.axis_index("sta"), lax.axis_index("gy")
    moments = residual.shape[2]

    numbers = material.astype(F32)[None]
    order = sorted(range(pieces), reverse=True)
    picked = {turn: lax.dynamic_index_in_dim(state, me ^ turn, 0, keepdims=False) for turn in order}
    own = source_strain[0].reshape(source_strain.shape[1:3] + (tile_x * tile_y, depth))
    own, picked = lax.optimization_barrier((own, picked))
    chunks = {turn: jnp.concatenate([picked[turn], numbers], 0) for turn in order}
    chunks = [swap(chunks[turn], "gy", turn) if turn else chunks[turn] for turn in range(pieces)]
    strains = [swap(own, "sta", turn) if turn else own for turn in range(groups)]

    def shape(*lead, kind=F32):
        return lead + (size_y, depth), kind

    vel_shape, pair_shape = shape(3, DEEP), shape(6, REACH)
    halo_shape, sent_shape = shape(3, REACH), shape(3 * PACKED, kind=BF16)

    results = call(
        assemble,
        [vel_shape, pair_shape, pair_shape, shape(DEEP), shape(4, REACH)] * 2,
        ([], chunks),
        [pltpu.VMEM((8, size_y, depth), F32)],
    )
    vels, middles, edges, cells, faces = ([results[at], results[5 + at]] for at in range(5))
    halos = [to_neighbour(faces[side], side) for side in range(2)]

    strains, cells = lax.optimization_barrier((strains, cells))
    (combined,) = call(
        functools.partial(combine, groups), [(own.shape, F32)], ([listed, src_pick], strains)
    )
    combined = combined.reshape(own.shape[:2] + (tile_x, tile_y, depth))
    sent, lights, lames, shears, old_halos, spots, amounts = ([None, None] for _ in range(7))
    fresh = [None, None]
    for side in range(2):
        results = call(
            functools.partial(first, side),
            [vel_shape, sent_shape, shape(DEEP), shape(DEEP + REACH), shape(DEEP + REACH), halo_shape]
            + [shape(DEEP), shape(moments)],
            (
                [material_table, residual, rec_cell],
                [vels[side], middles[side], middles[1 - side], edges[side], cells[side], halos[side]],
            ),
        )
        fresh[side], sent[side], lights[side], lames[side], shears[side], old_halos[side] = results[:6]
        spots[side], amounts[side] = results[6:]
        sent[side] = to_neighbour(sent[side], side)
    vels = fresh

    found, rates = {0: combined}, []
    exchanges = {0: [pieces // 2], 1: [w for w in range(1, pieces // 2) if w & (w - 1) == 0]}
    rest = [turn for turn in range(pieces) if turn & (turn - 1)]
    for moment in range(moments):
        last = moment == moments - 1
        if last:
            found, vels = lax.optimization_barrier((found, vels))
        results = call(
            functools.partial(inner, last),
            [pair_shape] * (2 if last else 4),
            ([], vels if last else vels + middles + lames + shears),
        )
        rates += results[:2]
        if not last:
            middles = results[2:]
        if moment in exchanges:
            ready, rates[-1] = lax.optimization_barrier((combined, rates[-1]))
            for turn in exchanges[moment]:
                found[turn] = swap(ready, "gy", turn)
        if moment == 5 * moments // 8:
            found, rates[-1] = lax.optimization_barrier((found, rates[-1]))
            for turn in rest:
                low = turn & -turn
                found[turn] = swap(found[turn ^ low], "gy", low)
        if last:
            early, late = list(range(pieces)), []
            jobs = {turn: list(range(moment)) for turn in early}
            (terms,) = call(
                functools.partial(correlate, jobs, moment),
                [((len(jobs), 2, tile_x, tile_y, depth), F32)],
                ([residual], rates[: 4 * moment] + [found[turn] for turn in jobs]),
            )
            terms, vels = lax.optimization_barrier((terms, vels))
        fresh = [None, None]
        for side in range(2):
            arrays = [vels[side], sent[side], edges[side]]
            outs = [pair_shape]
            if not last:
                arrays += [old_halos[side], middles[side], middles[1 - side]]
                arrays += [lights[side], lames[side], shears[side], spots[side], amounts[side]]
                outs += [pair_shape, halo_shape, vel_shape, sent_shape]
            results = call(functools.partial(outer, side, moment, last), outs, ([], arrays))
            rates.append(results[0])
            if not last:
                edges[side], old_halos[side], fresh[side] = results[1:4]
                sent[side] = to_neighbour(results[4], side)
        vels = fresh

    jobs = {turn: [moments - 1] if turn in early else list(range(moments)) for turn in early + late}
    (terms,) = call(
        functools.partial(correlate, jobs, moments),
        [((pieces, 2, tile_x, tile_y, depth), F32)],
        ([residual], rates + [found[turn] for turn in jobs] + [terms]),
    )
    held = {turn: terms[at] for at, turn in enumerate(jobs)}
    if pieces > 1:
        keep = [turn for turn in held if not turn & 1]
        got = swap(jnp.stack([held[turn ^ 1] for turn in keep]), "gy", 1)
        held = {turn: held[turn] + got[at] for at, turn in enumerate(keep)}
    share = tile_x // groups
    result = 0.0
    for across_sta in reversed(range(groups)):
        for turn in reversed(list(held)):
            part = lax.dynamic_slice_in_dim(held[turn], (group ^ across_sta) * share, share, 1)
            if across_sta or turn:
                pairs = [
                    (a * pieces + b, (a ^ across_sta) * pieces + (b ^ turn))
                    for a in range(groups)
                    for b in range(pieces)
                ]
                part = lax.ppermute(part, ("sta", "gy"), pairs)
            result = result + part
    return result


def solution(mesh):
    in_specs = (
        P("sta", None, None, "gx", "gy", None),
        P("sta", None, None, "gx", "gy", None),
        P("gx", "gy", None),
        P(),
        P("sta", None, None),
        P("sta", None),
        P(),
        P(),
    )
    out_specs = P(None, ("gx", "sta"), "gy", None)
    return jax.shard_map(local, mesh=mesh, in_specs=in_specs, out_specs=out_specs, check_vma=False)
```

```python
import functools

import jax
import jax.numpy as jnp
from jax import lax
from jax.experimental import pallas as pl
from jax.experimental.pallas import tpu as pltpu
from jax.sharding import PartitionSpec as P

NEAR = 8.0
UNIT = 12.0
SUBLANES = 8
TIME_STEP = 0.25
AMPLITUDE = 4.0
KERNEL_SCALE = 0.0625
STIFFNESS = 0.3
REACH = 2
DEEP = 2 * REACH
ALONG_X = (0, 3, 4)
NEAR_ROWS = 1
PACKED = DEEP + NEAR_ROWS

VMEM = pl.BlockSpec(memory_space=pltpu.VMEM)
SMEM = pl.BlockSpec(memory_space=pltpu.SMEM)
F32, BF16 = jnp.float32, jnp.bfloat16


def call(body, outs, ins, scratch=(), flops=8_000_000_000):
    scalars, arrays = ins
    return list(pl.pallas_call(
        body,
        out_shape=[jax.ShapeDtypeStruct(shape, kind) for shape, kind in outs],
        in_specs=[SMEM] * len(scalars) + [VMEM] * len(arrays),
        out_specs=[VMEM] * len(outs),
        scratch_shapes=list(scratch),
        compiler_params=pltpu.CompilerParams(vmem_limit_bytes=6 * 1024 * 1024),
        cost_estimate=pl.CostEstimate(flops=flops, bytes_accessed=2_000_000, transcendentals=0),
    )(*scalars, *arrays))


def band(depth):
    row = lax.broadcasted_iota(jnp.int32, (depth, depth), 0)
    step = row - lax.broadcasted_iota(jnp.int32, (depth, depth), 1)
    parts = jnp.where(step == 1, NEAR, 0.0) - jnp.where(step == -1, NEAR, 0.0)
    parts = parts - jnp.where(step == 2, 1.0, 0.0) + jnp.where(step == -2, 1.0, 0.0)
    parts = parts.astype(BF16)
    return jnp.concatenate([parts, parts], 0)


def along_depth(rows):
    stacked = jnp.concatenate(rows, 0)
    high = stacked.astype(BF16)
    low = (stacked - high.astype(F32)).astype(BF16)
    split = jnp.concatenate([high, low], 1)
    result = jnp.dot(split, band(stacked.shape[1]), preferred_element_type=F32)
    size = rows[0].shape[0]
    return [result[at * size : (at + 1) * size] for at in range(len(rows))]


def along_y(row):
    count = row.shape[0] // SUBLANES
    at = lax.broadcasted_iota(jnp.int32, (SUBLANES, row.shape[1]), 0)
    planes = [row[SUBLANES * p : SUBLANES * (p + 1)] for p in range(count)]
    before = [jnp.where(at > 0, pltpu.roll(plane, 1, 0), 0.0) for plane in planes[-2:]]
    after = [jnp.where(at < SUBLANES - 1, pltpu.roll(plane, SUBLANES - 1, 0), 0.0) for plane in planes[:2]]
    spread = before + planes + after

    def shifted(by):
        return jnp.concatenate(spread[2 + by : 2 + by + count], 0)

    return shifted(1) - shifted(-1), shifted(2) - shifted(-2)


def across(rows, out, side):
    near, far = rows(out + 1) - rows(out - 1), rows(out + 2) - rows(out - 2)
    return (-near, -far) if side else (near, far)


def across_and_along(rows, out, side, row):
    near_y, far_y = along_y(row)
    near, far = rows(out + 1) - rows(out - 1), rows(out + 2) - rows(out - 2)
    if side:
        return NEAR * (near_y - near) - (far_y - far)
    return NEAR * (near_y + near) - (far_y + far)


def derivative(pair):
    return NEAR * pair[0] - pair[1]


MIRRORED_VEL = (0,)
MIRRORED_STRESS = (3, 4)


def position():
    slab, me = lax.axis_index("gx"), lax.axis_index("gy")
    return slab, me, (slab + me) % 2


def sign_of(flip):
    return 1.0 - 2.0 * flip.astype(F32)


def row_of(flip, side, out, tile_x):
    x = tile_x // 2 - 1 - out if side else tile_x // 2 + out
    return x + flip * (tile_x - 1 - 2 * x)


def interleave(me, tiles, comp, row, held):
    tile_y = tiles[0].shape[2]
    for turn, tile in enumerate(tiles):
        held[pl.ds(pl.multiple_of((me ^ turn) * tile_y, tile_y), tile_y), :] = tile[comp, row]
    count = held.shape[0] // SUBLANES
    return jnp.concatenate([held[pl.ds(p, SUBLANES, stride=count), :] for p in range(count)], 0)


def assemble(*refs):
    count = len(refs) - 11
    tiles, sides, held = refs[:count], (refs[count : count + 5], refs[count + 5 : -1]), refs[-1]
    tile_x = tiles[0].shape[1]
    _, me, flip = position()
    sign = sign_of(flip)
    face_comps = tuple(3 + comp for comp in ALONG_X) + (9,)
    for side, (vel, middle, edge, cells, face) in enumerate(sides):
        for out in range(DEEP):
            row = row_of(flip, side, out, tile_x)
            part, at = (middle, out) if out < REACH else (edge, out - REACH)
            for comp in range(10):
                value = interleave(me, tiles, comp, row, held.at[(out * 10 + comp) % held.shape[0]])
                if comp in MIRRORED_VEL or comp - 3 in MIRRORED_STRESS:
                    value = sign * value
                if comp < 3:
                    vel[comp, out] = value
                elif comp < 9:
                    part[comp - 3, at] = value
                else:
                    cells[out] = value
                if out >= REACH and comp in face_comps:
                    face[face_comps.index(comp), out - REACH] = value


def push(side, spots, amount, stress_row, vel, light, vel_out, sent):
    rows = [functools.partial(stress_row, comp) for comp in range(6)]
    deep = along_depth([rows[comp](out) for out in range(DEEP) for comp in (4, 5, 2)])
    for out in range(DEEP):
        force_x = across_and_along(rows[0], out, side, rows[3](out)) + deep[3 * out]
        force_y = across_and_along(rows[3], out, side, rows[1](out)) + deep[3 * out + 1]
        force_z = across_and_along(rows[4], out, side, rows[5](out)) + deep[3 * out + 2]
        force_z = force_z + amount * spots[out]
        near = DEEP - 1 - out
        for comp, force in enumerate((force_x, force_y, force_z)):
            fresh = vel[comp, out] + light[out] * force
            vel_out[comp, out] = fresh
            if comp in MIRRORED_VEL:
                fresh = -fresh
            high = fresh.astype(BF16)
            if near < NEAR_ROWS:
                sent[comp * PACKED + 2 * near] = high
                sent[comp * PACKED + 2 * near + 1] = (fresh - high.astype(F32)).astype(BF16)
            else:
                sent[comp * PACKED + NEAR_ROWS + near] = high


def from_halo(halo, comp, near):
    if near < NEAR_ROWS:
        at = comp * PACKED + 2 * near
        return halo[at].astype(F32) + halo[at + 1].astype(F32)
    return halo[comp * PACKED + NEAR_ROWS + near].astype(F32)


def properties(table, number):
    parts = [jnp.full(number.shape, table[0, c], F32) for c in range(3)]
    for m in range(1, table.shape[0]):
        hit = number == float(m)
        parts = [jnp.where(hit, table[m, c], parts[c]) for c in range(3)]
    return parts


def materials(table, *refs):
    for cells, (light, lame, shear) in zip(refs[:2], (refs[2:5], refs[5:])):
        for out in range(DEEP):
            parts = properties(table, cells[out])
            light[out] = (TIME_STEP / UNIT) / parts[0]
            lame[out] = (TIME_STEP * STIFFNESS / UNIT) * parts[1]
            shear[out] = (TIME_STEP * STIFFNESS / UNIT) * parts[2]


def first(side, table, residual, rec_cell, vel, middle, other, edge, light, lame_own, shear_own, halo, *outs):
    vel_out, sent, lame, shear, halo_out, spots, amounts = outs
    size_y, depth = vel.shape[2:]
    planes = size_y // SUBLANES
    slab, me, flip = position()
    cell = rec_cell[0, me]
    spot_x, spot_y = cell // size_y - slab * (2 * DEEP), cell % size_y
    spot_x = spot_x + flip * (2 * DEEP - 1 - 2 * spot_x)
    spot_y = (spot_y % planes) * SUBLANES + spot_y // planes
    at_spot = (lax.broadcasted_iota(jnp.int32, (size_y, depth), 0) == spot_y) & (
        lax.broadcasted_iota(jnp.int32, (size_y, depth), 1) == 0
    )
    for out in range(DEEP):
        here = spot_x == (DEEP - 1 - out if side else DEEP + out)
        spots[out] = jnp.where(at_spot, jnp.where(here, UNIT * AMPLITUDE, 0.0), 0.0)
    for moment in range(residual.shape[2]):
        amounts[moment] = jnp.full((size_y, depth), residual[0, me, moment], F32)
    _, inside = partner(slab, me, lax.axis_size("gx"), side)
    share = jnp.where(inside, TIME_STEP * STIFFNESS / UNIT, 0.0)
    for out in range(DEEP):
        lame[out] = lame_own[out]
        shear[out] = shear_own[out]
    for out in range(DEEP, DEEP + REACH):
        parts = properties(table, halo[len(ALONG_X), REACH - 1 - (out - DEEP)])
        lame[out] = share * parts[1]
        shear[out] = share * parts[2]
    for at in range(len(ALONG_X)):
        for near in range(REACH):
            value = halo[at, REACH - 1 - near]
            halo_out[at, near] = -value if ALONG_X[at] in MIRRORED_STRESS else value
    push(side, spots, amounts[0], stress_rows(middle, other, edge, halo_out), vel, light, vel_out, sent)


def stress_rows(middle, other, edge, halo):
    def row(comp, out):
        if out < 0:
            return other[comp, -1 - out]
        if out < REACH:
            return middle[comp, out]
        if out < DEEP:
            return edge[comp, out - REACH]
        return halo[ALONG_X.index(comp), out - DEEP]

    return row


def strain_rates(vx, vy, vz, side, first_out, last_out, full_out):
    outs = range(first_out, last_out)
    wanted = [(vel, out) for out in outs for vel in (vx, vz)] + [(vy, out) for out in outs if out < full_out]
    deep = along_depth([vel(out) for vel, out in wanted])
    deep = {key: value for key, value in zip(wanted, deep)}
    for out in outs:
        rates = [
            derivative(across(vx, out, side)),
            derivative(along_y(vy(out))),
            deep[vz, out],
            across_and_along(vy, out, side, vx(out)),
            deep[vx, out] + derivative(across(vz, out, side)),
        ]
        if out < full_out:
            rates.append(deep[vy, out] + derivative(along_y(vz(out))))
        yield out, rates


def store(target, at, rates):
    count = rates[0].shape[0] // SUBLANES
    for comp, rate in enumerate(rates):
        for p in range(count):
            spot = pl.ds(p, SUBLANES, stride=count)
            target[comp, at, spot, :] = rate[SUBLANES * p : SUBLANES * (p + 1)]


def renew(rates, lame, shear, before):
    bulk = lame * (rates[0] + rates[1] + rates[2])
    twice = shear + shear
    return {
        comp: old + (bulk + twice * rates[comp] if comp < 3 else shear * rates[comp])
        for comp, old in before.items()
    }


def outer(side, moment, last, vel, halo, edge, *refs):
    if last:
        (rates_out,) = refs
    else:
        old_halo, middle, other, light, lame, shear, spots, amounts, rates_out, edge_out, halo_out, vel_out, sent = refs

    def rows(comp):
        return lambda out: vel[comp, out] if out < DEEP else from_halo(halo, comp, out - DEEP)

    until = DEEP if last else DEEP + REACH
    for out, rates in strain_rates(rows(0), rows(1), rows(2), side, REACH, until, DEEP):
        own = out < DEEP
        if own:
            store(rates_out, out - REACH, rates)
        if last:
            continue
        if own:
            fresh = renew(rates, lame[out], shear[out], {comp: edge[comp, out - REACH] for comp in range(6)})
            for comp, value in fresh.items():
                edge_out[comp, out - REACH] = value
        else:
            before = {comp: old_halo[at, out - DEEP] for at, comp in enumerate(ALONG_X)}
            fresh = renew(rates, lame[out], shear[out], before)
            for at, comp in enumerate(ALONG_X):
                halo_out[at, out - DEEP] = fresh[comp]
    if not last:
        rows = stress_rows(middle, other, edge_out, halo_out)
        push(side, spots, amounts[moment + 1], rows, vel, light, vel_out, sent)


def inner(last, *refs):
    vels = refs[:2]
    if last:
        rates_out = refs[2:]
    else:
        middles, lames, shears = refs[2:4], refs[4:6], refs[6:8]
        rates_out, middles_out = refs[8:10], refs[10:12]
    for side in range(2):

        def rows(comp):
            return lambda out: vels[side][comp, out] if out >= 0 else vels[1 - side][comp, -1 - out]

        for out, rates in strain_rates(rows(0), rows(1), rows(2), side, 0, REACH, REACH):
            store(rates_out[side], out, rates)
            if not last:
                before = {comp: middles[side][comp, out] for comp in range(6)}
                fresh = renew(rates, lames[side][out], shears[side][out], before)
                for comp, value in fresh.items():
                    middles_out[side][comp, out] = value


def correlate(jobs, moments, residual, *refs):
    count = 4 * moments
    rates, sources, before, terms = refs[:count], refs[count : count + len(jobs)], refs[count + len(jobs) : -1], refs[-1]
    tile_x, tile_y = sources[0].shape[2:4]
    _, me, flip = position()
    sign = sign_of(flip)
    for job, turn in enumerate(jobs):
        spot = pl.ds(pl.multiple_of((me ^ turn) * tile_y, tile_y), tile_y)
        for side in range(2):
            for out in range(DEEP):
                row = row_of(flip, side, out, tile_x)
                lam = mu = 0.0
                if before and job < before[0].shape[0]:
                    lam, mu = before[0][job, 0, row], before[0][job, 1, row]
                for moment in jobs[turn]:
                    weight = (KERNEL_SCALE / UNIT) * residual[0, me, moment]
                    held = rates[4 * moment + 2 * (out // REACH) + side]
                    rate = [held[c, out % REACH, spot, :] for c in range(6)]
                    source = [sources[job][moment, c, row] for c in range(6)]
                    bulk = (source[0] + source[1] + source[2]) * (rate[0] + rate[1] + rate[2])
                    diag = source[0] * rate[0] + source[1] * rate[1] + source[2] * rate[2]
                    off = sign * (source[3] * rate[3] + source[4] * rate[4]) + source[5] * rate[5]
                    lam = lam + weight * bulk
                    mu = mu + (2.0 * weight) * (diag + off)
                terms[job, 0, row] = lam
                terms[job, 1, row] = mu


def combine(groups, listed, src_pick, *refs):
    strains, out = refs[:groups], refs[groups]
    group = lax.axis_index("sta")
    moments, comps = out.shape[:2]
    for moment in range(moments):
        factors = []
        for turn in range(groups):
            factor = 0
            for at in range(src_pick.shape[0]):
                factor += jnp.where(src_pick[at, moment] == (group ^ turn), listed[at, moment, group], 0)
            factors.append(factor.astype(F32))
        for comp in range(comps):
            total = 0.0
            for factor, strain in zip(factors, strains):
                total = total + factor * strain[moment, comp].astype(F32)
            out[moment, comp] = total


def swap(array, axis, turn):
    count = lax.axis_size(axis)
    return lax.ppermute(array, axis, [(i, i ^ turn) for i in range(count)])


def partner(slab, piece, slabs, side):
    other = slab + 1 - 2 * ((slab + piece + side) % 2)
    return other, (other >= 0) & (other < slabs)


def to_neighbour(face, side):
    slabs, pieces = lax.axis_size("gx"), lax.axis_size("gy")
    pairs = []
    for slab in range(slabs):
        for piece in range(pieces):
            other, inside = partner(slab, piece, slabs, side)
            if inside:
                pairs.append((slab * pieces + piece, other * pieces + piece))
    return lax.ppermute(face, ("gx", "gy"), pairs)


def local(rec_state, source_strain, material, material_table, residual, rec_cell, listed, src_pick):
    state = rec_state[0]
    receivers, _, tile_x, tile_y, depth = state.shape
    pieces, slabs, groups = lax.axis_size("gy"), lax.axis_size("gx"), lax.axis_size("sta")
    assert receivers == pieces and tile_x == 2 * DEEP
    assert pieces & (pieces - 1) == 0 and groups & (groups - 1) == 0
    size_y = pieces * tile_y
    group, me = lax.axis_index("sta"), lax.axis_index("gy")
    moments = residual.shape[2]

    numbers = material.astype(F32)[None]
    order = sorted(range(pieces), reverse=True)
    picked = {turn: lax.dynamic_index_in_dim(state, me ^ turn, 0, keepdims=False) for turn in order}
    own = source_strain[0].reshape(source_strain.shape[1:3] + (tile_x * tile_y, depth))
    own, picked = lax.optimization_barrier((own, picked))
    chunks = {turn: jnp.concatenate([picked[turn], numbers], 0) for turn in order}
    chunks = [swap(chunks[turn], "gy", turn) if turn else chunks[turn] for turn in range(pieces)]
    strains = [swap(own, "sta", turn) if turn else own for turn in range(groups)]

    def shape(*lead, kind=F32):
        return lead + (size_y, depth), kind

    vel_shape, pair_shape = shape(3, DEEP), shape(6, REACH)
    halo_shape, sent_shape = shape(3, REACH), shape(3 * PACKED, kind=BF16)

    results = call(
        assemble,
        [vel_shape, pair_shape, pair_shape, shape(DEEP), shape(4, REACH)] * 2,
        ([], chunks),
        [pltpu.VMEM((8, size_y, depth), F32)],
    )
    vels, middles, edges, cells, faces = ([results[at], results[5 + at]] for at in range(5))
    halos = [to_neighbour(faces[side], side) for side in range(2)]

    strains, cells = lax.optimization_barrier((strains, cells))
    (combined,) = call(
        functools.partial(combine, groups), [(own.shape, F32)], ([listed, src_pick], strains)
    )
    combined = combined.reshape(own.shape[:2] + (tile_x, tile_y, depth))
    own_rows = call(materials, [shape(DEEP)] * 6, ([material_table], cells))
    own_rows = (own_rows[:3], own_rows[3:])
    sent, lights, lames, shears, old_halos, spots, amounts = ([None, None] for _ in range(7))
    fresh = [None, None]
    for side in range(2):
        results = call(
            functools.partial(first, side),
            [vel_shape, sent_shape, shape(DEEP + REACH), shape(DEEP + REACH), halo_shape]
            + [shape(DEEP), shape(moments)],
            (
                [material_table, residual, rec_cell],
                [vels[side], middles[side], middles[1 - side], edges[side], *own_rows[side], halos[side]],
            ),
        )
        fresh[side], sent[side], lames[side], shears[side], old_halos[side] = results[:5]
        spots[side], amounts[side] = results[5:]
        lights[side] = own_rows[side][0]
        sent[side] = to_neighbour(sent[side], side)
    vels = fresh

    found, rates = {0: combined}, []
    exchanges = {0: [pieces // 2], 1: [w for w in range(1, pieces // 2) if w & (w - 1) == 0]}
    rest = [turn for turn in range(pieces) if turn & (turn - 1)]
    for moment in range(moments):
        last = moment == moments - 1
        if last:
            found, vels = lax.optimization_barrier((found, vels))
        results = call(
            functools.partial(inner, last),
            [pair_shape] * (2 if last else 4),
            ([], vels if last else vels + middles + lames + shears),
        )
        rates += results[:2]
        if not last:
            middles = results[2:]
        if moment in exchanges:
            ready, rates[-1] = lax.optimization_barrier((combined, rates[-1]))
            for turn in exchanges[moment]:
                found[turn] = swap(ready, "gy", turn)
        if moment == 5 * moments // 8:
            found, rates[-1] = lax.optimization_barrier((found, rates[-1]))
            for turn in rest:
                low = turn & -turn
                found[turn] = swap(found[turn ^ low], "gy", low)
        if last:
            early, late = list(range(pieces)), []
            jobs = {turn: list(range(moment)) for turn in early}
            (terms,) = call(
                functools.partial(correlate, jobs, moment),
                [((len(jobs), 2, tile_x, tile_y, depth), F32)],
                ([residual], rates[: 4 * moment] + [found[turn] for turn in jobs]),
            )
            terms, vels = lax.optimization_barrier((terms, vels))
        fresh = [None, None]
        for side in range(2):
            arrays = [vels[side], sent[side], edges[side]]
            outs = [pair_shape]
            if not last:
                arrays += [old_halos[side], middles[side], middles[1 - side]]
                arrays += [lights[side], lames[side], shears[side], spots[side], amounts[side]]
                outs += [pair_shape, halo_shape, vel_shape, sent_shape]
            results = call(functools.partial(outer, side, moment, last), outs, ([], arrays))
            rates.append(results[0])
            if not last:
                edges[side], old_halos[side], fresh[side] = results[1:4]
                sent[side] = to_neighbour(results[4], side)
        vels = fresh

    jobs = {turn: [moments - 1] if turn in early else list(range(moments)) for turn in early + late}
    (terms,) = call(
        functools.partial(correlate, jobs, moments),
        [((pieces, 2, tile_x, tile_y, depth), F32)],
        ([residual], rates + [found[turn] for turn in jobs] + [terms]),
    )
    held = {turn: terms[at] for at, turn in enumerate(jobs)}
    if pieces > 1:
        keep = [turn for turn in held if not turn & 1]
        got = swap(jnp.stack([held[turn ^ 1] for turn in keep]), "gy", 1)
        held = {turn: held[turn] + got[at] for at, turn in enumerate(keep)}
    share = tile_x // groups
    result = 0.0
    for across_sta in reversed(range(groups)):
        for turn in reversed(list(held)):
            part = lax.dynamic_slice_in_dim(held[turn], (group ^ across_sta) * share, share, 1)
            if across_sta or turn:
                pairs = [
                    (a * pieces + b, (a ^ across_sta) * pieces + (b ^ turn))
                    for a in range(groups)
                    for b in range(pieces)
                ]
                part = lax.ppermute(part, ("sta", "gy"), pairs)
            result = result + part
    return result


def solution(mesh):
    in_specs = (
        P("sta", None, None, "gx", "gy", None),
        P("sta", None, None, "gx", "gy", None),
        P("gx", "gy", None),
        P(),
        P("sta", None, None),
        P("sta", None),
        P(),
        P(),
    )
    out_specs = P(None, ("gx", "sta"), "gy", None)
    return jax.shard_map(local, mesh=mesh, in_specs=in_specs, out_specs=out_specs, check_vma=False)
```
